32 devices in a mesh: groups: 2 (over y), adapter: 4 (over z), tensor: 2 (over x), sub: 2 (over core).
Axes of the slice: x: 2, y: 2, z: 4, core: 2. Of those that a mesh axis runs over, the one named last changes fastest.
Arguments:
- activations: bfloat16 [8192, 3072], P(('groups', 'adapter'), ('tensor', 'sub')), parts along dimension 0, may hold values from -6 to 6
- cotangent: bfloat16 [8192, 3072], P(('groups', 'adapter'), ('tensor', 'sub')), parts along dimension 0, may hold values from -6 to 6
- frozen_weight: bfloat16 [3072, 3072], P(('tensor', 'sub')), may hold values from -0.109375 to 0.109375
- adapter_down_maps: bfloat16 [8, 3072, 64], P(('groups', 'adapter'), ('tensor', 'sub')), parts along dimension 0, may hold values from -0.109375 to 0.109375
- adapter_up_maps: bfloat16 [8, 64, 3072], P(('groups', 'adapter'), None, ('tensor', 'sub')), parts along dimension 0, may hold values from -0.109375 to 0.109375
- adapter_per_tile: int32 [64], P('groups'), parts along dimension 0, may hold values from 0 to 3, as said below
- live_per_tile: int32 [64], P('groups'), parts along dimension 0, may hold values from 1 to 128, as said below
- adapter_stored_row: int32 [8], P('groups'), parts along dimension 0, may hold values from 0 to 3, as said below
Outputs:
- input_grad: bfloat16 [8192, 3072], P(('groups', 'adapter'), ('tensor', 'sub')), parts along dimension 0
- down_grad: bfloat16 [8, 3072, 64], P(('groups', 'adapter'), ('tensor', 'sub')), parts along dimension 0
- up_grad: bfloat16 [8, 64, 3072], P(('groups', 'adapter'), None, ('tensor', 'sub')), parts along dimension 0
The draws below stay inside these ranges and needn't reach their ends.
There are 2 independent parts, one for each index of `groups`. The reference program is written for one: setup_inputs(seed, part) draws one part's arguments, and reference() takes and returns one part's arrays. A program takes and returns all parts, laid end to end along the dimension named above; an argument that names none is the same for every part. Nothing has to cross between parts.
Inputs may be any that keep to these rules, and one draw needn't show every extreme that they name: `adapter_per_tile`: the owner of stored row j is j. In each block of 8 consecutive tiles, at most 2 tiles use adapters of one owner, and one owner, the same for all blocks and drawn from the seed, takes exactly 2 tiles of every block. `live_per_tile`: rows of a tile past its live count are padding. `adapter_stored_row`: A permutation: every stored row belongs to exactly one adapter.
All inputs are finite; a program needn't handle non-finite values.
Results may differ from the reference program's by a relative error of at most 0.017.
Values may be sent and summed in bfloat16 or wider, within the bound.
No kernel may reach another device: no remote copies, remote signals or barrier semaphores. Data moves between devices by JAX's collectives and lax.ppermute only.
A program may use at most 64 MiB of HBM per device.

```python
import math
import jax
import jax.numpy as jnp
from jax import lax

MODEL_WIDTH = 3072
ADAPTER_RANK = 64
TILE = 128
TOK_DEV = 1024
ADP_DEV = 1
TILES_DEV = 8
CAP = 2
TOKENS = 4096
TILES = 32
ADAPTER_TOTAL = 4
N_ADAPTER = 4


def plan_tables(key):
    key_perm, key_order, key_pick, key_hot, key_first = jax.random.split(key, 5)
    adapter_stored_row = jax.random.permutation(key_perm, ADAPTER_TOTAL).astype(jnp.int32)
    hottest = jax.random.randint(key_hot, (), 0, N_ADAPTER)
    owner_ids = jnp.arange(N_ADAPTER, dtype=jnp.int32)
    scores = jax.random.randint(key_order, (N_ADAPTER, N_ADAPTER), 0, 1 << 20) * N_ADAPTER + owner_ids[None, :]
    scores = jnp.where(owner_ids[None, :] == hottest, -1, scores)
    ordering = jnp.argsort(scores, axis=1).astype(jnp.int32)
    first_tile = jax.random.randint(key_first, (N_ADAPTER,), 0, TILES_DEV - (CAP - 1) * N_ADAPTER)
    position = (jnp.arange(TILES_DEV, dtype=jnp.int32)[None, :] - first_tile[:, None]) % N_ADAPTER
    owner_of_tile = jnp.take_along_axis(ordering, position, axis=1)
    within = jax.random.randint(key_pick, (N_ADAPTER, TILES_DEV), 0, ADP_DEV)
    stored_row = owner_of_tile * ADP_DEV + within
    inverse = jnp.argsort(adapter_stored_row).astype(jnp.int32)
    adapter_per_tile = inverse[stored_row].reshape(TILES).astype(jnp.int32)
    return (adapter_stored_row, adapter_per_tile)


def draw_adapter_stored_row(key, part):
    shared = plan_tables(key)
    return shared[0]


def draw_adapter_per_tile(key, part):
    shared = plan_tables(key)
    return shared[1]


def draw_live_per_tile(key, part):
    key = jax.random.fold_in(key, 7)
    key_kind, key_count = jax.random.split(key)
    partial_tile = jax.random.randint(key_kind, (TILES,), 0, 4) == 0
    shorter = jax.random.randint(key_count, (TILES,), 1, TILE)
    counts = jnp.where(partial_tile, shorter, TILE)
    counts = counts.at[0].set(TILE)
    counts = counts.at[1].set(shorter[1])
    return counts.astype(jnp.int32)


def block_scale(own_key, dims, shards, smallest, top_value):
    def one(dim, shards_of):
        steps = jax.random.uniform(jax.random.fold_in(jax.random.fold_in(own_key, 6), dim), (shards_of,), jnp.float32, smallest / len(shards), top_value / len(shards))
        return jnp.repeat(jnp.exp(steps), dims[dim] // shards_of).reshape((-1,) + (1,) * (len(dims) - dim - 1))

    level = one(*shards[0])
    for cut in shards[1:]:
        level = level * one(*cut)
    return level


def normal_values(stream_key, dims, scale, limit, cuts=(), kind=jnp.bfloat16):
    level = block_scale(stream_key, dims, cuts, -0.22, 0.18) if cuts else 1.0
    array = jax.random.normal(stream_key, dims, jnp.float32) * scale * level
    return jnp.minimum(jnp.maximum(array, -limit), limit).astype(kind)


def setup_inputs(seed: int = 0, part: int = 0) -> dict:
    streams_of = jax.random.split(jax.random.key(seed), 9)
    part_keys = jax.random.split(jax.random.fold_in(streams_of[8], part), 9)
    return {
        "activations": normal_values(part_keys[0], (TOKENS, MODEL_WIDTH), 1.0, 6.0, ((0, 4), (1, 4))),
        "cotangent": normal_values(part_keys[1], (TOKENS, MODEL_WIDTH), 1.0, 6.0, ((0, 4), (1, 4))),
        "frozen_weight": normal_values(streams_of[2], (MODEL_WIDTH, MODEL_WIDTH), MODEL_WIDTH ** -0.5, 0.109375, ((0, 4),)),
        "adapter_down_maps": normal_values(part_keys[3], (ADAPTER_TOTAL, MODEL_WIDTH, ADAPTER_RANK), MODEL_WIDTH ** -0.5, 0.109375, ((0, 4), (1, 4))),
        "adapter_up_maps": normal_values(part_keys[4], (ADAPTER_TOTAL, ADAPTER_RANK, MODEL_WIDTH), MODEL_WIDTH ** -0.5, 0.109375, ((0, 4), (2, 4))),
        "adapter_per_tile": draw_adapter_per_tile(jax.random.fold_in(jax.random.fold_in(streams_of[8], part), 71), part),
        "live_per_tile": draw_live_per_tile(jax.random.fold_in(jax.random.fold_in(streams_of[8], part), 71), part),
        "adapter_stored_row": draw_adapter_stored_row(jax.random.fold_in(jax.random.fold_in(streams_of[8], part), 71), part),
    }


def reference(activations, cotangent, frozen_weight, adapter_down_maps, adapter_up_maps, adapter_per_tile, live_per_tile, adapter_stored_row):
    stored = adapter_stored_row[adapter_per_tile].astype(jnp.int32).reshape(N_ADAPTER, TILES_DEV)
    live_blocks = live_per_tile.reshape(N_ADAPTER, TILES_DEV)
    act_blocks = activations.reshape(N_ADAPTER, TILES_DEV, TILE, MODEL_WIDTH)
    cot_blocks = cotangent.reshape(N_ADAPTER, TILES_DEV, TILE, MODEL_WIDTH)
    weight_full = frozen_weight.astype(jnp.float32)
    positions = jnp.arange(TILE, dtype=jnp.int32)
    columns = jnp.arange(ADAPTER_TOTAL, dtype=jnp.int32)
    highest = lax.Precision.HIGHEST

    def one_block(carry, block):
        down_total, up_total = carry
        act_block, cot_block, stored_rows_block, live_block = block
        down_selected = adapter_down_maps[stored_rows_block].astype(jnp.float32)
        up_selected = adapter_up_maps[stored_rows_block].astype(jnp.float32)
        live_mask = (positions[None, :] < live_block[:, None]).astype(jnp.float32)[:, :, None]
        act_f = act_block.astype(jnp.float32)
        cot_f = cot_block.astype(jnp.float32)
        hidden_state = (jnp.einsum('trd,tdq->trq', act_f, down_selected, precision=highest) * live_mask).astype(jnp.bfloat16)
        backward_result = (jnp.einsum('tro,tqo->trq', cot_f, up_selected, precision=highest) * live_mask).astype(jnp.bfloat16)
        base_grad = jnp.dot(cot_f.reshape(TOK_DEV, MODEL_WIDTH), weight_full.T, precision=highest, preferred_element_type=jnp.float32)
        adapter_term = jnp.einsum('trq,tdq->trd', backward_result.astype(jnp.float32), down_selected, precision=highest).astype(jnp.bfloat16)
        adapter_term = lax.optimization_barrier(adapter_term)
        input_grad = (base_grad + adapter_term.astype(jnp.float32).reshape(TOK_DEV, MODEL_WIDTH)).astype(jnp.bfloat16)
        selector = (stored_rows_block[:, None] == columns[None, :]).astype(jnp.float32)
        down_terms = jnp.einsum('trd,trq->tdq', act_f, backward_result.astype(jnp.float32), precision=highest)
        up_terms = jnp.einsum('trq,tro->tqo', hidden_state.astype(jnp.float32), cot_f, precision=highest)
        down_block = jnp.einsum('ta,tdq->adq', selector, down_terms, precision=highest).astype(jnp.bfloat16)
        up_block = jnp.einsum('ta,tqo->aqo', selector, up_terms, precision=highest).astype(jnp.bfloat16)
        down_block, up_block = lax.optimization_barrier((down_block, up_block))
        return ((down_total + down_block.astype(jnp.float32), up_total + up_block.astype(jnp.float32)), input_grad)
    start_carry = (jnp.zeros((ADAPTER_TOTAL, MODEL_WIDTH, ADAPTER_RANK), jnp.float32), jnp.zeros((ADAPTER_TOTAL, ADAPTER_RANK, MODEL_WIDTH), jnp.float32))
    totals, grads = lax.scan(one_block, start_carry, (act_blocks, cot_blocks, stored, live_blocks))
    grad_scale = math.sqrt(ADP_DEV / TOK_DEV)
    down_grad = (totals[0] * grad_scale).astype(jnp.bfloat16)
    up_grad = (totals[1] * grad_scale).astype(jnp.bfloat16)
    return (grads.reshape(TOKENS, MODEL_WIDTH), down_grad, up_grad)
```

```python
import functools

import jax
import jax.numpy as jnp
from jax import lax
from jax.experimental import pallas as pl
from jax.experimental.pallas import tpu as pltpu
from jax.sharding import PartitionSpec as P

TILE = 128
CHUNKS = 4
VMEM_BYTES = 40 * 1024 * 1024
NT = (((1,), (1,)), ((), ()))


def shift(array, axis, size, by):
    return lax.ppermute(array, axis, [(i, (i + by) % size) for i in range(size)])


def call(body, **kwargs):
    return pl.pallas_call(
        body, compiler_params=pltpu.CompilerParams(vmem_limit_bytes=VMEM_BYTES), **kwargs
    )


def whole(count):
    return [pl.BlockSpec(memory_space=pltpu.VMEM)] * count


def dot(a, b, dims=(((1,), (0,)), ((), ()))):
    return lax.dot_general(a, b, dims, preferred_element_type=jnp.float32)


def rank_kernel(n, rank, slot, live, half, act, cot, *refs):
    downs, ups, (keep, give) = refs[:n], refs[n : 2 * n], refs[2 * n :]
    down = jnp.concatenate([r[...] for r in downs], axis=0)
    up = jnp.concatenate([r[...] for r in ups], axis=0)
    width = 2 * rank
    tiles = act.shape[0] // TILE
    per_half = tiles // 2
    lane = lax.broadcasted_iota(jnp.int32, (TILE, n * rank), 1) // rank
    small = lax.broadcasted_iota(jnp.int32, (TILE, width), 1)
    row = lax.broadcasted_iota(jnp.int32, (TILE, width), 0)
    for tile in range(tiles):
        rows = pl.ds(tile * TILE, TILE)
        mask = lane == slot[tile]
        both = []
        for data, maps in ((act, down), (cot, up)):
            full = jnp.where(mask, dot(data[rows, :], maps, NT), 0.0)
            kept = functools.reduce(
                jnp.add, [full[:, g : g + width] for g in range(0, n * rank, width)]
            )
            both.append(kept + pltpu.roll(kept, rank, 1))
        out = jnp.where(small < rank, both[0], both[1])
        out = jnp.where(row < live[tile], out, 0.0).astype(jnp.bfloat16)
        here = pl.ds((tile % per_half) * TILE, TILE)

        @pl.when(half[0] == tile // per_half)
        def _():
            keep[here, :] = out

        @pl.when(half[0] != tile // per_half)
        def _():
            give[here, :] = out


def terms_kernel(n, rank, slot, half, mine, other, act, cot, *refs):
    terms, (spread, hid_t, back_t) = refs[:n], refs[n:]
    width = 2 * rank
    tiles = act.shape[0] // TILE
    per_half = tiles // 2
    hid_t[...] = jnp.zeros_like(hid_t)
    back_t[...] = jnp.zeros_like(back_t)
    lane = lax.broadcasted_iota(jnp.int32, (TILE, n * rank), 1) // rank
    small = lax.broadcasted_iota(jnp.int32, (TILE, width), 1)
    for tile in range(tiles):
        here = pl.ds((tile % per_half) * TILE, TILE)
        is_mine = half[0] == tile // per_half
        hb = jnp.where(is_mine, mine[here, :].astype(jnp.float32), other[here, :].astype(jnp.float32))
        hb_t = hb.T.astype(jnp.bfloat16)
        at = pl.ds(pl.multiple_of(slot[tile] * rank, rank), rank)
        hid_t[at, tile * TILE : (tile + 1) * TILE] = hb_t[:rank]
        back_t[at, tile * TILE : (tile + 1) * TILE] = hb_t[rank:]
        twice = jnp.where(small < rank, pltpu.roll(hb, rank, 1), hb)
        wide = jnp.concatenate([twice] * (n * rank // width), axis=1)
        spread[pl.ds(tile * TILE, TILE), :] = jnp.where(lane == slot[tile], wide, 0.0).astype(
            jnp.bfloat16
        )
    down = dot(back_t[...], act[...]).astype(jnp.bfloat16)
    up = dot(hid_t[...], cot[...]).astype(jnp.bfloat16)
    for k in range(n):
        terms[k][:rank, :] = down[k * rank : (k + 1) * rank]
        terms[k][rank:, :] = up[k * rank : (k + 1) * rank]


def near_kernel(n, place, own, pair, w_own, w_pair, spread, *refs):
    down = jnp.concatenate([r[...] for r in refs[:n]], axis=0)
    refs[n][...] = (
        dot(own[...], w_own[...], NT) + dot(pair[...], w_pair[...], NT) + dot(spread[...], down)
    )


def far_kernel(count, place, near, *refs):
    total = near[...]
    for data, weight in zip(refs[:count], refs[count : 2 * count]):
        total += dot(data[...], weight[...], NT)
    refs[-1][...] = total.astype(jnp.bfloat16)


def on_device(
    activations,
    cotangent,
    frozen_weight,
    adapter_down_maps,
    adapter_up_maps,
    adapter_per_tile,
    live_per_tile,
    adapter_stored_row,
):
    rows, features = activations.shape
    tiles = rows // TILE
    stored, _, rank = adapter_down_maps.shape
    n = lax.axis_size("adapter")
    tensors = lax.axis_size("tensor")
    subs = lax.axis_size("sub")
    me = lax.axis_index("adapter")
    t_me, s_me = lax.axis_index("tensor"), lax.axis_index("sub")
    chunk = rows // CHUNKS
    bf16, f32 = jnp.bfloat16, jnp.float32

    own_ids = lax.dynamic_slice_in_dim(adapter_per_tile, me * tiles, tiles)
    own_live = lax.dynamic_slice_in_dim(live_per_tile, me * tiles, tiles)
    matches = own_ids[:, None] == jnp.arange(adapter_stored_row.shape[0], dtype=jnp.int32)[None, :]
    own_rows = jnp.sum(jnp.where(matches, adapter_stored_row[None, :], 0), axis=1)
    slot = jnp.remainder(me - own_rows, n).astype(jnp.int32)
    half = s_me.astype(jnp.int32).reshape(1)

    down = jnp.swapaxes(adapter_down_maps, 1, 2).reshape(stored * rank, features)
    up = adapter_up_maps.reshape(stored * rank, features)
    downs = [down] + [shift(down, "adapter", n, k) for k in range(1, n)]
    ups = [up] + [shift(up, "adapter", n, k) for k in range(1, n)]

    pair = shift(cotangent, "sub", subs, 1)
    far = []
    for c in range(CHUNKS):
        part = cotangent[c * chunk : (c + 1) * chunk]
        direct = [shift(part, "tensor", tensors, k) for k in range(1, tensors)]
        far.append(direct + [shift(x, "sub", subs, 1) for x in direct])

    smem = pl.BlockSpec(memory_space=pltpu.SMEM)
    half_shape = jax.ShapeDtypeStruct((rows // 2, 2 * rank), bf16)
    keep, give = call(
        functools.partial(rank_kernel, n, rank),
        in_specs=[smem] * 3 + whole(2 + 2 * n),
        out_specs=whole(2),
        out_shape=[half_shape] * 2,
    )(slot, own_live, half, activations, cotangent, *downs, *ups)
    chip = keep.astype(f32) + shift(give, "sub", subs, 1).astype(f32)
    sent = chip.astype(bf16)
    for k in range(1, tensors):
        chip = chip + shift(sent, "tensor", tensors, k).astype(f32)
    mine = chip.astype(bf16)
    other = shift(mine, "sub", subs, 1)

    *terms, spread = call(
        functools.partial(terms_kernel, n, rank),
        in_specs=[smem] * 2 + whole(4),
        out_specs=whole(n + 1),
        out_shape=[jax.ShapeDtypeStruct((2 * rank, features), bf16)] * n
        + [jax.ShapeDtypeStruct((rows, n * rank), bf16)],
        scratch_shapes=[pltpu.VMEM((n * rank, rows), bf16)] * 2,
    )(slot, half, mine, other, activations, cotangent)

    arrived = [shift(terms[k], "adapter", n, -k) for k in range(1, n)]

    places = [t_me * subs + s_me, t_me * subs + (1 - s_me)]
    for s in (s_me, 1 - s_me):
        places += [jnp.remainder(t_me - k, tensors) * subs + s for k in range(1, tensors)]
    place = jnp.stack(places).astype(jnp.int32)

    def weight_spec(i):
        return pl.BlockSpec((features, features), lambda b, place: (0, place[i]))

    def row_spec(extent, width):
        return pl.BlockSpec((extent, width), lambda b, place: (b, 0))

    near = call(
        functools.partial(near_kernel, n),
        grid_spec=pltpu.PrefetchScalarGridSpec(
            num_scalar_prefetch=1,
            grid=(CHUNKS,),
            in_specs=[row_spec(chunk, features)] * 2
            + [weight_spec(0), weight_spec(1), row_spec(chunk, n * rank)]
            + [pl.BlockSpec((rank, features), lambda b, place: (0, 0))] * n,
            out_specs=row_spec(chunk, features),
        ),
        out_shape=jax.ShapeDtypeStruct((rows, features), f32),
    )(place, cotangent, pair, frozen_weight, frozen_weight, spread, *downs)

    out = None
    count = len(far[0])
    for c in range(CHUNKS):
        def chunk_spec(b, place, c=c):
            return (c, 0)

        operands = [place, near, *far[c], *[frozen_weight] * count]
        in_specs = (
            [pl.BlockSpec((chunk, features), chunk_spec)]
            + [pl.BlockSpec((chunk, features), lambda b, place: (0, 0))] * count
            + [weight_spec(2 + i) for i in range(count)]
        )
        body, aliases = functools.partial(far_kernel, count), {}
        if out is not None:
            aliases = {len(operands): 0}
            operands.append(out)
            in_specs.append(pl.BlockSpec(memory_space=pl.ANY))
        out = call(
            body,
            grid_spec=pltpu.PrefetchScalarGridSpec(
                num_scalar_prefetch=1,
                grid=(1,),
                in_specs=in_specs,
                out_specs=pl.BlockSpec((chunk, features), chunk_spec),
            ),
            out_shape=jax.ShapeDtypeStruct((rows, features), bf16),
            input_output_aliases=aliases,
        )(*operands)

    total = terms[0].astype(f32)
    for x in arrived:
        total = total + x.astype(f32)
    total = (total * (stored / rows) ** 0.5).astype(bf16)
    down_grad = jnp.swapaxes(total[:rank].reshape(stored, rank, features), 1, 2)
    up_grad = total[rank:].reshape(stored, rank, features)
    return (out, down_grad, up_grad)


def solution(mesh):
    return jax.shard_map(
        on_device,
        mesh=mesh,
        in_specs=(
            P(("groups", "adapter"), ("tensor", "sub")),
            P(("groups", "adapter"), ("tensor", "sub")),
            P(("tensor", "sub"), None),
            P(("groups", "adapter"), ("tensor", "sub"), None),
            P(("groups", "adapter"), None, ("tensor", "sub")),
            P("groups"),
            P("groups"),
            P("groups"),
        ),
        out_specs=(
            P(("groups", "adapter"), ("tensor", "sub")),
            P(("groups", "adapter"), ("tensor", "sub"), None),
            P(("groups", "adapter"), None, ("tensor", "sub")),
        ),
        check_vma=False,
    )
```

```python
import functools

import jax
import jax.numpy as jnp
from jax import lax
from jax.experimental import pallas as pl
from jax.experimental.pallas import tpu as pltpu
from jax.sharding import PartitionSpec as P

TILE = 128
HEAVY = 1 << 36
CHUNKS = (2, 4, 4, 2, 4)
NT = (((1,), (1,)), ((), ()))
SMEM = pl.BlockSpec(memory_space=pltpu.SMEM)
VMEM = pl.BlockSpec(memory_space=pltpu.VMEM)
ANY = pl.BlockSpec(memory_space=pl.ANY)
HBM = pl.BlockSpec(memory_space=pltpu.HBM)


def shift(array, axis, size, by):
    return lax.ppermute(array, axis, [(i, (i + by) % size) for i in range(size)])


def call(body, mib=12, flops=0, **kwargs):
    params = pltpu.CompilerParams(vmem_limit_bytes=mib * 1024 * 1024)
    cost = pl.CostEstimate(flops=flops, bytes_accessed=0, transcendentals=0)
    name = getattr(body, "func", body).__name__
    return pl.pallas_call(body, compiler_params=params, cost_estimate=cost, name=name, **kwargs)


def dot(a, b, dims=(((1,), (0,)), ((), ()))):
    return lax.dot_general(a, b, dims, preferred_element_type=jnp.float32)


def tile_rows(index):
    return pl.ds(pl.multiple_of(index * TILE, TILE), TILE)


def slot_rows(data, tile, entries):
    return jnp.concatenate([data[tile_rows(tile[e]), :] for e in entries], axis=0)


def plan_kernel(n, cap, tiles, ids, live_all, stored, me, *refs):
    tile, live, count = refs[-3:]
    for k in range(n):
        count[k] = 0
    for e in range(n * cap):
        tile[e] = 0
        live[e] = 0
    for t in range(tiles):
        at = me[0] * tiles + t
        k = lax.rem(me[0] - stored[ids[at]] + n, n)
        e = jnp.minimum(k * cap + count[k], n * cap - 1)
        tile[e] = t
        live[e] = live_all[at]
        count[k] = count[k] + 1


def rank_kernel(slots, cap, tile, live, half, act, cot, *refs):
    packs = refs[: len(slots)]
    keep, give, held = refs[-3:]
    width = packs[0].shape[0]
    part = lax.broadcasted_iota(jnp.int32, packs[0].shape, 0) < width // 2
    row = lax.broadcasted_iota(jnp.int32, (TILE, width), 0)
    for i, (slot, pack) in enumerate(zip(slots, packs)):
        entries = range(slot * cap, (slot + 1) * cap)
        maps = pack[...]
        zero = jnp.zeros_like(maps)
        both = dot(slot_rows(act, tile, entries), jnp.where(part, maps, zero), NT)
        both += dot(slot_rows(cot, tile, entries), jnp.where(part, zero, maps), NT)
        for c, e in enumerate(entries):
            at = (i * cap + c) * TILE
            held[at : at + TILE, :] = jnp.where(
                row < live[e], both[c * TILE : (c + 1) * TILE], 0.0
            ).astype(jnp.bfloat16)
    extent = keep.shape[0]
    keep[...] = held[pl.ds(pl.multiple_of(half[0] * extent, TILE // 2), extent), :]
    give[...] = held[pl.ds(pl.multiple_of((1 - half[0]) * extent, TILE // 2), extent), :]


def sum_kernel(count, place, *refs):
    total = refs[0][...].astype(jnp.float32)
    for x in refs[1:count]:
        total += x[...].astype(jnp.float32)
    out = refs[place]
    out[...] = total.astype(out.dtype)


def gate_kernel(*refs):
    pass


def join(half, mine, other, held):
    extent = mine.shape[0]
    held[pl.ds(pl.multiple_of(half[0] * extent, TILE // 2), extent), :] = mine[...]
    held[pl.ds(pl.multiple_of((1 - half[0]) * extent, TILE // 2), extent), :] = other[...]


def terms_kernel(slots, cap, tile, half, mine, other, act, cot, *refs):
    terms, held = refs[-1 - len(slots) : -1], refs[-1]
    rank = held.shape[1] // 2
    join(half, mine, other, held)
    for i, slot in enumerate(slots):
        entries = range(slot * cap, (slot + 1) * cap)
        both = held[i * cap * TILE : (i + 1) * cap * TILE, :].astype(jnp.float32)
        both = both.T.astype(jnp.bfloat16)
        terms[i][:rank, :] = dot(both[rank:], slot_rows(act, tile, entries)).astype(jnp.bfloat16)
        terms[i][rank:, :] = dot(both[:rank], slot_rows(cot, tile, entries)).astype(jnp.bfloat16)


def weight_columns(weight, place):
    features = weight.shape[0]
    return weight[:, pl.ds(pl.multiple_of(place * features, 128), features)]


def near_kernel(place, own, pair, weight, *refs):
    out = refs[-1]
    out[...] = dot(own[...], weight_columns(weight, place[0]), NT)
    out[...] += dot(pair[...], weight_columns(weight, place[1]), NT)


def far_sum(total, place, weight, blocks):
    for i, block in enumerate(blocks):
        total += dot(block[...], weight_columns(weight, place[2 + i]), NT)
    return total.astype(jnp.bfloat16)


def middle_kernel(groups, cap, count, tile, half, place, *refs):
    n = sum(len(g) for g in groups)
    sums, refs = refs[: 2 * len(groups)], refs[2 * len(groups) :]
    packs, (near, weight), refs = refs[:n], refs[n : n + 2], refs[n + 2 :]
    out, term, *helds, done, sem = refs[-4 - len(groups) :]
    term[...] = jnp.zeros_like(term)
    for g, slots in enumerate(groups):
        join(half, sums[2 * g], sums[2 * g + 1], helds[g])
        for i, slot in enumerate(slots):
            maps = packs[slot][...]
            rank = maps.shape[0] // 2
            maps = jnp.concatenate([jnp.zeros_like(maps[:rank]), maps[:rank]], axis=0)
            found = dot(helds[g][i * cap * TILE : (i + 1) * cap * TILE, :], maps)
            for c in range(cap):
                rows = tile_rows(tile[slot * cap + c])
                before = term[rows, :].astype(jnp.float32)
                term[rows, :] = (before + found[c * TILE : (c + 1) * TILE]).astype(term.dtype)
    start = 0
    for c in range(3):
        blocks = refs[c * count : (c + 1) * count]
        rows = slice(start, start + blocks[0].shape[0])
        total = near[rows, :] + term[rows, :].astype(jnp.float32)
        done[rows, :] = far_sum(total, place, weight, blocks)
        start = rows.stop
    copy = pltpu.make_async_copy(done, out.at[pl.ds(0, start), :], sem)
    copy.start()
    copy.wait()


def far_kernel(count, start, place, near, term, weight, *refs):
    out, token, done, sem = refs[-4:]
    rows = slice(start, start + done.shape[0])
    total = near[rows, :] + term[rows, :].astype(jnp.float32)
    done[...] = far_sum(total, place, weight, refs[:count])
    copy = pltpu.make_async_copy(done, out.at[pl.ds(start, done.shape[0]), :], sem)
    copy.start()
    token[...] = jnp.zeros_like(token)
    copy.wait()


def final_kernel(count, scale, *refs):
    down, up, token = refs[-3:]
    token[...] = jnp.zeros_like(token)
    rank = down.shape[0]
    for out, rows in ((down, slice(0, rank)), (up, slice(rank, 2 * rank))):
        total = refs[0][rows, :].astype(jnp.float32)
        for x in refs[1:count]:
            total += x[rows, :].astype(jnp.float32)
        out[...] = (total * scale).astype(out.dtype)


def on_device(
    activations,
    cotangent,
    frozen_weight,
    adapter_down_maps,
    adapter_up_maps,
    adapter_per_tile,
    live_per_tile,
    adapter_stored_row,
):
    rows, features = activations.shape
    tiles = rows // TILE
    stored, _, rank = adapter_down_maps.shape
    n = lax.axis_size("adapter")
    tensors = lax.axis_size("tensor")
    subs = lax.axis_size("sub")
    me = lax.axis_index("adapter")
    t_me, s_me = lax.axis_index("tensor"), lax.axis_index("sub")
    extents = [rows * c // sum(CHUNKS) for c in CHUNKS]
    starts = [sum(extents[:c]) for c in range(len(extents))]
    bf16, f32 = jnp.bfloat16, jnp.float32

    cap = -(-tiles // n)
    half = s_me.astype(jnp.int32).reshape(1)

    places = [t_me * subs + s_me, t_me * subs + (1 - s_me)]
    for s in (s_me, 1 - s_me):
        places += [jnp.remainder(t_me - k, tensors) * subs + s for k in range(1, tensors)]
    place = jnp.stack(places).astype(jnp.int32)

    groups = [[k for k in range(n) if min(k, n - k) <= n // 4]]
    groups.append([k for k in range(n) if k not in groups[0]])

    down = jnp.swapaxes(adapter_down_maps, 1, 2).reshape(stored * rank, features)
    up = adapter_up_maps.reshape(stored * rank, features)
    pack = jnp.concatenate([down, up], axis=0)
    packs = {0: pack}
    for g in groups:
        for k in g:
            if k:
                packs[k] = shift(pack, "adapter", n, k)

    def across(part):
        return [shift(part, "tensor", tensors, k) for k in range(1, tensors)]

    def forward(blocks):
        return [shift(x, "sub", subs, 1) for x in blocks]

    parts = [cotangent[: extents[0]]]
    held_back, _ = lax.optimization_barrier((cotangent, pack))
    parts += [held_back[s : s + e] for s, e in zip(starts[1:], extents[1:])]
    direct = [across(parts[0]), across(parts[1])]
    pair = shift(cotangent, "sub", subs, 1)

    near = call(
        near_kernel,
        mib=20,
        flops=HEAVY,
        in_specs=[SMEM] + [VMEM] * 4,
        out_specs=VMEM,
        out_shape=jax.ShapeDtypeStruct((rows, features), f32),
    )(place, cotangent, pair, frozen_weight, activations)

    table = jax.ShapeDtypeStruct((n * cap,), jnp.int32)
    tile, live = call(
        functools.partial(plan_kernel, n, cap, tiles),
        in_specs=[SMEM] * 4 + [ANY] * len(direct[0]),
        out_specs=[SMEM] * 2,
        out_shape=[table] * 2,
        scratch_shapes=[pltpu.SMEM((n,), jnp.int32)],
    )(adapter_per_tile, live_per_tile, adapter_stored_row, me.astype(jnp.int32).reshape(1), *direct[0])

    def after(arrays):
        return [ANY] * len(arrays)

    def gate(blocks, ready):
        found = call(
            gate_kernel,
            in_specs=after(blocks) + [ANY],
            out_specs=after(blocks),
            out_shape=[jax.ShapeDtypeStruct(x.shape, x.dtype) for x in blocks],
            input_output_aliases={i: i for i in range(len(blocks))},
        )(*blocks, ready)
        return list(found)

    def ranks(g, *wait):
        extent = len(g) * cap * TILE
        half_shape = jax.ShapeDtypeStruct((extent // 2, 2 * rank), bf16)
        return call(
            functools.partial(rank_kernel, g, cap),
            in_specs=[SMEM] * 3 + [VMEM] * (2 + len(g)) + after(wait),
            out_specs=[VMEM] * 2,
            out_shape=[half_shape] * 2,
            scratch_shapes=[pltpu.VMEM((extent, 2 * rank), bf16)],
        )(tile, live, half, activations, cotangent, *[packs[k] for k in g], *wait)

    def chip_sum(keep, given, *wait):
        return call(
            functools.partial(sum_kernel, 2, -1),
            in_specs=[VMEM] * 2 + after(wait),
            out_specs=VMEM,
            out_shape=jax.ShapeDtypeStruct(keep.shape, bf16),
        )(keep, given, *wait)

    def slice_sum(keep, given, sent, held_parts, *wait):
        found = [keep, given, *across(sent)]
        shapes = [jax.ShapeDtypeStruct(x.shape, x.dtype) for x in held_parts]
        return call(
            functools.partial(sum_kernel, len(found), -1 - len(shapes)),
            in_specs=[VMEM] * len(found) + after(held_parts) + after(wait),
            out_specs=[VMEM] + after(held_parts),
            out_shape=[jax.ShapeDtypeStruct(keep.shape, bf16)] + shapes,
            input_output_aliases={len(found) + i: 1 + i for i in range(len(shapes))},
        )(*found, *held_parts, *wait)

    def adapter_terms(g, mine, other, *wait):
        extent = len(g) * cap * TILE
        found = call(
            functools.partial(terms_kernel, g, cap),
            in_specs=[SMEM] * 2 + [VMEM] * 4 + after(wait),
            out_specs=[VMEM] * len(g),
            out_shape=[jax.ShapeDtypeStruct((2 * rank, features), bf16)] * len(g),
            scratch_shapes=[pltpu.VMEM((extent, 2 * rank), bf16)],
        )(tile, half, mine, other, activations, cotangent, *wait)
        return dict(zip(g, found))

    first, second = groups
    forwards = [forward(direct[0])]
    keep, give = ranks(first, near, *forwards[0])
    given = shift(give, "sub", subs, 1)
    sent = chip_sum(keep, given, *direct[1])
    mine, part = slice_sum(keep, given, sent, parts[2:3], *[packs[k] for k in second])
    direct.append(across(part))
    other = shift(mine, "sub", subs, 1)
    sums = [mine, other]

    keep, give = ranks(second, other)
    terms = adapter_terms(first, mine, other, give)
    for c in (1, 2):
        direct[c] = gate(direct[c], terms[0])
        forwards.append(forward(direct[c]))
    given = shift(give, "sub", subs, 1)
    sent = chip_sum(keep, given, terms[0])
    mine, *rest = slice_sum(keep, given, sent, parts[3:], *direct[2])
    direct += [across(part) for part in rest]
    other = shift(mine, "sub", subs, 1)
    sums += [mine, other]
    arrived = {k: shift(terms[k], "adapter", n, -k) for k in first if k}
    terms |= adapter_terms(second, mine, other, *forwards[1], *forwards[2], *list(arrived.values())[:1])
    wait = [*list(arrived.values())[1:], terms[second[0]]]
    arrived |= {k: shift(terms[k], "adapter", n, -k) for k in second}

    blocks = [direct[c] + forwards[c] for c in range(3)]
    count = len(blocks[0])
    operands = [tile, half, place, *sums, *[packs[k] for k in range(n)], near, frozen_weight]
    operands += [x for block in blocks for x in block]
    whole_shape = jax.ShapeDtypeStruct((rows, features), bf16)
    out, term = call(
        functools.partial(middle_kernel, groups, cap, count),
        mib=20,
        flops=HEAVY,
        in_specs=[SMEM] * 3 + [VMEM] * (len(operands) - 3) + after(wait),
        out_specs=[HBM, VMEM],
        out_shape=[whole_shape] * 2,
        scratch_shapes=[pltpu.VMEM((len(g) * cap * TILE, 2 * rank), bf16) for g in groups]
        + [pltpu.VMEM((starts[3], features), bf16), pltpu.SemaphoreType.DMA],
    )(*operands, *wait)

    def far(c, out, *wait):
        operands = [place, near, term, frozen_weight, *direct[c], *forwards[c]]
        return call(
            functools.partial(far_kernel, count, starts[c]),
            mib=16,
            in_specs=[SMEM] + [VMEM] * (len(operands) - 1) + [HBM] + after(wait),
            out_specs=[HBM, VMEM],
            out_shape=[whole_shape, jax.ShapeDtypeStruct((8, 128), f32)],
            scratch_shapes=[pltpu.VMEM((extents[c], features), bf16), pltpu.SemaphoreType.DMA],
            input_output_aliases={len(operands): 0},
        )(*operands, out, *wait)

    maps_shape = jax.ShapeDtypeStruct((rank, features), bf16)
    down_grad, up_grad, token = call(
        functools.partial(final_kernel, n, (stored / rows) ** 0.5),
        in_specs=[VMEM] * n + [ANY],
        out_specs=[VMEM] * 3,
        out_shape=[maps_shape] * 2 + [jax.ShapeDtypeStruct((8, 128), f32)],
    )(terms[0], *[arrived[k] for k in range(1, n)], term)
    direct[3] = gate(direct[3], term)
    forwards.append(forward(direct[3]))
    out, token = far(3, out, token)
    direct[4] = gate(direct[4], token)
    forwards.append(forward(direct[4]))
    out, _ = far(4, out)
    down_grad = jnp.swapaxes(down_grad.reshape(stored, rank, features), 1, 2)
    up_grad = up_grad.reshape(stored, rank, features)
    return (out, down_grad, up_grad)


def solution(mesh):
    return jax.shard_map(
        on_device,
        mesh=mesh,
        in_specs=(
            P(("groups", "adapter"), ("tensor", "sub")),
            P(("groups", "adapter"), ("tensor", "sub")),
            P(("tensor", "sub"), None),
            P(("groups", "adapter"), ("tensor", "sub"), None),
            P(("groups", "adapter"), None, ("tensor", "sub")),
            P("groups"),
            P("groups"),
            P("groups"),
        ),
        out_specs=(
            P(("groups", "adapter"), ("tensor", "sub")),
            P(("groups", "adapter"), ("tensor", "sub"), None),
            P(("groups", "adapter"), None, ("tensor", "sub")),
        ),
        check_vma=False,
    )
```

```python
import functools

import jax
import jax.numpy as jnp
from jax import lax
from jax.experimental import pallas as pl
from jax.experimental.pallas import tpu as pltpu
from jax.sharding import PartitionSpec as P

TILE = 128
HEAVY = 1 << 36
CHUNKS = (4, 3, 3, 6)
NT = (((1,), (1,)), ((), ()))
SMEM = pl.BlockSpec(memory_space=pltpu.SMEM)
VMEM = pl.BlockSpec(memory_space=pltpu.VMEM)
ANY = pl.BlockSpec(memory_space=pl.ANY)
HBM = pl.BlockSpec(memory_space=pltpu.HBM)


def shift(array, axis, size, by):
    return lax.ppermute(array, axis, [(i, (i + by) % size) for i in range(size)])


def call(body, mib=12, flops=0, **kwargs):
    params = pltpu.CompilerParams(vmem_limit_bytes=mib * 1024 * 1024)
    cost = pl.CostEstimate(flops=flops, bytes_accessed=0, transcendentals=0)
    name = getattr(body, "func", body).__name__
    return pl.pallas_call(body, compiler_params=params, cost_estimate=cost, name=name, **kwargs)


def dot(a, b, dims=(((1,), (0,)), ((), ()))):
    return lax.dot_general(a, b, dims, preferred_element_type=jnp.float32)


def tile_rows(index):
    return pl.ds(pl.multiple_of(index * TILE, TILE), TILE)


def slot_rows(data, tile, entries):
    return jnp.concatenate([data[tile_rows(tile[e]), :] for e in entries], axis=0)


def head_kernel(cot, down, up, *refs):
    parts, pack, sems = refs[:-2], refs[-2], refs[-1]
    rank, start = down.shape[0], 0
    pairs = [(down, pack.at[pl.ds(0, rank), :]), (up, pack.at[pl.ds(rank, rank), :])]
    for part in parts:
        pairs.append((cot.at[pl.ds(start, part.shape[0]), :], part))
        start += part.shape[0]
    copies = [pltpu.make_async_copy(a, b, sems.at[i]) for i, (a, b) in enumerate(pairs)]
    for copy in copies:
        copy.start()
    for copy in copies:
        copy.wait()


def plan_kernel(n, cap, tiles, ids, live_all, stored, me, _, tile, live, count):
    for k in range(n):
        count[k] = 0
    for e in range(n * cap):
        tile[e] = 0
        live[e] = 0
    for t in range(tiles):
        at = me[0] * tiles + t
        k = lax.rem(me[0] - stored[ids[at]] + n, n)
        e = jnp.minimum(k * cap + count[k], n * cap - 1)
        tile[e] = t
        live[e] = live_all[at]
        count[k] = count[k] + 1


def rank_kernel(slots, cap, tile, live, act, cot, *refs):
    packs, out = refs[: len(slots)], refs[-1]
    width = packs[0].shape[0]
    part = lax.broadcasted_iota(jnp.int32, packs[0].shape, 0) < width // 2
    row = lax.broadcasted_iota(jnp.int32, (TILE, width), 0)
    for i, (slot, pack) in enumerate(zip(slots, packs)):
        entries = range(slot * cap, (slot + 1) * cap)
        maps = pack[...]
        zero = jnp.zeros_like(maps)
        both = dot(slot_rows(act, tile, entries), jnp.where(part, maps, zero), NT)
        both += dot(slot_rows(cot, tile, entries), jnp.where(part, zero, maps), NT)
        for c, e in enumerate(entries):
            at = (i * cap + c) * TILE
            out[at : at + TILE, :] = jnp.where(
                row < live[e], both[c * TILE : (c + 1) * TILE], 0.0
            ).astype(jnp.bfloat16)


def sum_kernel(count, place, *refs):
    total = refs[0][...].astype(jnp.float32)
    for x in refs[1:count]:
        total += x[...].astype(jnp.float32)
    out = refs[place]
    out[...] = total.astype(out.dtype)


def gate_kernel(*refs):
    pass


def terms_kernel(slots, cap, tile, held, act, cot, *refs):
    terms = refs[-len(slots) :]
    rank = held.shape[1] // 2
    for i, slot in enumerate(slots):
        entries = range(slot * cap, (slot + 1) * cap)
        both = held[i * cap * TILE : (i + 1) * cap * TILE, :].astype(jnp.float32)
        both = both.T.astype(jnp.bfloat16)
        terms[i][:rank, :] = dot(both[rank:], slot_rows(act, tile, entries)).astype(jnp.bfloat16)
        terms[i][rank:, :] = dot(both[:rank], slot_rows(cot, tile, entries)).astype(jnp.bfloat16)


def weight_columns(weight, place):
    features = weight.shape[0]
    return weight[:, pl.ds(pl.multiple_of(place * features, 128), features)]


def near_kernel(place, own, pair, weight, _, out):
    out[...] = dot(own[...], weight_columns(weight, place[0]), NT)
    out[...] += dot(pair[...], weight_columns(weight, place[1]), NT)


def row_sums(start, count, place, near, term, weight, blocks, out, done, sem):
    at = 0
    for first in range(0, len(blocks), count):
        extent = blocks[first].shape[0]
        rows = slice(start + at, start + at + extent)
        total = near[rows, :] + term[rows, :].astype(jnp.float32)
        for i in range(count):
            total += dot(blocks[first + i][...], weight_columns(weight, place[2 + i]), NT)
        done[at : at + extent, :] = total.astype(jnp.bfloat16)
        at += extent
    copy = pltpu.make_async_copy(done, out.at[pl.ds(start, at), :], sem)
    copy.start()
    copy.wait()


def middle_kernel(groups, cap, count, tile, place, *refs):
    n = sum(len(g) for g in groups)
    sums, refs = refs[: len(groups)], refs[len(groups) :]
    packs, (near, weight), refs = refs[:n], refs[n : n + 2], refs[n + 2 :]
    out, term, done, sem = refs[-4:]
    term[...] = jnp.zeros_like(term)
    for g, slots in enumerate(groups):
        for i, slot in enumerate(slots):
            maps = packs[slot][...]
            rank = maps.shape[0] // 2
            maps = jnp.concatenate([jnp.zeros_like(maps[:rank]), maps[:rank]], axis=0)
            found = dot(sums[g][i * cap * TILE : (i + 1) * cap * TILE, :], maps)
            for c in range(cap):
                rows = tile_rows(tile[slot * cap + c])
                before = term[rows, :].astype(jnp.float32)
                term[rows, :] = (before + found[c * TILE : (c + 1) * TILE]).astype(term.dtype)
    row_sums(0, count, place, near, term, weight, refs[: 2 * count], out, done, sem)


def far_kernel(count, start, place, near, term, weight, *refs):
    out, done, sem = refs[-3:]
    row_sums(start, count, place, near, term, weight, refs[: 2 * count], out, done, sem)


def final_kernel(count, scale, *refs):
    down, up, token = refs[-3:]
    token[...] = jnp.zeros_like(token)
    rank = down.shape[0]
    for out, rows in ((down, slice(0, rank)), (up, slice(rank, 2 * rank))):
        total = refs[0][rows, :].astype(jnp.float32)
        for x in refs[1:count]:
            total += x[rows, :].astype(jnp.float32)
        out[...] = (total * scale).astype(out.dtype)


def on_device(
    activations,
    cotangent,
    frozen_weight,
    adapter_down_maps,
    adapter_up_maps,
    adapter_per_tile,
    live_per_tile,
    adapter_stored_row,
):
    rows, features = activations.shape
    tiles = rows // TILE
    stored, _, rank = adapter_down_maps.shape
    n = lax.axis_size("adapter")
    tensors = lax.axis_size("tensor")
    subs = lax.axis_size("sub")
    me = lax.axis_index("adapter")
    t_me, s_me = lax.axis_index("tensor"), lax.axis_index("sub")
    extents = [rows * c // sum(CHUNKS) for c in CHUNKS]
    starts = [sum(extents[:c]) for c in range(len(extents))]
    bf16, f32 = jnp.bfloat16, jnp.float32

    cap = -(-tiles // n)
    places = [t_me * subs + s_me, t_me * subs + (1 - s_me)]
    for s in (s_me, 1 - s_me):
        places += [jnp.remainder(t_me - k, tensors) * subs + s for k in range(1, tensors)]
    place = jnp.stack(places).astype(jnp.int32)

    groups = [[k for k in range(n) if min(k, n - k) <= n // 4]]
    groups.append([k for k in range(n) if k not in groups[0]])

    down = jnp.swapaxes(adapter_down_maps, 1, 2).reshape(stored * rank, features)
    up = adapter_up_maps.reshape(stored * rank, features)
    *parts, pack = call(
        head_kernel,
        mib=56,
        in_specs=[ANY] * 3,
        out_specs=[ANY] * (len(extents) + 1),
        out_shape=[jax.ShapeDtypeStruct((e, features), bf16) for e in extents]
        + [jax.ShapeDtypeStruct((2 * rank, features), bf16)],
        scratch_shapes=[pltpu.SemaphoreType.DMA((len(extents) + 2,))],
    )(cotangent, down, up)
    packs = {0: pack}
    for g in groups:
        for k in g:
            if k:
                packs[k] = shift(pack, "adapter", n, k)

    def across(part):
        return [shift(part, "tensor", tensors, k) for k in range(1, tensors)]

    def forward(blocks):
        return [shift(x, "sub", subs, 1) for x in blocks]

    direct = [across(parts[0]), across(parts[1])]
    pair = shift(cotangent, "sub", subs, 1)

    table = jax.ShapeDtypeStruct((n * cap,), jnp.int32)
    tile, live = call(
        functools.partial(plan_kernel, n, cap, tiles),
        flops=HEAVY,
        in_specs=[SMEM] * 4 + [ANY],
        out_specs=[SMEM] * 2,
        out_shape=[table] * 2,
        scratch_shapes=[pltpu.SMEM((n,), jnp.int32)],
    )(adapter_per_tile, live_per_tile, adapter_stored_row, me.astype(jnp.int32).reshape(1), pair)

    def after(arrays):
        return [ANY] * len(arrays)

    def gate(blocks, ready):
        found = call(
            gate_kernel,
            in_specs=after(blocks) + [ANY],
            out_specs=after(blocks),
            out_shape=[jax.ShapeDtypeStruct(x.shape, x.dtype) for x in blocks],
            input_output_aliases={i: i for i in range(len(blocks))},
        )(*blocks, ready)
        return list(found)

    def ranks(g, *wait):
        return call(
            functools.partial(rank_kernel, g, cap),
            in_specs=[SMEM] * 2 + [VMEM] * (2 + len(g)) + after(wait),
            out_specs=VMEM,
            out_shape=jax.ShapeDtypeStruct((len(g) * cap * TILE, 2 * rank), bf16),
        )(tile, live, activations, cotangent, *[packs[k] for k in g], *wait)

    def chip_sum(own, *wait):
        given = shift(own, "sub", subs, 1)
        sent = call(
            functools.partial(sum_kernel, 2, -1),
            in_specs=[VMEM] * 2 + after(wait),
            out_specs=VMEM,
            out_shape=jax.ShapeDtypeStruct(own.shape, bf16),
        )(own, given, *wait)
        return given, sent

    def slice_sum(own, given, sent, held_parts, *wait):
        found = [own, given, *across(sent)]
        shapes = [jax.ShapeDtypeStruct(x.shape, x.dtype) for x in held_parts]
        return call(
            functools.partial(sum_kernel, len(found), -1 - len(shapes)),
            in_specs=[VMEM] * len(found) + after(held_parts) + after(wait),
            out_specs=[VMEM] + after(held_parts),
            out_shape=[jax.ShapeDtypeStruct(own.shape, bf16)] + shapes,
            input_output_aliases={len(found) + i: 1 + i for i in range(len(shapes))},
        )(*found, *held_parts, *wait)

    def adapter_terms(g, held, *wait):
        found = call(
            functools.partial(terms_kernel, g, cap),
            in_specs=[SMEM] + [VMEM] * 3 + after(wait),
            out_specs=[VMEM] * len(g),
            out_shape=[jax.ShapeDtypeStruct((2 * rank, features), bf16)] * len(g),
        )(tile, held, activations, cotangent, *wait)
        return dict(zip(g, found))

    first, second = groups
    own = ranks(first)
    forwards = [forward(direct[0])]
    given, sent = chip_sum(own, *direct[1])
    near = call(
        near_kernel,
        mib=20,
        flops=HEAVY,
        in_specs=[SMEM] + [VMEM] * 3 + [ANY],
        out_specs=VMEM,
        out_shape=jax.ShapeDtypeStruct((rows, features), f32),
    )(place, cotangent, pair, frozen_weight, sent)
    wait = [*forwards[0], near, *[packs[k] for k in second]]
    held, part = slice_sum(own, given, sent, parts[2:3], *wait)
    direct.append(across(part))
    sums = [held]

    own = ranks(second, held)
    terms = adapter_terms(first, held, own)
    forwards.append(forward(direct[1]))
    given, sent = chip_sum(own, terms[0])
    held, part = slice_sum(own, given, sent, parts[3:4], *forwards[1], *direct[2])
    direct.append(across(part))
    sums.append(held)
    arrived = {k: shift(terms[k], "adapter", n, -k) for k in first if k}
    blocks = [direct[c] + forwards[c] for c in range(2)]
    count = len(blocks[0])
    operands = [tile, place, *sums, *[packs[k] for k in range(n)], near, frozen_weight]
    operands += [x for block in blocks for x in block]
    whole_shape = jax.ShapeDtypeStruct((rows, features), bf16)
    out, term = call(
        functools.partial(middle_kernel, groups, cap, count),
        mib=20,
        flops=HEAVY,
        in_specs=[SMEM] * 2 + [VMEM] * (len(operands) - 2),
        out_specs=[HBM, VMEM],
        out_shape=[whole_shape] * 2,
        scratch_shapes=[pltpu.VMEM((starts[2], features), bf16), pltpu.SemaphoreType.DMA],
    )(*operands)

    terms |= adapter_terms(second, held, term, *arrived.values())
    arrived |= {k: shift(terms[k], "adapter", n, -k) for k in second}
    for c in (2, 3):
        direct[c] = gate(direct[c], terms[second[0]])
        forwards.append(forward(direct[c]))
    maps_shape = jax.ShapeDtypeStruct((rank, features), bf16)
    down_grad, up_grad, token = call(
        functools.partial(final_kernel, n, (stored / rows) ** 0.5),
        flops=HEAVY,
        in_specs=[VMEM] * n,
        out_specs=[VMEM] * 3,
        out_shape=[maps_shape] * 2 + [jax.ShapeDtypeStruct((8, 128), f32)],
    )(terms[0], *[arrived[k] for k in range(1, n)])
    blocks = [direct[c] + forwards[c] for c in (2, 3)]
    operands = [place, near, term, frozen_weight, *[x for block in blocks for x in block]]
    out = call(
        functools.partial(far_kernel, count, starts[2]),
        mib=16,
        in_specs=[SMEM] + [VMEM] * (len(operands) - 1) + [HBM, ANY],
        out_specs=HBM,
        out_shape=whole_shape,
        scratch_shapes=[pltpu.VMEM((rows - starts[2], features), bf16), pltpu.SemaphoreType.DMA],
        input_output_aliases={len(operands): 0},
    )(*operands, out, token)
    down_grad = jnp.swapaxes(down_grad.reshape(stored, rank, features), 1, 2)
    up_grad = up_grad.reshape(stored, rank, features)
    return (out, down_grad, up_grad)


def solution(mesh):
    return jax.shard_map(
        on_device,
        mesh=mesh,
        in_specs=(
            P(("groups", "adapter"), ("tensor", "sub")),
            P(("groups", "adapter"), ("tensor", "sub")),
            P(("tensor", "sub"), None),
            P(("groups", "adapter"), ("tensor", "sub"), None),
            P(("groups", "adapter"), None, ("tensor", "sub")),
            P("groups"),
            P("groups"),
            P("groups"),
        ),
        out_specs=(
            P(("groups", "adapter"), ("tensor", "sub")),
            P(("groups", "adapter"), ("tensor", "sub"), None),
            P(("groups", "adapter"), None, ("tensor", "sub")),
        ),
        check_vma=False,
    )
```

```python
import functools

import jax
import jax.numpy as jnp
from jax import lax
from jax.experimental import pallas as pl
from jax.experimental.pallas import tpu as pltpu
from jax.sharding import PartitionSpec as P

TILE = 128
HEAVY = 1 << 36
CHUNKS = (2, 6, 4, 4)
NT = (((1,), (1,)), ((), ()))
SMEM = pl.BlockSpec(memory_space=pltpu.SMEM)
VMEM = pl.BlockSpec(memory_space=pltpu.VMEM)
ANY = pl.BlockSpec(memory_space=pl.ANY)
HBM = pl.BlockSpec(memory_space=pltpu.HBM)


def shift(array, axis, size, by):
    return lax.ppermute(array, axis, [(i, (i + by) % size) for i in range(size)])


def call(body, mib=12, flops=0, **kwargs):
    params = pltpu.CompilerParams(vmem_limit_bytes=mib * 1024 * 1024)
    cost = pl.CostEstimate(flops=flops, bytes_accessed=0, transcendentals=0)
    name = getattr(body, "func", body).__name__
    return pl.pallas_call(body, compiler_params=params, cost_estimate=cost, name=name, **kwargs)


def dot(a, b, dims=(((1,), (0,)), ((), ()))):
    return lax.dot_general(a, b, dims, preferred_element_type=jnp.float32)


def tile_rows(index):
    return pl.ds(pl.multiple_of(index * TILE, TILE), TILE)


def slot_rows(data, tile, entries):
    return jnp.concatenate([data[tile_rows(tile[e]), :] for e in entries], axis=0)


def copy_all(pairs, sems):
    copies = [pltpu.make_async_copy(a, b, sems.at[i]) for i, (a, b) in enumerate(pairs)]
    for copy in copies:
        copy.start()
    return copies


def head_kernel(cot, down, up, *refs):
    *outs, held, pack_held, sems = refs
    count, rank, start = len(outs), down.shape[0], 0
    here = []
    for part in outs[:-1]:
        here.append(held.at[pl.ds(start, part.shape[0]), :])
        start += part.shape[0]
    loads = [(down, pack_held.at[pl.ds(0, rank), :]), (up, pack_held.at[pl.ds(rank, rank), :])]
    start = 0
    for place in here:
        loads.append((cot.at[pl.ds(start, place.shape[0]), :], place))
        start += place.shape[0]
    loads = copy_all(loads, sems.at[0])
    stores = []
    for i, (place, part) in enumerate(zip([pack_held, *here], [outs[-1], *outs[:-1]])):
        for load in loads[:2] if i == 0 else [loads[i + 1]]:
            load.wait()
        stores.append(pltpu.make_async_copy(place, part, sems.at[1, i]))
        stores[-1].start()
    for store in stores:
        store.wait()


def plan_kernel(n, cap, tiles, ids, live_all, stored, me, tile, live, count):
    for k in range(n):
        count[k] = 0
    for e in range(n * cap):
        tile[e] = 0
        live[e] = 0
    for t in range(tiles):
        at = me[0] * tiles + t
        k = lax.rem(me[0] - stored[ids[at]] + n, n)
        e = jnp.minimum(k * cap + count[k], n * cap - 1)
        tile[e] = t
        live[e] = live_all[at]
        count[k] = count[k] + 1


def rank_kernel(slots, cap, tile, live, act, cot, *refs):
    packs, out = refs[: len(slots)], refs[-1]
    width = packs[0].shape[0]
    part = lax.broadcasted_iota(jnp.int32, packs[0].shape, 0) < width // 2
    row = lax.broadcasted_iota(jnp.int32, (TILE, width), 0)
    for i, (slot, pack) in enumerate(zip(slots, packs)):
        entries = range(slot * cap, (slot + 1) * cap)
        maps = pack[...]
        zero = jnp.zeros_like(maps)
        both = dot(slot_rows(act, tile, entries), jnp.where(part, maps, zero), NT)
        both += dot(slot_rows(cot, tile, entries), jnp.where(part, zero, maps), NT)
        for c, e in enumerate(entries):
            at = (i * cap + c) * TILE
            out[at : at + TILE, :] = jnp.where(
                row < live[e], both[c * TILE : (c + 1) * TILE], 0.0
            ).astype(jnp.bfloat16)


def sum_kernel(count, place, *refs):
    total = refs[0][...].astype(jnp.float32)
    for x in refs[1:count]:
        total += x[...].astype(jnp.float32)
    out = refs[place]
    out[...] = total.astype(out.dtype)


def gate_kernel(*refs):
    pass


def terms_kernel(slots, cap, tile, held, act, cot, *refs):
    terms = refs[-len(slots) :]
    rank = held.shape[1] // 2
    for i, slot in enumerate(slots):
        entries = range(slot * cap, (slot + 1) * cap)
        both = held[i * cap * TILE : (i + 1) * cap * TILE, :].astype(jnp.float32)
        both = both.T.astype(jnp.bfloat16)
        terms[i][:rank, :] = dot(both[rank:], slot_rows(act, tile, entries)).astype(jnp.bfloat16)
        terms[i][rank:, :] = dot(both[:rank], slot_rows(cot, tile, entries)).astype(jnp.bfloat16)


def weight_columns(weight, place):
    features = weight.shape[0]
    return weight[:, pl.ds(pl.multiple_of(place * features, 128), features)]


def near_kernel(place, own, pair, weight, *refs):
    out = refs[-1]
    out[...] = dot(own[...], weight_columns(weight, place[0]), NT)
    out[...] += dot(pair[...], weight_columns(weight, place[1]), NT)


def row_sums(start, count, place, near, term, weight, blocks, out, done, sem):
    at = 0
    for first in range(0, len(blocks), count):
        extent = blocks[first].shape[0]
        rows = slice(start + at, start + at + extent)
        total = near[rows, :] + term[rows, :].astype(jnp.float32)
        for i in range(count):
            total += dot(blocks[first + i][...], weight_columns(weight, place[2 + i]), NT)
        done[at : at + extent, :] = total.astype(jnp.bfloat16)
        at += extent
    copy = pltpu.make_async_copy(done, out.at[pl.ds(start, at), :], sem)
    copy.start()
    copy.wait()


def middle_kernel(groups, cap, count, tile, place, *refs):
    n = sum(len(g) for g in groups)
    sums, refs = refs[: len(groups)], refs[len(groups) :]
    packs, (near, weight), refs = refs[:n], refs[n : n + 2], refs[n + 2 :]
    out, term, done, sem = refs[-4:]
    term[...] = jnp.zeros_like(term)
    for g, slots in enumerate(groups):
        for i, slot in enumerate(slots):
            maps = packs[slot][...]
            rank = maps.shape[0] // 2
            maps = jnp.concatenate([jnp.zeros_like(maps[:rank]), maps[:rank]], axis=0)
            found = dot(sums[g][i * cap * TILE : (i + 1) * cap * TILE, :], maps)
            for c in range(cap):
                rows = tile_rows(tile[slot * cap + c])
                before = term[rows, :].astype(jnp.float32)
                term[rows, :] = (before + found[c * TILE : (c + 1) * TILE]).astype(term.dtype)
    row_sums(0, count, place, near, term, weight, refs[: 2 * count], out, done, sem)


def far_kernel(count, start, place, near, term, weight, *refs):
    out, done, sem = refs[-3:]
    row_sums(start, count, place, near, term, weight, refs[: 2 * count], out, done, sem)


def final_kernel(count, scale, *refs):
    down, up, token = refs[-3:]
    token[...] = jnp.zeros_like(token)
    rank = down.shape[0]
    for out, rows in ((down, slice(0, rank)), (up, slice(rank, 2 * rank))):
        total = refs[0][rows, :].astype(jnp.float32)
        for x in refs[1:count]:
            total += x[rows, :].astype(jnp.float32)
        out[...] = (total * scale).astype(out.dtype)


def on_device(
    activations,
    cotangent,
    frozen_weight,
    adapter_down_maps,
    adapter_up_maps,
    adapter_per_tile,
    live_per_tile,
    adapter_stored_row,
):
    rows, features = activations.shape
    tiles = rows // TILE
    stored, _, rank = adapter_down_maps.shape
    n = lax.axis_size("adapter")
    tensors = lax.axis_size("tensor")
    subs = lax.axis_size("sub")
    me = lax.axis_index("adapter")
    t_me, s_me = lax.axis_index("tensor"), lax.axis_index("sub")
    extents = [rows * c // sum(CHUNKS) for c in CHUNKS]
    starts = [sum(extents[:c]) for c in range(len(extents))]
    bf16, f32 = jnp.bfloat16, jnp.float32

    cap = -(-tiles // n)
    places = [t_me * subs + s_me, t_me * subs + (1 - s_me)]
    for s in (s_me, 1 - s_me):
        places += [jnp.remainder(t_me - k, tensors) * subs + s for k in range(1, tensors)]
    place = jnp.stack(places).astype(jnp.int32)

    groups = [[k for k in range(n) if 1 <= min(k, n - k) <= n // 4]]
    groups.append([k for k in range(n) if k not in groups[0]])

    down = jnp.swapaxes(adapter_down_maps, 1, 2).reshape(stored * rank, features)
    up = adapter_up_maps.reshape(stored * rank, features)
    *parts, pack = call(
        head_kernel,
        mib=56,
        in_specs=[ANY] * 3,
        out_specs=[ANY] * (len(extents) + 1),
        out_shape=[jax.ShapeDtypeStruct((e, features), bf16) for e in extents]
        + [jax.ShapeDtypeStruct((2 * rank, features), bf16)],
        scratch_shapes=[
            pltpu.VMEM((rows, features), bf16),
            pltpu.VMEM((2 * rank, features), bf16),
            pltpu.SemaphoreType.DMA((2, len(extents) + 2)),
        ],
    )(cotangent, down, up)
    packs = {0: pack}
    for g in groups:
        for k in g:
            if k:
                packs[k] = shift(pack, "adapter", n, k)

    def across(part):
        return [shift(part, "tensor", tensors, k) for k in range(1, tensors)]

    def forward(blocks):
        return [shift(x, "sub", subs, 1) for x in blocks]

    direct = [across(parts[0]), across(parts[1])]
    pair = shift(cotangent, "sub", subs, 1)

    table = jax.ShapeDtypeStruct((n * cap,), jnp.int32)
    tile, live = call(
        functools.partial(plan_kernel, n, cap, tiles),
        flops=HEAVY,
        in_specs=[SMEM] * 4,
        out_specs=[SMEM] * 2,
        out_shape=[table] * 2,
        scratch_shapes=[pltpu.SMEM((n,), jnp.int32)],
    )(adapter_per_tile, live_per_tile, adapter_stored_row, me.astype(jnp.int32).reshape(1))

    def after(arrays):
        return [ANY] * len(arrays)

    def gate(blocks, ready):
        found = call(
            gate_kernel,
            in_specs=after(blocks) + [ANY],
            out_specs=after(blocks),
            out_shape=[jax.ShapeDtypeStruct(x.shape, x.dtype) for x in blocks],
            input_output_aliases={i: i for i in range(len(blocks))},
        )(*blocks, ready)
        return list(found)

    def ranks(g, *wait):
        return call(
            functools.partial(rank_kernel, g, cap),
            in_specs=[SMEM] * 2 + [VMEM] * (2 + len(g)) + after(wait),
            out_specs=VMEM,
            out_shape=jax.ShapeDtypeStruct((len(g) * cap * TILE, 2 * rank), bf16),
        )(tile, live, activations, cotangent, *[packs[k] for k in g], *wait)

    def chip_sum(own, *wait):
        given = shift(own, "sub", subs, 1)
        sent = call(
            functools.partial(sum_kernel, 2, -1),
            in_specs=[VMEM] * 2 + after(wait),
            out_specs=VMEM,
            out_shape=jax.ShapeDtypeStruct(own.shape, bf16),
        )(own, given, *wait)
        return given, sent

    def slice_sum(own, given, sent, held_parts, *wait):
        found = [own, given, *across(sent)]
        shapes = [jax.ShapeDtypeStruct(x.shape, x.dtype) for x in held_parts]
        return call(
            functools.partial(sum_kernel, len(found), -1 - len(shapes)),
            in_specs=[VMEM] * len(found) + after(held_parts) + after(wait),
            out_specs=[VMEM] + after(held_parts),
            out_shape=[jax.ShapeDtypeStruct(own.shape, bf16)] + shapes,
            input_output_aliases={len(found) + i: 1 + i for i in range(len(shapes))},
        )(*found, *held_parts, *wait)

    def adapter_terms(g, held, *wait):
        found = call(
            functools.partial(terms_kernel, g, cap),
            in_specs=[SMEM] + [VMEM] * 3 + after(wait),
            out_specs=[VMEM] * len(g),
            out_shape=[jax.ShapeDtypeStruct((2 * rank, features), bf16)] * len(g),
        )(tile, held, activations, cotangent, *wait)
        return dict(zip(g, found))

    near = call(
        near_kernel,
        flops=HEAVY,
        in_specs=[SMEM] + [VMEM] * 3 + after(direct[0]),
        out_specs=VMEM,
        out_shape=jax.ShapeDtypeStruct((rows, features), f32),
    )(place, cotangent, pair, frozen_weight, *direct[0])

    first, second = groups
    own = ranks(first, near)
    forwards = [forward(direct[0])]
    given, sent = chip_sum(own, *direct[1])
    held, part = slice_sum(own, given, sent, parts[2:3], *forwards[0])
    direct.append(across(part))
    sums = [held]

    terms = adapter_terms(first, held)
    own = ranks(second, terms[first[0]])
    forwards.append(forward(direct[1]))
    arrived = {k: shift(terms[k], "adapter", n, -k) for k in first}
    early, late = list(arrived.values())[: len(first) // 2], list(arrived.values())[len(first) // 2 :]
    given, sent = chip_sum(own, *early)
    held, part = slice_sum(own, given, sent, parts[3:4], *forwards[1], *direct[2], *late)
    direct.append(across(part))
    sums.append(held)
    terms |= adapter_terms(second, held)
    blocks = [direct[c] + forwards[c] for c in range(2)]
    count = len(blocks[0])
    operands = [tile, place, *sums, *[packs[k] for k in range(n)], near, frozen_weight]
    operands += [x for block in blocks for x in block]
    whole_shape = jax.ShapeDtypeStruct((rows, features), bf16)
    out, term = call(
        functools.partial(middle_kernel, groups, cap, count),
        mib=20,
        flops=HEAVY,
        in_specs=[SMEM] * 2 + [VMEM] * (len(operands) - 2) + [ANY],
        out_specs=[HBM, VMEM],
        out_shape=[whole_shape] * 2,
        scratch_shapes=[pltpu.VMEM((starts[2], features), bf16), pltpu.SemaphoreType.DMA],
    )(*operands, terms[second[-1]])

    arrived |= {k: shift(terms[k], "adapter", n, -k) for k in second if k}
    for c in (2, 3):
        direct[c] = gate(direct[c], term)
        forwards.append(forward(direct[c]))
    maps_shape = jax.ShapeDtypeStruct((rank, features), bf16)
    down_grad, up_grad, token = call(
        functools.partial(final_kernel, n, (stored / rows) ** 0.5),
        flops=HEAVY,
        in_specs=[VMEM] * n,
        out_specs=[VMEM] * 3,
        out_shape=[maps_shape] * 2 + [jax.ShapeDtypeStruct((8, 128), f32)],
    )(terms[0], *[arrived[k] for k in range(1, n)])
    blocks = [direct[c] + forwards[c] for c in (2, 3)]
    operands = [place, near, term, frozen_weight, *[x for block in blocks for x in block]]
    out = call(
        functools.partial(far_kernel, count, starts[2]),
        mib=16,
        in_specs=[SMEM] + [VMEM] * (len(operands) - 1) + [HBM, ANY],
        out_specs=HBM,
        out_shape=whole_shape,
        scratch_shapes=[pltpu.VMEM((rows - starts[2], features), bf16), pltpu.SemaphoreType.DMA],
        input_output_aliases={len(operands): 0},
    )(*operands, out, token)
    down_grad = jnp.swapaxes(down_grad.reshape(stored, rank, features), 1, 2)
    up_grad = up_grad.reshape(stored, rank, features)
    return (out, down_grad, up_grad)


def solution(mesh):
    return jax.shard_map(
        on_device,
        mesh=mesh,
        in_specs=(
            P(("groups", "adapter"), ("tensor", "sub")),
            P(("groups", "adapter"), ("tensor", "sub")),
            P(("tensor", "sub"), None),
            P(("groups", "adapter"), ("tensor", "sub"), None),
            P(("groups", "adapter"), None, ("tensor", "sub")),
            P("groups"),
            P("groups"),
            P("groups"),
        ),
        out_specs=(
            P(("groups", "adapter"), ("tensor", "sub")),
            P(("groups", "adapter"), ("tensor", "sub"), None),
            P(("groups", "adapter"), None, ("tensor", "sub")),
        ),
        check_vma=False,
    )
```

```python
import functools

import jax
import jax.numpy as jnp
from jax import lax
from jax.experimental import pallas as pl
from jax.experimental.pallas import tpu as pltpu
from jax.sharding import PartitionSpec as P

TILE = 128
HEAVY = 1 << 36
CHUNKS = (2, 8, 6)
NT = (((1,), (1,)), ((), ()))
SMEM = pl.BlockSpec(memory_space=pltpu.SMEM)
VMEM = pl.BlockSpec(memory_space=pltpu.VMEM)
ANY = pl.BlockSpec(memory_space=pl.ANY)
HBM = pl.BlockSpec(memory_space=pltpu.HBM)


def shift(array, axis, size, by):
    return lax.ppermute(array, axis, [(i, (i + by) % size) for i in range(size)])


def call(body, mib=12, flops=0, **kwargs):
    params = pltpu.CompilerParams(vmem_limit_bytes=mib * 1024 * 1024)
    cost = pl.CostEstimate(flops=flops, bytes_accessed=0, transcendentals=0)
    name = getattr(body, "func", body).__name__
    return pl.pallas_call(body, compiler_params=params, cost_estimate=cost, name=name, **kwargs)


def dot(a, b, dims=(((1,), (0,)), ((), ()))):
    return lax.dot_general(a, b, dims, preferred_element_type=jnp.float32)


def tile_rows(index):
    return pl.ds(pl.multiple_of(index * TILE, TILE), TILE)


def slot_rows(data, tile, entries):
    return jnp.concatenate([data[tile_rows(tile[e]), :] for e in entries], axis=0)


def copy_all(pairs, sems):
    copies = [pltpu.make_async_copy(a, b, sems.at[i]) for i, (a, b) in enumerate(pairs)]
    for copy in copies:
        copy.start()
    return copies


def head_kernel(cot, down, up, *refs):
    *outs, held, pack_held, sems = refs
    count, rank, start = len(outs), down.shape[0], 0
    here = []
    for part in outs[:-1]:
        here.append(held.at[pl.ds(start, part.shape[0]), :])
        start += part.shape[0]
    loads = [(down, pack_held.at[pl.ds(0, rank), :]), (up, pack_held.at[pl.ds(rank, rank), :])]
    start = 0
    for place in here:
        loads.append((cot.at[pl.ds(start, place.shape[0]), :], place))
        start += place.shape[0]
    loads = copy_all(loads, sems.at[0])
    stores = []
    for i, (place, part) in enumerate(zip([pack_held, *here], [outs[-1], *outs[:-1]])):
        for load in loads[:2] if i == 0 else [loads[i + 1]]:
            load.wait()
        stores.append(pltpu.make_async_copy(place, part, sems.at[1, i]))
        stores[-1].start()
    for store in stores:
        store.wait()


def plan_kernel(n, cap, tiles, ids, live_all, stored, me, tile, live, count):
    for k in range(n):
        count[k] = 0
    for e in range(n * cap):
        tile[e] = 0
        live[e] = 0
    for t in range(tiles):
        at = me[0] * tiles + t
        k = lax.rem(me[0] - stored[ids[at]] + n, n)
        e = jnp.minimum(k * cap + count[k], n * cap - 1)
        tile[e] = t
        live[e] = live_all[at]
        count[k] = count[k] + 1


def rank_kernel(slots, cap, tile, live, act, cot, *refs):
    packs, out = refs[: len(slots)], refs[-1]
    width = packs[0].shape[0]
    part = lax.broadcasted_iota(jnp.int32, packs[0].shape, 0) < width // 2
    row = lax.broadcasted_iota(jnp.int32, (TILE, width), 0)
    for i, (slot, pack) in enumerate(zip(slots, packs)):
        entries = range(slot * cap, (slot + 1) * cap)
        maps = pack[...]
        zero = jnp.zeros_like(maps)
        both = dot(slot_rows(act, tile, entries), jnp.where(part, maps, zero), NT)
        both += dot(slot_rows(cot, tile, entries), jnp.where(part, zero, maps), NT)
        for c, e in enumerate(entries):
            at = (i * cap + c) * TILE
            out[at : at + TILE, :] = jnp.where(
                row < live[e], both[c * TILE : (c + 1) * TILE], 0.0
            ).astype(jnp.bfloat16)


def sum_kernel(count, place, *refs):
    total = refs[0][...].astype(jnp.float32)
    for x in refs[1:count]:
        total += x[...].astype(jnp.float32)
    out = refs[place]
    out[...] = total.astype(out.dtype)


def gate_kernel(*refs):
    pass


def terms_kernel(slots, cap, tile, held, act, cot, *refs):
    terms = refs[-len(slots) :]
    rank = held.shape[1] // 2
    for i, slot in enumerate(slots):
        entries = range(slot * cap, (slot + 1) * cap)
        both = held[i * cap * TILE : (i + 1) * cap * TILE, :].astype(jnp.float32)
        both = both.T.astype(jnp.bfloat16)
        terms[i][:rank, :] = dot(both[rank:], slot_rows(act, tile, entries)).astype(jnp.bfloat16)
        terms[i][rank:, :] = dot(both[:rank], slot_rows(cot, tile, entries)).astype(jnp.bfloat16)


def weight_columns(weight, place):
    features = weight.shape[0]
    return weight[:, pl.ds(pl.multiple_of(place * features, 128), features)]


def near_kernel(place, own, pair, weight, *refs):
    out = refs[-1]
    out[...] = dot(own[...], weight_columns(weight, place[0]), NT)
    out[...] += dot(pair[...], weight_columns(weight, place[1]), NT)


def row_sums(start, count, place, near, term, weight, blocks, out, done, sem):
    at = 0
    for first in range(0, len(blocks), count):
        extent = blocks[first].shape[0]
        rows = slice(start + at, start + at + extent)
        total = near[rows, :] + term[rows, :].astype(jnp.float32)
        for i in range(count):
            total += dot(blocks[first + i][...], weight_columns(weight, place[2 + i]), NT)
        done[at : at + extent, :] = total.astype(jnp.bfloat16)
        at += extent
    copy = pltpu.make_async_copy(done, out.at[pl.ds(start, at), :], sem)
    copy.start()
    copy.wait()


def middle_kernel(groups, cap, count, tile, place, *refs):
    n = sum(len(g) for g in groups)
    sums, refs = refs[: len(groups)], refs[len(groups) :]
    packs, (near, weight), refs = refs[:n], refs[n : n + 2], refs[n + 2 :]
    out, term, done, sem = refs[-4:]
    term[...] = jnp.zeros_like(term)
    for g, slots in enumerate(groups):
        for i, slot in enumerate(slots):
            maps = packs[slot][...]
            rank = maps.shape[0] // 2
            maps = jnp.concatenate([jnp.zeros_like(maps[:rank]), maps[:rank]], axis=0)
            found = dot(sums[g][i * cap * TILE : (i + 1) * cap * TILE, :], maps)
            for c in range(cap):
                rows = tile_rows(tile[slot * cap + c])
                before = term[rows, :].astype(jnp.float32)
                term[rows, :] = (before + found[c * TILE : (c + 1) * TILE]).astype(term.dtype)
    row_sums(0, count, place, near, term, weight, refs[: 2 * count], out, done, sem)


def far_kernel(count, start, place, near, term, weight, *refs):
    out, done, sem = refs[-3:]
    row_sums(start, count, place, near, term, weight, refs[:count], out, done, sem)


def final_kernel(count, scale, *refs):
    down, up, token = refs[-3:]
    token[...] = jnp.zeros_like(token)
    rank = down.shape[0]
    for out, rows in ((down, slice(0, rank)), (up, slice(rank, 2 * rank))):
        total = refs[0][rows, :].astype(jnp.float32)
        for x in refs[1:count]:
            total += x[rows, :].astype(jnp.float32)
        out[...] = (total * scale).astype(out.dtype)


def on_device(
    activations,
    cotangent,
    frozen_weight,
    adapter_down_maps,
    adapter_up_maps,
    adapter_per_tile,
    live_per_tile,
    adapter_stored_row,
):
    rows, features = activations.shape
    tiles = rows // TILE
    stored, _, rank = adapter_down_maps.shape
    n = lax.axis_size("adapter")
    tensors = lax.axis_size("tensor")
    subs = lax.axis_size("sub")
    me = lax.axis_index("adapter")
    t_me, s_me = lax.axis_index("tensor"), lax.axis_index("sub")
    extents = [rows * c // sum(CHUNKS) for c in CHUNKS]
    starts = [sum(extents[:c]) for c in range(len(extents))]
    bf16, f32 = jnp.bfloat16, jnp.float32

    cap = -(-tiles // n)
    places = [t_me * subs + s_me, t_me * subs + (1 - s_me)]
    for s in (s_me, 1 - s_me):
        places += [jnp.remainder(t_me - k, tensors) * subs + s for k in range(1, tensors)]
    place = jnp.stack(places).astype(jnp.int32)

    groups = [[k for k in range(n) if min(k, n - k) <= n // 4]]
    groups.append([k for k in range(n) if k not in groups[0]])

    down = jnp.swapaxes(adapter_down_maps, 1, 2).reshape(stored * rank, features)
    up = adapter_up_maps.reshape(stored * rank, features)
    *parts, pack = call(
        head_kernel,
        mib=56,
        in_specs=[ANY] * 3,
        out_specs=[ANY] * (len(extents) + 1),
        out_shape=[jax.ShapeDtypeStruct((e, features), bf16) for e in extents]
        + [jax.ShapeDtypeStruct((2 * rank, features), bf16)],
        scratch_shapes=[
            pltpu.VMEM((rows, features), bf16),
            pltpu.VMEM((2 * rank, features), bf16),
            pltpu.SemaphoreType.DMA((2, len(extents) + 2)),
        ],
    )(cotangent, down, up)
    def across(part, aside=0):
        slice_axes, found = ("tensor", "sub"), []
        for k in range(1, tensors):
            to = [(t + k) % tensors * subs + (s + aside) % subs for t in range(tensors) for s in range(subs)]
            found.append(lax.ppermute(part, slice_axes, list(enumerate(to))))
        return found

    def forward(blocks):
        return [shift(x, "sub", subs, 1) for x in blocks]

    direct = [across(parts[0]), across(parts[1])]
    pair = shift(cotangent, "sub", subs, 1)
    packs = {0: pack}
    for g in groups:
        for k in g:
            if k:
                packs[k] = shift(pack, "adapter", n, k)


    table = jax.ShapeDtypeStruct((n * cap,), jnp.int32)
    tile, live = call(
        functools.partial(plan_kernel, n, cap, tiles),
        flops=HEAVY,
        in_specs=[SMEM] * 4,
        out_specs=[SMEM] * 2,
        out_shape=[table] * 2,
        scratch_shapes=[pltpu.SMEM((n,), jnp.int32)],
    )(adapter_per_tile, live_per_tile, adapter_stored_row, me.astype(jnp.int32).reshape(1))

    def after(arrays):
        return [ANY] * len(arrays)

    def gate(blocks, ready):
        found = call(
            gate_kernel,
            in_specs=after(blocks) + [ANY],
            out_specs=after(blocks),
            out_shape=[jax.ShapeDtypeStruct(x.shape, x.dtype) for x in blocks],
            input_output_aliases={i: i for i in range(len(blocks))},
        )(*blocks, ready)
        return list(found)

    def ranks(g, *wait):
        return call(
            functools.partial(rank_kernel, g, cap),
            in_specs=[SMEM] * 2 + [VMEM] * (2 + len(g)) + after(wait),
            out_specs=VMEM,
            out_shape=jax.ShapeDtypeStruct((len(g) * cap * TILE, 2 * rank), bf16),
        )(tile, live, activations, cotangent, *[packs[k] for k in g], *wait)

    def chip_sum(own, *wait):
        given = shift(own, "sub", subs, 1)
        sent = call(
            functools.partial(sum_kernel, 2, -1),
            in_specs=[VMEM] * 2 + after(wait),
            out_specs=VMEM,
            out_shape=jax.ShapeDtypeStruct(own.shape, bf16),
        )(own, given, *wait)
        return given, sent

    def slice_sum(own, given, others, held_parts, *wait):
        found = [own, given, *others]
        shapes = [jax.ShapeDtypeStruct(x.shape, x.dtype) for x in held_parts]
        return call(
            functools.partial(sum_kernel, len(found), -1 - len(shapes)),
            in_specs=[VMEM] * len(found) + after(held_parts) + after(wait),
            out_specs=[VMEM] + after(held_parts),
            out_shape=[jax.ShapeDtypeStruct(own.shape, bf16)] + shapes,
            input_output_aliases={len(found) + i: 1 + i for i in range(len(shapes))},
        )(*found, *held_parts, *wait)

    def adapter_terms(g, held, *wait):
        found = call(
            functools.partial(terms_kernel, g, cap),
            in_specs=[SMEM] + [VMEM] * 3 + after(wait),
            out_specs=[VMEM] * len(g),
            out_shape=[jax.ShapeDtypeStruct((2 * rank, features), bf16)] * len(g),
        )(tile, held, activations, cotangent, *wait)
        return dict(zip(g, found))

    near = call(
        near_kernel,
        flops=HEAVY,
        in_specs=[SMEM] + [VMEM] * 3 + after(direct[0]),
        out_specs=VMEM,
        out_shape=jax.ShapeDtypeStruct((rows, features), f32),
    )(place, cotangent, pair, frozen_weight, *direct[0])

    first, second = groups
    own = ranks(first, near)
    more = ranks(second, own)
    given, sent = chip_sum(own, *direct[1], more)
    given_more, sent_more = chip_sum(more, sent)
    forwards = [forward(direct[0])]
    others, others_more = across(sent), across(sent_more)
    (held,) = slice_sum(own, given, others, [], *others_more, *forwards[0])
    held_more, part = slice_sum(more, given_more, others_more, parts[2:], held)
    sums = [held, held_more]
    direct.append(across(part))
    terms = adapter_terms(first, held, held_more)
    terms |= adapter_terms(second, held_more)
    direct[1] = gate(direct[1], held)
    forwards.append(forward(direct[1]))
    arrived = {k: shift(terms[k], "adapter", n, -k) for g in groups for k in g if k}

    blocks = [direct[c] + forwards[c] for c in range(2)]
    count = len(blocks[0])
    operands = [tile, place, *sums, *[packs[k] for k in range(n)], near, frozen_weight]
    operands += [x for block in blocks for x in block]
    whole_shape = jax.ShapeDtypeStruct((rows, features), bf16)
    out, term = call(
        functools.partial(middle_kernel, groups, cap, count),
        mib=20,
        flops=HEAVY,
        in_specs=[SMEM] * 2 + [VMEM] * (len(operands) - 2) + [ANY],
        out_specs=[HBM, VMEM],
        out_shape=[whole_shape] * 2,
        scratch_shapes=[pltpu.VMEM((starts[2], features), bf16), pltpu.SemaphoreType.DMA],
    )(*operands, terms[second[-1]])

    direct[2] = gate(direct[2], term)
    forwards.append(forward(direct[2]))
    maps_shape = jax.ShapeDtypeStruct((rank, features), bf16)
    token_shape = jax.ShapeDtypeStruct((8, 128), f32)
    down_grad, up_grad, token = call(
        functools.partial(final_kernel, n, (stored / rows) ** 0.5),
        flops=HEAVY,
        in_specs=[VMEM] * n,
        out_specs=[VMEM] * 3,
        out_shape=[maps_shape] * 2 + [token_shape],
    )(terms[0], *[arrived[k] for k in range(1, n)])
    operands = [place, near, term, frozen_weight, *direct[2], *forwards[2]]
    out = call(
        functools.partial(far_kernel, count, starts[2]),
        mib=16,
        in_specs=[SMEM] + [VMEM] * (len(operands) - 1) + [HBM, VMEM],
        out_specs=HBM,
        out_shape=whole_shape,
        scratch_shapes=[pltpu.VMEM((rows - starts[2], features), bf16), pltpu.SemaphoreType.DMA],
        input_output_aliases={len(operands): 0},
    )(*operands, out, token)
    down_grad = jnp.swapaxes(down_grad.reshape(stored, rank, features), 1, 2)
    up_grad = up_grad.reshape(stored, rank, features)
    return (out, down_grad, up_grad)


def solution(mesh):
    return jax.shard_map(
        on_device,
        mesh=mesh,
        in_specs=(
            P(("groups", "adapter"), ("tensor", "sub")),
            P(("groups", "adapter"), ("tensor", "sub")),
            P(("tensor", "sub"), None),
            P(("groups", "adapter"), ("tensor", "sub"), None),
            P(("groups", "adapter"), None, ("tensor", "sub")),
            P("groups"),
            P("groups"),
            P("groups"),
        ),
        out_specs=(
            P(("groups", "adapter"), ("tensor", "sub")),
            P(("groups", "adapter"), ("tensor", "sub"), None),
            P(("groups", "adapter"), None, ("tensor", "sub")),
        ),
        check_vma=False,
    )
```

```python
import functools

import jax
import jax.numpy as jnp
from jax import lax
from jax.experimental import pallas as pl
from jax.experimental.pallas import tpu as pltpu
from jax.sharding import PartitionSpec as P

TILE = 128
HEAVY = 1 << 36
CHUNKS = (9, 7)
NT = (((1,), (1,)), ((), ()))
SMEM = pl.BlockSpec(memory_space=pltpu.SMEM)
VMEM = pl.BlockSpec(memory_space=pltpu.VMEM)
ANY = pl.BlockSpec(memory_space=pl.ANY)
HBM = pl.BlockSpec(memory_space=pltpu.HBM)


def shift(array, axis, size, by):
    return lax.ppermute(array, axis, [(i, (i + by) % size) for i in range(size)])


def call(body, mib=12, flops=0, **kwargs):
    params = pltpu.CompilerParams(vmem_limit_bytes=mib * 1024 * 1024)
    cost = pl.CostEstimate(flops=flops, bytes_accessed=0, transcendentals=0)
    name = getattr(body, "func", body).__name__
    return pl.pallas_call(body, compiler_params=params, cost_estimate=cost, name=name, **kwargs)


def dot(a, b, dims=(((1,), (0,)), ((), ()))):
    return lax.dot_general(a, b, dims, preferred_element_type=jnp.float32)


def tile_rows(index):
    return pl.ds(pl.multiple_of(index * TILE, TILE), TILE)


def slot_rows(data, tile, entries):
    return jnp.concatenate([data[tile_rows(tile[e]), :] for e in entries], axis=0)


def copy_all(pairs, sems):
    copies = [pltpu.make_async_copy(a, b, sems.at[i]) for i, (a, b) in enumerate(pairs)]
    for copy in copies:
        copy.start()
    return copies


def head_kernel(cot, down, up, *refs):
    *outs, held, pack_held, sems = refs
    count, rank, start = len(outs), down.shape[0], 0
    here = []
    for part in outs[:-1]:
        here.append(held.at[pl.ds(start, part.shape[0]), :])
        start += part.shape[0]
    loads = [(down, pack_held.at[pl.ds(0, rank), :]), (up, pack_held.at[pl.ds(rank, rank), :])]
    start = 0
    for place in here:
        loads.append((cot.at[pl.ds(start, place.shape[0]), :], place))
        start += place.shape[0]
    loads = copy_all(loads, sems.at[0])
    stores = []
    for i, (place, part) in enumerate(zip([pack_held, *here], [outs[-1], *outs[:-1]])):
        for load in loads[:2] if i == 0 else [loads[i + 1]]:
            load.wait()
        stores.append(pltpu.make_async_copy(place, part, sems.at[1, i]))
        stores[-1].start()
    for store in stores:
        store.wait()


def plan_kernel(n, cap, tiles, ids, live_all, stored, me, tile, live, count):
    for k in range(n):
        count[k] = 0
    for e in range(n * cap):
        tile[e] = 0
        live[e] = 0
    for t in range(tiles):
        at = me[0] * tiles + t
        k = lax.rem(me[0] - stored[ids[at]] + n, n)
        e = jnp.minimum(k * cap + count[k], n * cap - 1)
        tile[e] = t
        live[e] = live_all[at]
        count[k] = count[k] + 1


def rank_kernel(slots, cap, tile, live, act, cot, *refs):
    packs, out = refs[: len(slots)], refs[-1]
    width = packs[0].shape[0]
    part = lax.broadcasted_iota(jnp.int32, packs[0].shape, 0) < width // 2
    row = lax.broadcasted_iota(jnp.int32, (TILE, width), 0)
    for i, (slot, pack) in enumerate(zip(slots, packs)):
        entries = range(slot * cap, (slot + 1) * cap)
        maps = pack[...]
        zero = jnp.zeros_like(maps)
        both = dot(slot_rows(act, tile, entries), jnp.where(part, maps, zero), NT)
        both += dot(slot_rows(cot, tile, entries), jnp.where(part, zero, maps), NT)
        for c, e in enumerate(entries):
            at = (i * cap + c) * TILE
            out[at : at + TILE, :] = jnp.where(
                row < live[e], both[c * TILE : (c + 1) * TILE], 0.0
            ).astype(jnp.bfloat16)


def sum_kernel(count, place, *refs):
    total = refs[0][...].astype(jnp.float32)
    for x in refs[1:count]:
        total += x[...].astype(jnp.float32)
    out = refs[place]
    out[...] = total.astype(out.dtype)


def gate_kernel(*refs):
    pass


def terms_kernel(slots, cap, tile, held, act, cot, *refs):
    terms = refs[-len(slots) :]
    rank = held.shape[1] // 2
    for i, slot in enumerate(slots):
        entries = range(slot * cap, (slot + 1) * cap)
        both = held[i * cap * TILE : (i + 1) * cap * TILE, :].astype(jnp.float32)
        both = both.T.astype(jnp.bfloat16)
        terms[i][:rank, :] = dot(both[rank:], slot_rows(act, tile, entries)).astype(jnp.bfloat16)
        terms[i][rank:, :] = dot(both[:rank], slot_rows(cot, tile, entries)).astype(jnp.bfloat16)


def weight_columns(weight, place):
    features = weight.shape[0]
    return weight[:, pl.ds(pl.multiple_of(place * features, 128), features)]


def near_kernel(place, own, pair, weight, *refs):
    out = refs[-1]
    out[...] = dot(own[...], weight_columns(weight, place[0]), NT)
    out[...] += dot(pair[...], weight_columns(weight, place[1]), NT)


def row_sums(start, count, place, near, term, weight, blocks, out, done, sem):
    at = 0
    for first in range(0, len(blocks), count):
        extent = blocks[first].shape[0]
        rows = slice(start + at, start + at + extent)
        total = near[rows, :] + term[rows, :].astype(jnp.float32)
        for i in range(count):
            total += dot(blocks[first + i][...], weight_columns(weight, place[2 + i]), NT)
        done[at : at + extent, :] = total.astype(jnp.bfloat16)
        at += extent
    copy = pltpu.make_async_copy(done, out.at[pl.ds(start, at), :], sem)
    copy.start()
    copy.wait()


def middle_kernel(groups, cap, count, tile, place, *refs):
    n = sum(len(g) for g in groups)
    block, refs = refs[:count], refs[count:]
    sums, refs = refs[: len(groups)], refs[len(groups) :]
    packs, (near, weight), refs = refs[:n], refs[n : n + 2], refs[n + 2 :]
    out, term, done, sem = refs[-4:]
    term[...] = jnp.zeros_like(term)
    for g, slots in enumerate(groups):
        for i, slot in enumerate(slots):
            maps = packs[slot][...]
            rank = maps.shape[0] // 2
            maps = jnp.concatenate([jnp.zeros_like(maps[:rank]), maps[:rank]], axis=0)
            found = dot(sums[g][i * cap * TILE : (i + 1) * cap * TILE, :], maps)
            for c in range(cap):
                rows = tile_rows(tile[slot * cap + c])
                before = term[rows, :].astype(jnp.float32)
                term[rows, :] = (before + found[c * TILE : (c + 1) * TILE]).astype(term.dtype)
    row_sums(0, count, place, near, term, weight, block, out, done, sem)


def far_kernel(count, start, place, near, term, weight, *refs):
    out, done, sem = refs[-3:]
    row_sums(start, count, place, near, term, weight, refs[:count], out, done, sem)


def final_kernel(count, scale, *refs):
    down, up, token = refs[-3:]
    token[...] = jnp.zeros_like(token)
    rank = down.shape[0]
    for out, rows in ((down, slice(0, rank)), (up, slice(rank, 2 * rank))):
        total = refs[0][rows, :].astype(jnp.float32)
        for x in refs[1:count]:
            total += x[rows, :].astype(jnp.float32)
        out[...] = (total * scale).astype(out.dtype)


def on_device(
    activations,
    cotangent,
    frozen_weight,
    adapter_down_maps,
    adapter_up_maps,
    adapter_per_tile,
    live_per_tile,
    adapter_stored_row,
):
    rows, features = activations.shape
    tiles = rows // TILE
    stored, _, rank = adapter_down_maps.shape
    n = lax.axis_size("adapter")
    tensors = lax.axis_size("tensor")
    subs = lax.axis_size("sub")
    me = lax.axis_index("adapter")
    t_me, s_me = lax.axis_index("tensor"), lax.axis_index("sub")
    extents = [rows * c // sum(CHUNKS) for c in CHUNKS]
    starts = [sum(extents[:c]) for c in range(len(extents))]
    bf16, f32 = jnp.bfloat16, jnp.float32

    cap = -(-tiles // n)
    places = [t_me * subs + s_me, t_me * subs + (1 - s_me)]
    for s in (s_me, 1 - s_me):
        places += [jnp.remainder(t_me - k, tensors) * subs + s for k in range(1, tensors)]
    place = jnp.stack(places).astype(jnp.int32)

    groups = [[k for k in range(n) if min(k, n - k) <= n // 4]]
    groups.append([k for k in range(n) if k not in groups[0]])

    down = jnp.swapaxes(adapter_down_maps, 1, 2).reshape(stored * rank, features)
    up = adapter_up_maps.reshape(stored * rank, features)
    *parts, pack = call(
        head_kernel,
        mib=56,
        in_specs=[ANY] * 3,
        out_specs=[ANY] * (len(extents) + 1),
        out_shape=[jax.ShapeDtypeStruct((e, features), bf16) for e in extents]
        + [jax.ShapeDtypeStruct((2 * rank, features), bf16)],
        scratch_shapes=[
            pltpu.VMEM((rows, features), bf16),
            pltpu.VMEM((2 * rank, features), bf16),
            pltpu.SemaphoreType.DMA((2, len(extents) + 2)),
        ],
    )(cotangent, down, up)
    def across(part, aside=0):
        slice_axes, found = ("tensor", "sub"), []
        for k in range(1, tensors):
            to = [(t + k) % tensors * subs + (s + aside) % subs for t in range(tensors) for s in range(subs)]
            found.append(lax.ppermute(part, slice_axes, list(enumerate(to))))
        return found

    def forward(blocks):
        return [shift(x, "sub", subs, 1) for x in blocks]

    direct = [across(parts[0])]
    pair = shift(cotangent, "sub", subs, 1)
    packs = {0: pack}
    for g in groups:
        for k in g:
            if k:
                packs[k] = shift(pack, "adapter", n, k)


    table = jax.ShapeDtypeStruct((n * cap,), jnp.int32)
    tile, live = call(
        functools.partial(plan_kernel, n, cap, tiles),
        flops=HEAVY,
        in_specs=[SMEM] * 4,
        out_specs=[SMEM] * 2,
        out_shape=[table] * 2,
        scratch_shapes=[pltpu.SMEM((n,), jnp.int32)],
    )(adapter_per_tile, live_per_tile, adapter_stored_row, me.astype(jnp.int32).reshape(1))

    def after(arrays):
        return [ANY] * len(arrays)

    def gate(blocks, ready):
        found = call(
            gate_kernel,
            in_specs=after(blocks) + [ANY],
            out_specs=after(blocks),
            out_shape=[jax.ShapeDtypeStruct(x.shape, x.dtype) for x in blocks],
            input_output_aliases={i: i for i in range(len(blocks))},
        )(*blocks, ready)
        return list(found)

    def ranks(g, *wait):
        return call(
            functools.partial(rank_kernel, g, cap),
            in_specs=[SMEM] * 2 + [VMEM] * (2 + len(g)) + after(wait),
            out_specs=VMEM,
            out_shape=jax.ShapeDtypeStruct((len(g) * cap * TILE, 2 * rank), bf16),
        )(tile, live, activations, cotangent, *[packs[k] for k in g], *wait)

    def chip_sum(own, *wait):
        given = shift(own, "sub", subs, 1)
        sent = call(
            functools.partial(sum_kernel, 2, -1),
            in_specs=[VMEM] * 2 + after(wait),
            out_specs=VMEM,
            out_shape=jax.ShapeDtypeStruct(own.shape, bf16),
        )(own, given, *wait)
        return given, sent

    def slice_sum(own, given, others, held_parts, *wait):
        found = [own, given, *others]
        shapes = [jax.ShapeDtypeStruct(x.shape, x.dtype) for x in held_parts]
        return call(
            functools.partial(sum_kernel, len(found), -1 - len(shapes)),
            in_specs=[VMEM] * len(found) + after(held_parts) + after(wait),
            out_specs=[VMEM] + after(held_parts),
            out_shape=[jax.ShapeDtypeStruct(own.shape, bf16)] + shapes,
            input_output_aliases={len(found) + i: 1 + i for i in range(len(shapes))},
        )(*found, *held_parts, *wait)

    def adapter_terms(g, held, *wait):
        found = call(
            functools.partial(terms_kernel, g, cap),
            in_specs=[SMEM] + [VMEM] * 3 + after(wait),
            out_specs=[VMEM] * len(g),
            out_shape=[jax.ShapeDtypeStruct((2 * rank, features), bf16)] * len(g),
        )(tile, held, activations, cotangent, *wait)
        return dict(zip(g, found))

    near = call(
        near_kernel,
        flops=HEAVY,
        in_specs=[SMEM] + [VMEM] * 3,
        out_specs=VMEM,
        out_shape=jax.ShapeDtypeStruct((rows, features), f32),
    )(place, cotangent, pair, frozen_weight)

    first, second = groups
    own = ranks(first, near)
    more = ranks(second, own)
    given, sent = chip_sum(own, *direct[0], more)
    given_more, sent_more = chip_sum(more, sent)
    others, others_more = across(sent), across(sent_more)
    (held,) = slice_sum(own, given, others, [], *others_more)
    held_more, part = slice_sum(more, given_more, others_more, parts[1:], held)
    sums = [held, held_more]
    direct.append(across(part))
    terms = adapter_terms(first, held, held_more)
    terms |= adapter_terms(second, held_more)
    direct[0] = gate(direct[0], held)
    forwards = [forward(direct[0])]
    arrived = {k: shift(terms[k], "adapter", n, -k) for g in groups for k in g if k}

    block = direct[0] + forwards[0]
    count = len(block)
    operands = [tile, place, *block, *sums, *[packs[k] for k in range(n)], near, frozen_weight]
    whole_shape = jax.ShapeDtypeStruct((rows, features), bf16)
    out, term = call(
        functools.partial(middle_kernel, groups, cap, count),
        mib=20,
        flops=HEAVY,
        in_specs=[SMEM] * 2 + [VMEM] * (len(operands) - 2) + [ANY],
        out_specs=[HBM, VMEM],
        out_shape=[whole_shape] * 2,
        scratch_shapes=[pltpu.VMEM((starts[1], features), bf16), pltpu.SemaphoreType.DMA],
    )(*operands, terms[second[-1]])

    direct[1] = gate(direct[1], term)
    forwards.append(forward(direct[1]))
    maps_shape = jax.ShapeDtypeStruct((rank, features), bf16)
    token_shape = jax.ShapeDtypeStruct((8, 128), f32)
    down_grad, up_grad, token = call(
        functools.partial(final_kernel, n, (stored / rows) ** 0.5),
        flops=HEAVY,
        in_specs=[VMEM] * n,
        out_specs=[VMEM] * 3,
        out_shape=[maps_shape] * 2 + [token_shape],
    )(terms[0], *[arrived[k] for k in range(1, n)])
    operands = [place, near, term, frozen_weight, *direct[1], *forwards[1]]
    out = call(
        functools.partial(far_kernel, count, starts[1]),
        mib=16,
        in_specs=[SMEM] + [VMEM] * (len(operands) - 1) + [HBM, VMEM],
        out_specs=HBM,
        out_shape=whole_shape,
        scratch_shapes=[pltpu.VMEM((rows - starts[1], features), bf16), pltpu.SemaphoreType.DMA],
        input_output_aliases={len(operands): 0},
    )(*operands, out, token)
    down_grad = jnp.swapaxes(down_grad.reshape(stored, rank, features), 1, 2)
    up_grad = up_grad.reshape(stored, rank, features)
    return (out, down_grad, up_grad)


def solution(mesh):
    return jax.shard_map(
        on_device,
        mesh=mesh,
        in_specs=(
            P(("groups", "adapter"), ("tensor", "sub")),
            P(("groups", "adapter"), ("tensor", "sub")),
            P(("tensor", "sub"), None),
            P(("groups", "adapter"), ("tensor", "sub"), None),
            P(("groups", "adapter"), None, ("tensor", "sub")),
            P("groups"),
            P("groups"),
            P("groups"),
        ),
        out_specs=(
            P(("groups", "adapter"), ("tensor", "sub")),
            P(("groups", "adapter"), ("tensor", "sub"), None),
            P(("groups", "adapter"), None, ("tensor", "sub")),
        ),
        check_vma=False,
    )
```

```python
import functools

import jax
import jax.numpy as jnp
from jax import lax
from jax.experimental import pallas as pl
from jax.experimental.pallas import tpu as pltpu
from jax.sharding import PartitionSpec as P

TILE = 128
HEAVY = 1 << 36
CHUNKS = (3, 4, 4, 5)
FIRST = 2
NT = (((1,), (1,)), ((), ()))
SMEM = pl.BlockSpec(memory_space=pltpu.SMEM)
VMEM = pl.BlockSpec(memory_space=pltpu.VMEM)
ANY = pl.BlockSpec(memory_space=pl.ANY)
HBM = pl.BlockSpec(memory_space=pltpu.HBM)


def shift(array, axis, size, by):
    return lax.ppermute(array, axis, [(i, (i + by) % size) for i in range(size)])


def call(body, mib=12, flops=0, **kwargs):
    params = pltpu.CompilerParams(vmem_limit_bytes=mib * 1024 * 1024)
    cost = pl.CostEstimate(flops=flops, bytes_accessed=0, transcendentals=0)
    name = getattr(body, "func", body).__name__
    return pl.pallas_call(body, compiler_params=params, cost_estimate=cost, name=name, **kwargs)


def dot(a, b, dims=(((1,), (0,)), ((), ()))):
    return lax.dot_general(a, b, dims, preferred_element_type=jnp.float32)


def tile_rows(index):
    return pl.ds(pl.multiple_of(index * TILE, TILE), TILE)


def slot_rows(data, tile, entries):
    return jnp.concatenate([data[tile_rows(tile[e]), :] for e in entries], axis=0)


def copy_all(pairs, sems):
    copies = [pltpu.make_async_copy(a, b, sems.at[i]) for i, (a, b) in enumerate(pairs)]
    for copy in copies:
        copy.start()
    return copies


def cut_kernel(cot, *refs):
    *parts, held, sems = refs
    rows, start = [], 0
    for part in parts:
        rows.append(pl.ds(start, part.shape[0]))
        start += part.shape[0]
    loads = copy_all([(cot.at[r, :], held.at[r, :]) for r in rows], sems.at[0])
    stores = []
    for i, load in enumerate(loads):
        load.wait()
        stores.append(pltpu.make_async_copy(held.at[rows[i], :], parts[i], sems.at[1, i]))
        stores[-1].start()
    for store in stores:
        store.wait()


def pack_kernel(down, up, *refs):
    out, again, held, sems = refs[-4:]
    rank = down.shape[0]
    places = [held.at[pl.ds(0, rank), :], held.at[pl.ds(rank, rank), :]]
    for load in copy_all(list(zip((down, up), places)), sems):
        load.wait()
    for copy in copy_all([(held, out), (held, again)], sems):
        copy.wait()


def plan_kernel(n, cap, tiles, ids, live_all, stored, me, tile, live, count):
    for k in range(n):
        count[k] = 0
    for e in range(n * cap):
        tile[e] = 0
        live[e] = 0
    for t in range(tiles):
        at = me[0] * tiles + t
        k = lax.rem(me[0] - stored[ids[at]] + n, n)
        e = jnp.minimum(k * cap + count[k], n * cap - 1)
        tile[e] = t
        live[e] = live_all[at]
        count[k] = count[k] + 1


def rank_kernel(slots, cap, tile, live, act, cot, *refs):
    packs, out = refs[: len(slots)], refs[-1]
    width = packs[0].shape[0]
    part = lax.broadcasted_iota(jnp.int32, packs[0].shape, 0) < width // 2
    row = lax.broadcasted_iota(jnp.int32, (TILE, width), 0)
    for i, (slot, pack) in enumerate(zip(slots, packs)):
        entries = range(slot * cap, (slot + 1) * cap)
        maps = pack[...]
        zero = jnp.zeros_like(maps)
        both = dot(slot_rows(act, tile, entries), jnp.where(part, maps, zero), NT)
        both += dot(slot_rows(cot, tile, entries), jnp.where(part, zero, maps), NT)
        for c, e in enumerate(entries):
            at = (i * cap + c) * TILE
            out[at : at + TILE, :] = jnp.where(
                row < live[e], both[c * TILE : (c + 1) * TILE], 0.0
            ).astype(jnp.bfloat16)


def sum_kernel(count, place, *refs):
    total = refs[0][...].astype(jnp.float32)
    for x in refs[1:count]:
        total += x[...].astype(jnp.float32)
    out = refs[place]
    out[...] = total.astype(out.dtype)


def gate_kernel(*refs):
    pass


def tick_kernel(*refs):
    refs[-1][...] = jnp.zeros_like(refs[-1])


def terms_kernel(slots, cap, tile, held, act, cot, *refs):
    terms = refs[-len(slots) :]
    rank = held.shape[1] // 2
    for i, slot in enumerate(slots):
        entries = range(slot * cap, (slot + 1) * cap)
        both = held[i * cap * TILE : (i + 1) * cap * TILE, :].astype(jnp.float32)
        both = both.T.astype(jnp.bfloat16)
        terms[i][:rank, :] = dot(both[rank:], slot_rows(act, tile, entries)).astype(jnp.bfloat16)
        terms[i][rank:, :] = dot(both[:rank], slot_rows(cot, tile, entries)).astype(jnp.bfloat16)


def weight_columns(weight, place):
    features = weight.shape[0]
    return weight[:, pl.ds(pl.multiple_of(place * features, 128), features)]


def near_kernel(count, place, own, pair, weight, *refs):
    out, *parts = refs[-count:]
    start = own.shape[0] - sum(part.shape[0] for part in parts)
    for part in parts:
        part[...] = own[start : start + part.shape[0], :]
        start += part.shape[0]
    out[...] = dot(own[...], weight_columns(weight, place[0]), NT)
    out[...] += dot(pair[...], weight_columns(weight, place[1]), NT)


def row_sums(start, count, place, near, term, weight, blocks, out, done, sem):
    at = 0
    for first in range(0, len(blocks), count):
        extent = blocks[first].shape[0]
        rows = slice(start + at, start + at + extent)
        total = near[rows, :] + term[rows, :].astype(jnp.float32)
        for i in range(count):
            total += dot(blocks[first + i][...], weight_columns(weight, place[2 + i]), NT)
        done[at : at + extent, :] = total.astype(jnp.bfloat16)
        at += extent
    copy = pltpu.make_async_copy(done, out.at[pl.ds(start, at), :], sem)
    copy.start()
    copy.wait()


def middle_kernel(groups, cap, count, tile, place, *refs):
    n = sum(len(g) for g in groups)
    blocks, refs = refs[: 3 * count], refs[3 * count :]
    sums, refs = refs[: len(groups)], refs[len(groups) :]
    packs, (near, weight), refs = refs[:n], refs[n : n + 2], refs[n + 2 :]
    out, term, done, sem = refs[-4:]
    term[...] = jnp.zeros_like(term)
    for g, slots in enumerate(groups):
        for i, slot in enumerate(slots):
            maps = packs[slot][...]
            rank = maps.shape[0] // 2
            maps = jnp.concatenate([jnp.zeros_like(maps[:rank]), maps[:rank]], axis=0)
            found = dot(sums[g][i * cap * TILE : (i + 1) * cap * TILE, :], maps)
            for c in range(cap):
                rows = tile_rows(tile[slot * cap + c])
                before = term[rows, :].astype(jnp.float32)
                term[rows, :] = (before + found[c * TILE : (c + 1) * TILE]).astype(term.dtype)
    row_sums(0, count, place, near, term, weight, blocks, out, done, sem)


def far_kernel(count, start, place, near, term, weight, *refs):
    out, token, done, sem = refs[-4:]
    token[...] = jnp.zeros_like(token)
    row_sums(start, count, place, near, term, weight, refs[:count], out, done, sem)


def final_kernel(count, scale, *refs):
    down, up = refs[-2:]
    rank = down.shape[0]
    for out, rows in ((down, slice(0, rank)), (up, slice(rank, 2 * rank))):
        total = refs[0][rows, :].astype(jnp.float32)
        for x in refs[1:count]:
            total += x[rows, :].astype(jnp.float32)
        out[...] = (total * scale).astype(out.dtype)


def on_device(
    activations,
    cotangent,
    frozen_weight,
    adapter_down_maps,
    adapter_up_maps,
    adapter_per_tile,
    live_per_tile,
    adapter_stored_row,
):
    rows, features = activations.shape
    tiles = rows // TILE
    stored, _, rank = adapter_down_maps.shape
    n = lax.axis_size("adapter")
    tensors = lax.axis_size("tensor")
    subs = lax.axis_size("sub")
    me = lax.axis_index("adapter")
    t_me, s_me = lax.axis_index("tensor"), lax.axis_index("sub")
    extents = [rows * c // sum(CHUNKS) for c in CHUNKS]
    starts = [sum(extents[:c]) for c in range(len(extents))]
    bf16, f32 = jnp.bfloat16, jnp.float32

    cap = -(-tiles // n)
    places = [t_me * subs + s_me, t_me * subs + (1 - s_me)]
    for s in (s_me, 1 - s_me):
        places += [jnp.remainder(t_me - k, tensors) * subs + s for k in range(1, tensors)]
    place = jnp.stack(places).astype(jnp.int32)

    groups = [[k for k in range(n) if 1 <= min(k, n - k) <= n // 4]]
    groups.append([k for k in range(n) if k not in groups[0]])

    down = jnp.swapaxes(adapter_down_maps, 1, 2).reshape(stored * rank, features)
    up = adapter_up_maps.reshape(stored * rank, features)
    parts = call(
        cut_kernel,
        mib=56,
        in_specs=[ANY],
        out_specs=[ANY] * FIRST,
        out_shape=[jax.ShapeDtypeStruct((e, features), bf16) for e in extents[:FIRST]],
        scratch_shapes=[
            pltpu.VMEM((starts[FIRST], features), bf16),
            pltpu.SemaphoreType.DMA((2, FIRST)),
        ],
    )(cotangent)
    pack, pack_again = call(
        pack_kernel,
        mib=56,
        in_specs=[ANY] * 3,
        out_specs=[ANY] * 2,
        out_shape=[jax.ShapeDtypeStruct((2 * rank, features), bf16)] * 2,
        scratch_shapes=[pltpu.VMEM((2 * rank, features), bf16), pltpu.SemaphoreType.DMA((2,))],
    )(down, up, parts[0])
    def across(part, aside=0):
        slice_axes, found = ("tensor", "sub"), []
        for k in range(1, tensors):
            to = [(t + k) % tensors * subs + (s + aside) % subs for t in range(tensors) for s in range(subs)]
            found.append(lax.ppermute(part, slice_axes, list(enumerate(to))))
        return found

    def forward(blocks):
        return [shift(x, "sub", subs, 1) for x in blocks]

    direct = [across(part) for part in parts]
    pair = shift(cotangent, "sub", subs, 1)
    table = jax.ShapeDtypeStruct((n * cap,), jnp.int32)
    tile, live = call(
        functools.partial(plan_kernel, n, cap, tiles),
        in_specs=[SMEM] * 4,
        out_specs=[SMEM] * 2,
        out_shape=[table] * 2,
        scratch_shapes=[pltpu.SMEM((n,), jnp.int32)],
    )(adapter_per_tile, live_per_tile, adapter_stored_row, me.astype(jnp.int32).reshape(1))

    def after(arrays):
        return [ANY] * len(arrays)

    def gate(blocks, ready):
        found = call(
            gate_kernel,
            in_specs=after(blocks) + [ANY],
            out_specs=after(blocks),
            out_shape=[jax.ShapeDtypeStruct(x.shape, x.dtype) for x in blocks],
            input_output_aliases={i: i for i in range(len(blocks))},
        )(*blocks, ready)
        return list(found)

    def tick(*ready):
        return call(
            tick_kernel,
            flops=HEAVY,
            in_specs=after(ready),
            out_specs=VMEM,
            out_shape=jax.ShapeDtypeStruct((8, 128), f32),
        )(*ready)

    def ranks(g, *wait):
        return call(
            functools.partial(rank_kernel, g, cap),
            in_specs=[SMEM] * 2 + [VMEM] * (2 + len(g)) + after(wait),
            out_specs=VMEM,
            out_shape=jax.ShapeDtypeStruct((len(g) * cap * TILE, 2 * rank), bf16),
        )(tile, live, activations, cotangent, *[packs[k] for k in g], *wait)

    def chip_sum(own, *wait):
        given = shift(own, "sub", subs, 1)
        sent = call(
            functools.partial(sum_kernel, 2, -1),
            in_specs=[VMEM] * 2 + after(wait),
            out_specs=VMEM,
            out_shape=jax.ShapeDtypeStruct(own.shape, bf16),
        )(own, given, *wait)
        return given, sent

    def slice_sum(own, given, others, held_parts, *wait):
        found = [own, given, *others]
        shapes = [jax.ShapeDtypeStruct(x.shape, x.dtype) for x in held_parts]
        return call(
            functools.partial(sum_kernel, len(found), -1 - len(shapes)),
            in_specs=[VMEM] * len(found) + after(held_parts) + after(wait),
            out_specs=[VMEM] + after(held_parts),
            out_shape=[jax.ShapeDtypeStruct(own.shape, bf16)] + shapes,
            input_output_aliases={len(found) + i: 1 + i for i in range(len(shapes))},
        )(*found, *held_parts, *wait)

    def adapter_terms(g, held, *wait):
        found = call(
            functools.partial(terms_kernel, g, cap),
            in_specs=[SMEM] + [VMEM] * 3 + after(wait),
            out_specs=[VMEM] * len(g),
            out_shape=[jax.ShapeDtypeStruct((2 * rank, features), bf16)] * len(g),
        )(tile, held, activations, cotangent, *wait)
        return dict(zip(g, found))

    near, *rest = call(
        functools.partial(near_kernel, 1 + len(extents) - FIRST),
        flops=HEAVY,
        in_specs=[SMEM] + [VMEM] * 3 + after(direct[0]),
        out_specs=[VMEM] * (1 + len(extents) - FIRST),
        out_shape=[jax.ShapeDtypeStruct((rows, features), f32)]
        + [jax.ShapeDtypeStruct((e, features), bf16) for e in extents[FIRST:]],
    )(place, cotangent, pair, frozen_weight, *direct[0])
    parts = [*parts, *rest]

    first, second = groups
    packs = {0: pack} | {k: shift(pack, "adapter", n, k) for k in first}
    (pack_again,) = gate([pack_again], tile)
    packs |= {k: shift(pack_again, "adapter", n, k) for k in second if k}
    forwards = [forward(direct[0])]

    own = ranks(first, near, *forwards[0])
    given, sent = chip_sum(own, tick(own))
    direct[1] = gate(direct[1], sent)
    forwards.append(forward(direct[1]))
    held, part = slice_sum(own, given, across(sent), parts[2:3], tick(sent), *forwards[1])
    direct.append(across(part))
    sums = [held]
    terms = adapter_terms(first, held)
    arrived = {k: shift(terms[k], "adapter", n, -k) for k in first}

    own = ranks(second, terms[first[0]])
    given, sent = chip_sum(own, tick(own))
    held, part = slice_sum(own, given, across(sent), parts[3:4], tick(sent))
    direct.append(across(part))
    direct[2] = gate(direct[2], held)
    forwards.append(forward(direct[2]))
    sums.append(held)
    terms |= adapter_terms(second, held)
    arrived |= {k: shift(terms[k], "adapter", n, -k) for k in second if k}

    blocks = [x for c in range(3) for x in direct[c] + forwards[c]]
    count = len(blocks) // 3
    operands = [tile, place, *blocks, *sums, *[packs[k] for k in range(n)], near, frozen_weight]
    whole_shape = jax.ShapeDtypeStruct((rows, features), bf16)
    out, term = call(
        functools.partial(middle_kernel, groups, cap, count),
        mib=20,
        flops=HEAVY,
        in_specs=[SMEM] * 2 + [VMEM] * (len(operands) - 2) + [ANY] * 2,
        out_specs=[HBM, VMEM],
        out_shape=[whole_shape] * 2,
        scratch_shapes=[pltpu.VMEM((starts[3], features), bf16), pltpu.SemaphoreType.DMA],
    )(*operands, terms[second[-1]], tick(held))
    direct[3] = gate(direct[3], term)
    forwards.append(forward(direct[3]))
    token_shape = jax.ShapeDtypeStruct((8, 128), f32)
    operands = [place, near, term, frozen_weight, *direct[3], *forwards[3]]
    out, token = call(
        functools.partial(far_kernel, count, starts[3]),
        mib=16,
        in_specs=[SMEM] + [VMEM] * (len(operands) - 1) + [HBM, ANY],
        out_specs=[HBM, VMEM],
        out_shape=[whole_shape, token_shape],
        scratch_shapes=[pltpu.VMEM((rows - starts[3], features), bf16), pltpu.SemaphoreType.DMA],
        input_output_aliases={len(operands): 0},
    )(*operands, out, tick(term))
    maps_shape = jax.ShapeDtypeStruct((rank, features), bf16)
    down_grad, up_grad = call(
        functools.partial(final_kernel, n, (stored / rows) ** 0.5),
        in_specs=[VMEM] * n + [ANY],
        out_specs=[VMEM] * 2,
        out_shape=[maps_shape] * 2,
    )(terms[0], *[arrived[k] for k in range(1, n)], token)
    down_grad = jnp.swapaxes(down_grad.reshape(stored, rank, features), 1, 2)
    up_grad = up_grad.reshape(stored, rank, features)
    return (out, down_grad, up_grad)


def solution(mesh):
    return jax.shard_map(
        on_device,
        mesh=mesh,
        in_specs=(
            P(("groups", "adapter"), ("tensor", "sub")),
            P(("groups", "adapter"), ("tensor", "sub")),
            P(("tensor", "sub"), None),
            P(("groups", "adapter"), ("tensor", "sub"), None),
            P(("groups", "adapter"), None, ("tensor", "sub")),
            P("groups"),
            P("groups"),
            P("groups"),
        ),
        out_specs=(
            P(("groups", "adapter"), ("tensor", "sub")),
            P(("groups", "adapter"), ("tensor", "sub"), None),
            P(("groups", "adapter"), None, ("tensor", "sub")),
        ),
        check_vma=False,
    )
```

```python
import functools

import jax
import jax.numpy as jnp
from jax import lax
from jax.experimental import pallas as pl
from jax.experimental.pallas import tpu as pltpu
from jax.sharding import PartitionSpec as P

TILE = 128
HEAVY = 1 << 36
CHUNKS = (3, 5, 4, 4)
FIRST = 2
NT = (((1,), (1,)), ((), ()))
SMEM = pl.BlockSpec(memory_space=pltpu.SMEM)
VMEM = pl.BlockSpec(memory_space=pltpu.VMEM)
ANY = pl.BlockSpec(memory_space=pl.ANY)
HBM = pl.BlockSpec(memory_space=pltpu.HBM)


def shift(array, axis, size, by):
    return lax.ppermute(array, axis, [(i, (i + by) % size) for i in range(size)])


def call(body, mib=12, flops=0, **kwargs):
    params = pltpu.CompilerParams(vmem_limit_bytes=mib * 1024 * 1024)
    cost = pl.CostEstimate(flops=flops, bytes_accessed=0, transcendentals=0)
    name = getattr(body, "func", body).__name__
    return pl.pallas_call(body, compiler_params=params, cost_estimate=cost, name=name, **kwargs)


def dot(a, b, dims=(((1,), (0,)), ((), ()))):
    return lax.dot_general(a, b, dims, preferred_element_type=jnp.float32)


def tile_rows(index):
    return pl.ds(pl.multiple_of(index * TILE, TILE), TILE)


def slot_rows(data, tile, entries):
    return jnp.concatenate([data[tile_rows(tile[e]), :] for e in entries], axis=0)


def copy_all(pairs, sems):
    copies = [pltpu.make_async_copy(a, b, sems.at[i]) for i, (a, b) in enumerate(pairs)]
    for copy in copies:
        copy.start()
    return copies


def cut_kernel(cot, *refs):
    *parts, held, sems = refs
    rows, start = [], 0
    for part in parts:
        rows.append(pl.ds(start, part.shape[0]))
        start += part.shape[0]
    loads = copy_all([(cot.at[r, :], held.at[r, :]) for r in rows], sems.at[0])
    stores = []
    for i, load in enumerate(loads):
        load.wait()
        stores.append(pltpu.make_async_copy(held.at[rows[i], :], parts[i], sems.at[1, i]))
        stores[-1].start()
    for store in stores:
        store.wait()


def pack_kernel(down, up, *refs):
    out, again, held, sems = refs[-4:]
    rank = down.shape[0]
    places = [held.at[pl.ds(0, rank), :], held.at[pl.ds(rank, rank), :]]
    for load in copy_all(list(zip((down, up), places)), sems):
        load.wait()
    for copy in copy_all([(held, out), (held, again)], sems):
        copy.wait()


def plan_kernel(n, cap, tiles, ids, live_all, stored, me, tile, live, count):
    for k in range(n):
        count[k] = 0
    for e in range(n * cap):
        tile[e] = 0
        live[e] = 0
    for t in range(tiles):
        at = me[0] * tiles + t
        k = lax.rem(me[0] - stored[ids[at]] + n, n)
        e = jnp.minimum(k * cap + count[k], n * cap - 1)
        tile[e] = t
        live[e] = live_all[at]
        count[k] = count[k] + 1


def rank_kernel(slots, cap, tile, live, act, cot, *refs):
    packs, out = refs[: len(slots)], refs[-1]
    width = packs[0].shape[0]
    part = lax.broadcasted_iota(jnp.int32, packs[0].shape, 0) < width // 2
    row = lax.broadcasted_iota(jnp.int32, (TILE, width), 0)
    for i, (slot, pack) in enumerate(zip(slots, packs)):
        entries = range(slot * cap, (slot + 1) * cap)
        maps = pack[...]
        zero = jnp.zeros_like(maps)
        both = dot(slot_rows(act, tile, entries), jnp.where(part, maps, zero), NT)
        both += dot(slot_rows(cot, tile, entries), jnp.where(part, zero, maps), NT)
        for c, e in enumerate(entries):
            at = (i * cap + c) * TILE
            out[at : at + TILE, :] = jnp.where(
                row < live[e], both[c * TILE : (c + 1) * TILE], 0.0
            ).astype(jnp.bfloat16)


def sum_kernel(count, place, *refs):
    total = refs[0][...].astype(jnp.float32)
    for x in refs[1:count]:
        total += x[...].astype(jnp.float32)
    out = refs[place]
    out[...] = total.astype(out.dtype)


def gate_kernel(*refs):
    pass


def tick_kernel(*refs):
    refs[-1][...] = jnp.zeros_like(refs[-1])


def terms_kernel(slots, cap, tile, held, act, cot, *refs):
    terms = refs[-len(slots) :]
    rank = held.shape[1] // 2
    for i, slot in enumerate(slots):
        entries = range(slot * cap, (slot + 1) * cap)
        both = held[i * cap * TILE : (i + 1) * cap * TILE, :].astype(jnp.float32)
        both = both.T.astype(jnp.bfloat16)
        terms[i][:rank, :] = dot(both[rank:], slot_rows(act, tile, entries)).astype(jnp.bfloat16)
        terms[i][rank:, :] = dot(both[:rank], slot_rows(cot, tile, entries)).astype(jnp.bfloat16)


def weight_columns(weight, place):
    features = weight.shape[0]
    return weight[:, pl.ds(pl.multiple_of(place * features, 128), features)]


def rest_kernel(count, own, *refs):
    parts = refs[-count:]
    start = own.shape[0] - sum(part.shape[0] for part in parts)
    for part in parts:
        part[...] = own[start : start + part.shape[0], :]
        start += part.shape[0]


def near_kernel(place, own, pair, weight, *refs):
    out = refs[-1]
    out[...] = dot(own[...], weight_columns(weight, place[0]), NT)
    out[...] += dot(pair[...], weight_columns(weight, place[1]), NT)


def row_sums(start, count, place, near, term, weight, blocks, out, done, sem):
    at = 0
    for first in range(0, len(blocks), count):
        extent = blocks[first].shape[0]
        rows = slice(start + at, start + at + extent)
        total = near[rows, :] + term[rows, :].astype(jnp.float32)
        for i in range(count):
            total += dot(blocks[first + i][...], weight_columns(weight, place[2 + i]), NT)
        done[at : at + extent, :] = total.astype(jnp.bfloat16)
        at += extent
    copy = pltpu.make_async_copy(done, out.at[pl.ds(start, at), :], sem)
    copy.start()
    copy.wait()


def middle_kernel(groups, cap, count, tile, place, *refs):
    n = sum(len(g) for g in groups)
    blocks, refs = refs[: 3 * count], refs[3 * count :]
    sums, refs = refs[: len(groups)], refs[len(groups) :]
    packs, (near, weight), refs = refs[:n], refs[n : n + 2], refs[n + 2 :]
    out, term, done, sem = refs[-4:]
    term[...] = jnp.zeros_like(term)
    for g, slots in enumerate(groups):
        for i, slot in enumerate(slots):
            maps = packs[slot][...]
            rank = maps.shape[0] // 2
            maps = jnp.concatenate([jnp.zeros_like(maps[:rank]), maps[:rank]], axis=0)
            found = dot(sums[g][i * cap * TILE : (i + 1) * cap * TILE, :], maps)
            for c in range(cap):
                rows = tile_rows(tile[slot * cap + c])
                before = term[rows, :].astype(jnp.float32)
                term[rows, :] = (before + found[c * TILE : (c + 1) * TILE]).astype(term.dtype)
    row_sums(0, count, place, near, term, weight, blocks, out, done, sem)


def far_kernel(count, start, place, near, term, weight, *refs):
    out, token, done, sem = refs[-4:]
    token[...] = jnp.zeros_like(token)
    row_sums(start, count, place, near, term, weight, refs[:count], out, done, sem)


def final_kernel(count, scale, *refs):
    down, up = refs[-2:]
    rank = down.shape[0]
    for out, rows in ((down, slice(0, rank)), (up, slice(rank, 2 * rank))):
        total = refs[0][rows, :].astype(jnp.float32)
        for x in refs[1:count]:
            total += x[rows, :].astype(jnp.float32)
        out[...] = (total * scale).astype(out.dtype)


def on_device(
    activations,
    cotangent,
    frozen_weight,
    adapter_down_maps,
    adapter_up_maps,
    adapter_per_tile,
    live_per_tile,
    adapter_stored_row,
):
    rows, features = activations.shape
    tiles = rows // TILE
    stored, _, rank = adapter_down_maps.shape
    n = lax.axis_size("adapter")
    tensors = lax.axis_size("tensor")
    subs = lax.axis_size("sub")
    me = lax.axis_index("adapter")
    t_me, s_me = lax.axis_index("tensor"), lax.axis_index("sub")
    extents = [rows * c // sum(CHUNKS) for c in CHUNKS]
    starts = [sum(extents[:c]) for c in range(len(extents))]
    bf16, f32 = jnp.bfloat16, jnp.float32

    cap = -(-tiles // n)
    places = [t_me * subs + s_me, t_me * subs + (1 - s_me)]
    for s in (s_me, 1 - s_me):
        places += [jnp.remainder(t_me - k, tensors) * subs + s for k in range(1, tensors)]
    place = jnp.stack(places).astype(jnp.int32)

    groups = [[k for k in range(n) if 1 <= min(k, n - k) <= n // 4]]
    groups.append([k for k in range(n) if k not in groups[0]])

    down = jnp.swapaxes(adapter_down_maps, 1, 2).reshape(stored * rank, features)
    up = adapter_up_maps.reshape(stored * rank, features)
    parts = call(
        cut_kernel,
        mib=56,
        in_specs=[ANY],
        out_specs=[ANY] * FIRST,
        out_shape=[jax.ShapeDtypeStruct((e, features), bf16) for e in extents[:FIRST]],
        scratch_shapes=[
            pltpu.VMEM((starts[FIRST], features), bf16),
            pltpu.SemaphoreType.DMA((2, FIRST)),
        ],
    )(cotangent)
    pack, pack_again = call(
        pack_kernel,
        mib=56,
        in_specs=[ANY] * 3,
        out_specs=[ANY] * 2,
        out_shape=[jax.ShapeDtypeStruct((2 * rank, features), bf16)] * 2,
        scratch_shapes=[pltpu.VMEM((2 * rank, features), bf16), pltpu.SemaphoreType.DMA((2,))],
    )(down, up, parts[0])
    def across(part, aside=0):
        slice_axes, found = ("tensor", "sub"), []
        for k in range(1, tensors):
            to = [(t + k) % tensors * subs + (s + aside) % subs for t in range(tensors) for s in range(subs)]
            found.append(lax.ppermute(part, slice_axes, list(enumerate(to))))
        return found

    def forward(blocks):
        return [shift(x, "sub", subs, 1) for x in blocks]

    direct = [across(part) for part in parts]
    pair = shift(cotangent, "sub", subs, 1)
    table = jax.ShapeDtypeStruct((n * cap,), jnp.int32)
    tile, live = call(
        functools.partial(plan_kernel, n, cap, tiles),
        in_specs=[SMEM] * 4,
        out_specs=[SMEM] * 2,
        out_shape=[table] * 2,
        scratch_shapes=[pltpu.SMEM((n,), jnp.int32)],
    )(adapter_per_tile, live_per_tile, adapter_stored_row, me.astype(jnp.int32).reshape(1))

    def after(arrays):
        return [ANY] * len(arrays)

    def gate(blocks, ready):
        found = call(
            gate_kernel,
            in_specs=after(blocks) + [ANY],
            out_specs=after(blocks),
            out_shape=[jax.ShapeDtypeStruct(x.shape, x.dtype) for x in blocks],
            input_output_aliases={i: i for i in range(len(blocks))},
        )(*blocks, ready)
        return list(found)

    def tick(*ready):
        return call(
            tick_kernel,
            flops=HEAVY,
            in_specs=after(ready),
            out_specs=VMEM,
            out_shape=jax.ShapeDtypeStruct((8, 128), f32),
        )(*ready)

    def ranks(g, *wait):
        return call(
            functools.partial(rank_kernel, g, cap),
            in_specs=[SMEM] * 2 + [VMEM] * (2 + len(g)) + after(wait),
            out_specs=VMEM,
            out_shape=jax.ShapeDtypeStruct((len(g) * cap * TILE, 2 * rank), bf16),
        )(tile, live, activations, cotangent, *[packs[k] for k in g], *wait)

    def chip_sum(own, *wait):
        given = shift(own, "sub", subs, 1)
        sent = call(
            functools.partial(sum_kernel, 2, -1),
            in_specs=[VMEM] * 2 + after(wait),
            out_specs=VMEM,
            out_shape=jax.ShapeDtypeStruct(own.shape, bf16),
        )(own, given, *wait)
        return given, sent

    def slice_sum(own, given, others, held_parts, *wait):
        found = [own, given, *others]
        shapes = [jax.ShapeDtypeStruct(x.shape, x.dtype) for x in held_parts]
        return call(
            functools.partial(sum_kernel, len(found), -1 - len(shapes)),
            in_specs=[VMEM] * len(found) + after(held_parts) + after(wait),
            out_specs=[VMEM] + after(held_parts),
            out_shape=[jax.ShapeDtypeStruct(own.shape, bf16)] + shapes,
            input_output_aliases={len(found) + i: 1 + i for i in range(len(shapes))},
        )(*found, *held_parts, *wait)

    def adapter_terms(g, held, *wait):
        found = call(
            functools.partial(terms_kernel, g, cap),
            in_specs=[SMEM] + [VMEM] * 3 + after(wait),
            out_specs=[VMEM] * len(g),
            out_shape=[jax.ShapeDtypeStruct((2 * rank, features), bf16)] * len(g),
        )(tile, held, activations, cotangent, *wait)
        return dict(zip(g, found))

    later = extents[FIRST:]
    rest = call(
        functools.partial(rest_kernel, len(later)),
        in_specs=[VMEM] + after(direct[0]),
        out_specs=[VMEM] * len(later),
        out_shape=[jax.ShapeDtypeStruct((e, features), bf16) for e in later],
    )(cotangent, *direct[0])
    parts = [*parts, *rest]

    first, second = groups
    packs = {0: pack} | {k: shift(pack, "adapter", n, k) for k in first}
    (pack_again,) = gate([pack_again], tile)
    packs |= {k: shift(pack_again, "adapter", n, k) for k in second if k}

    forwards = [forward(direct[0])]
    own = ranks(first, parts[-1])
    given, sent = chip_sum(own, tick(own), *forwards[0])
    mark = tick(sent)
    direct[1] = gate(direct[1], sent)
    forwards.append(forward(direct[1]))
    direct.append(across(*gate([parts[2]], mark)))
    (held,) = slice_sum(own, given, across(sent), [], mark, *forwards[1])
    sums = [held]
    own = ranks(second, held)
    terms = adapter_terms(first, held, own)
    arrived = {k: shift(terms[k], "adapter", n, -k) for k in first}

    given, sent = chip_sum(own, tick(own), terms[first[0]])
    held, part = slice_sum(own, given, across(sent), parts[3:4], tick(sent))
    direct.append(across(part))
    sums.append(held)
    terms |= adapter_terms(second, held)
    arrived |= {k: shift(terms[k], "adapter", n, -k) for k in second if k}
    direct[2] = gate(direct[2], held)
    forwards.append(forward(direct[2]))

    near = call(
        near_kernel,
        flops=HEAVY,
        in_specs=[SMEM] + [VMEM] * 3 + [ANY],
        out_specs=VMEM,
        out_shape=jax.ShapeDtypeStruct((rows, features), f32),
    )(place, cotangent, pair, frozen_weight, terms[second[-1]])
    blocks = [x for c in range(3) for x in direct[c] + forwards[c]]
    count = len(blocks) // 3
    operands = [tile, place, *blocks, *sums, *[packs[k] for k in range(n)], near, frozen_weight]
    whole_shape = jax.ShapeDtypeStruct((rows, features), bf16)
    out, term = call(
        functools.partial(middle_kernel, groups, cap, count),
        mib=20,
        flops=HEAVY,
        in_specs=[SMEM] * 2 + [VMEM] * (len(operands) - 2),
        out_specs=[HBM, VMEM],
        out_shape=[whole_shape] * 2,
        scratch_shapes=[pltpu.VMEM((starts[3], features), bf16), pltpu.SemaphoreType.DMA],
    )(*operands)
    direct[3] = gate(direct[3], term)
    forwards.append(forward(direct[3]))
    token_shape = jax.ShapeDtypeStruct((8, 128), f32)
    operands = [place, near, term, frozen_weight, *direct[3], *forwards[3]]
    out, token = call(
        functools.partial(far_kernel, count, starts[3]),
        mib=16,
        in_specs=[SMEM] + [VMEM] * (len(operands) - 1) + [HBM, ANY],
        out_specs=[HBM, VMEM],
        out_shape=[whole_shape, token_shape],
        scratch_shapes=[pltpu.VMEM((rows - starts[3], features), bf16), pltpu.SemaphoreType.DMA],
        input_output_aliases={len(operands): 0},
    )(*operands, out, tick(term))
    maps_shape = jax.ShapeDtypeStruct((rank, features), bf16)
    down_grad, up_grad = call(
        functools.partial(final_kernel, n, (stored / rows) ** 0.5),
        in_specs=[VMEM] * n + [ANY],
        out_specs=[VMEM] * 2,
        out_shape=[maps_shape] * 2,
    )(terms[0], *[arrived[k] for k in range(1, n)], token)
    down_grad = jnp.swapaxes(down_grad.reshape(stored, rank, features), 1, 2)
    up_grad = up_grad.reshape(stored, rank, features)
    return (out, down_grad, up_grad)


def solution(mesh):
    return jax.shard_map(
        on_device,
        mesh=mesh,
        in_specs=(
            P(("groups", "adapter"), ("tensor", "sub")),
            P(("groups", "adapter"), ("tensor", "sub")),
            P(("tensor", "sub"), None),
            P(("groups", "adapter"), ("tensor", "sub"), None),
            P(("groups", "adapter"), None, ("tensor", "sub")),
            P("groups"),
            P("groups"),
            P("groups"),
        ),
        out_specs=(
            P(("groups", "adapter"), ("tensor", "sub")),
            P(("groups", "adapter"), ("tensor", "sub"), None),
            P(("groups", "adapter"), None, ("tensor", "sub")),
        ),
        check_vma=False,
    )
```

```python
import functools

import jax
import jax.numpy as jnp
from jax import lax
from jax.experimental import pallas as pl
from jax.experimental.pallas import tpu as pltpu
from jax.sharding import PartitionSpec as P

TILE = 128
HEAVY = 1 << 33
CHUNKS = (3, 4, 4, 5)
FIRST = 2
NT = (((1,), (1,)), ((), ()))
SMEM = pl.BlockSpec(memory_space=pltpu.SMEM)
VMEM = pl.BlockSpec(memory_space=pltpu.VMEM)
ANY = pl.BlockSpec(memory_space=pl.ANY)
HBM = pl.BlockSpec(memory_space=pltpu.HBM)


def shift(array, axis, size, by):
    return lax.ppermute(array, axis, [(i, (i + by) % size) for i in range(size)])


def call(body, mib=12, flops=0, **kwargs):
    params = pltpu.CompilerParams(vmem_limit_bytes=mib * 1024 * 1024)
    cost = pl.CostEstimate(flops=flops, bytes_accessed=0, transcendentals=0)
    name = getattr(body, "func", body).__name__
    return pl.pallas_call(body, compiler_params=params, cost_estimate=cost, name=name, **kwargs)


def dot(a, b, dims=(((1,), (0,)), ((), ()))):
    return lax.dot_general(a, b, dims, preferred_element_type=jnp.float32)


def tile_rows(index):
    return pl.ds(pl.multiple_of(index * TILE, TILE), TILE)


def slot_rows(data, tile, entries):
    return jnp.concatenate([data[tile_rows(tile[e]), :] for e in entries], axis=0)


def copy_all(pairs, sems):
    copies = [pltpu.make_async_copy(a, b, sems.at[i]) for i, (a, b) in enumerate(pairs)]
    for copy in copies:
        copy.start()
    return copies


def head_kernel(cot, down, up, *refs):
    *parts, pack, again, held, pack_held, sems = refs
    rank, rows, start = down.shape[0], [], 0
    for part in parts:
        rows.append(pl.ds(start, part.shape[0]))
        start += part.shape[0]
    pairs = [(cot.at[r, :], held.at[r, :]) for r in rows]
    pairs += [(down, pack_held.at[pl.ds(0, rank), :]), (up, pack_held.at[pl.ds(rank, rank), :])]
    loads = copy_all(pairs, sems.at[0])
    stores = []
    for i, part in enumerate(parts):
        loads[i].wait()
        stores.append(pltpu.make_async_copy(held.at[rows[i], :], part, sems.at[1, i]))
        stores[-1].start()
    for load in loads[-2:]:
        load.wait()
    stores += copy_all([(pack_held, pack), (pack_held, again)], sems.at[2])
    for store in stores:
        store.wait()


def plan_kernel(n, cap, tiles, ids, live_all, stored, me, tile, live, count):
    for k in range(n):
        count[k] = 0
    for e in range(n * cap):
        tile[e] = 0
        live[e] = 0
    for t in range(tiles):
        at = me[0] * tiles + t
        k = lax.rem(me[0] - stored[ids[at]] + n, n)
        e = jnp.minimum(k * cap + count[k], n * cap - 1)
        tile[e] = t
        live[e] = live_all[at]
        count[k] = count[k] + 1


def rank_kernel(slots, cap, tile, live, act, cot, *refs):
    packs, out = refs[: len(slots)], refs[-1]
    width = packs[0].shape[0]
    part = lax.broadcasted_iota(jnp.int32, packs[0].shape, 0) < width // 2
    row = lax.broadcasted_iota(jnp.int32, (TILE, width), 0)
    for i, (slot, pack) in enumerate(zip(slots, packs)):
        entries = range(slot * cap, (slot + 1) * cap)
        maps = pack[...]
        zero = jnp.zeros_like(maps)
        both = dot(slot_rows(act, tile, entries), jnp.where(part, maps, zero), NT)
        both += dot(slot_rows(cot, tile, entries), jnp.where(part, zero, maps), NT)
        for c, e in enumerate(entries):
            at = (i * cap + c) * TILE
            out[at : at + TILE, :] = jnp.where(
                row < live[e], both[c * TILE : (c + 1) * TILE], 0.0
            ).astype(jnp.bfloat16)


def sum_kernel(count, place, *refs):
    total = refs[0][...].astype(jnp.float32)
    for x in refs[1:count]:
        total += x[...].astype(jnp.float32)
    out = refs[place]
    out[...] = total.astype(out.dtype)


def gate_kernel(*refs):
    pass


def tick_kernel(*refs):
    refs[-1][...] = jnp.zeros_like(refs[-1])


def terms_kernel(slots, cap, tile, held, act, cot, *refs):
    terms = refs[-len(slots) :]
    rank = held.shape[1] // 2
    for i, slot in enumerate(slots):
        entries = range(slot * cap, (slot + 1) * cap)
        both = held[i * cap * TILE : (i + 1) * cap * TILE, :].astype(jnp.float32)
        both = both.T.astype(jnp.bfloat16)
        terms[i][:rank, :] = dot(both[rank:], slot_rows(act, tile, entries)).astype(jnp.bfloat16)
        terms[i][rank:, :] = dot(both[:rank], slot_rows(cot, tile, entries)).astype(jnp.bfloat16)


def weight_columns(weight, place):
    features = weight.shape[0]
    return weight[:, pl.ds(pl.multiple_of(place * features, 128), features)]


def near_kernel(count, place, own, pair, weight, *refs):
    out, *parts = refs[-count:]
    start = own.shape[0] - sum(part.shape[0] for part in parts)
    for part in parts:
        part[...] = own[start : start + part.shape[0], :]
        start += part.shape[0]
    out[...] = dot(own[...], weight_columns(weight, place[0]), NT)
    out[...] += dot(pair[...], weight_columns(weight, place[1]), NT)


def row_sums(start, count, place, near, term, weight, blocks, out, done, sem):
    at = 0
    for first in range(0, len(blocks), count):
        extent = blocks[first].shape[0]
        rows = slice(start + at, start + at + extent)
        total = near[rows, :] + term[rows, :].astype(jnp.float32)
        for i in range(count):
            total += dot(blocks[first + i][...], weight_columns(weight, place[2 + i]), NT)
        done[at : at + extent, :] = total.astype(jnp.bfloat16)
        at += extent
    copy = pltpu.make_async_copy(done, out.at[pl.ds(start, at), :], sem)
    copy.start()
    copy.wait()


def middle_kernel(groups, cap, count, tile, place, *refs):
    n = sum(len(g) for g in groups)
    blocks, refs = refs[: 3 * count], refs[3 * count :]
    sums, refs = refs[: len(groups)], refs[len(groups) :]
    packs, (near, weight), refs = refs[:n], refs[n : n + 2], refs[n + 2 :]
    out, term, done, sem = refs[-4:]
    term[...] = jnp.zeros_like(term)
    for g, slots in enumerate(groups):
        for i, slot in enumerate(slots):
            maps = packs[slot][...]
            rank = maps.shape[0] // 2
            maps = jnp.concatenate([jnp.zeros_like(maps[:rank]), maps[:rank]], axis=0)
            found = dot(sums[g][i * cap * TILE : (i + 1) * cap * TILE, :], maps)
            for c in range(cap):
                rows = tile_rows(tile[slot * cap + c])
                before = term[rows, :].astype(jnp.float32)
                term[rows, :] = (before + found[c * TILE : (c + 1) * TILE]).astype(term.dtype)
    row_sums(0, count, place, near, term, weight, blocks, out, done, sem)


def far_kernel(count, start, place, near, term, weight, *refs):
    out, done, sem = refs[-3:]
    row_sums(start, count, place, near, term, weight, refs[:count], out, done, sem)


def final_kernel(count, scale, *refs):
    down, up, token = refs[-3:]
    token[...] = jnp.zeros_like(token)
    rank = down.shape[0]
    for out, rows in ((down, slice(0, rank)), (up, slice(rank, 2 * rank))):
        total = refs[0][rows, :].astype(jnp.float32)
        for x in refs[1:count]:
            total += x[rows, :].astype(jnp.float32)
        out[...] = (total * scale).astype(out.dtype)


def on_device(
    activations,
    cotangent,
    frozen_weight,
    adapter_down_maps,
    adapter_up_maps,
    adapter_per_tile,
    live_per_tile,
    adapter_stored_row,
):
    rows, features = activations.shape
    tiles = rows // TILE
    stored, _, rank = adapter_down_maps.shape
    n = lax.axis_size("adapter")
    tensors = lax.axis_size("tensor")
    subs = lax.axis_size("sub")
    me = lax.axis_index("adapter")
    t_me, s_me = lax.axis_index("tensor"), lax.axis_index("sub")
    extents = [rows * c // sum(CHUNKS) for c in CHUNKS]
    starts = [sum(extents[:c]) for c in range(len(extents))]
    bf16, f32 = jnp.bfloat16, jnp.float32

    cap = -(-tiles // n)
    places = [t_me * subs + s_me, t_me * subs + (1 - s_me)]
    for s in (s_me, 1 - s_me):
        places += [jnp.remainder(t_me - k, tensors) * subs + s for k in range(1, tensors)]
    place = jnp.stack(places).astype(jnp.int32)

    groups = [[k for k in range(n) if 1 <= min(k, n - k) <= n // 4]]
    groups.append([k for k in range(n) if k not in groups[0]])

    down = jnp.swapaxes(adapter_down_maps, 1, 2).reshape(stored * rank, features)
    up = adapter_up_maps.reshape(stored * rank, features)
    pack_shape = jax.ShapeDtypeStruct((2 * rank, features), bf16)
    *parts, pack, pack_again = call(
        head_kernel,
        mib=56,
        in_specs=[ANY] * 3,
        out_specs=[ANY] * (FIRST + 2),
        out_shape=[jax.ShapeDtypeStruct((e, features), bf16) for e in extents[:FIRST]]
        + [pack_shape] * 2,
        scratch_shapes=[
            pltpu.VMEM((starts[FIRST], features), bf16),
            pltpu.VMEM(pack_shape.shape, bf16),
            pltpu.SemaphoreType.DMA((3, FIRST + 2)),
        ],
    )(cotangent, down, up)
    def across(part, aside=0):
        slice_axes, found = ("tensor", "sub"), []
        for k in range(1, tensors):
            to = [(t + k) % tensors * subs + (s + aside) % subs for t in range(tensors) for s in range(subs)]
            found.append(lax.ppermute(part, slice_axes, list(enumerate(to))))
        return found

    def forward(blocks):
        return [shift(x, "sub", subs, 1) for x in blocks]

    direct = [across(part) for part in parts]
    pair = shift(cotangent, "sub", subs, 1)
    table = jax.ShapeDtypeStruct((n * cap,), jnp.int32)
    tile, live = call(
        functools.partial(plan_kernel, n, cap, tiles),
        in_specs=[SMEM] * 4,
        out_specs=[SMEM] * 2,
        out_shape=[table] * 2,
        scratch_shapes=[pltpu.SMEM((n,), jnp.int32)],
    )(adapter_per_tile, live_per_tile, adapter_stored_row, me.astype(jnp.int32).reshape(1))

    def after(arrays):
        return [ANY] * len(arrays)

    def gate(blocks, ready):
        found = call(
            gate_kernel,
            in_specs=after(blocks) + [ANY],
            out_specs=after(blocks),
            out_shape=[jax.ShapeDtypeStruct(x.shape, x.dtype) for x in blocks],
            input_output_aliases={i: i for i in range(len(blocks))},
        )(*blocks, ready)
        return list(found)

    def tick(*ready):
        return call(
            tick_kernel,
            flops=HEAVY,
            in_specs=after(ready),
            out_specs=VMEM,
            out_shape=jax.ShapeDtypeStruct((8, 128), f32),
        )(*ready)

    def ranks(g, *wait):
        return call(
            functools.partial(rank_kernel, g, cap),
            in_specs=[SMEM] * 2 + [VMEM] * (2 + len(g)) + after(wait),
            out_specs=VMEM,
            out_shape=jax.ShapeDtypeStruct((len(g) * cap * TILE, 2 * rank), bf16),
        )(tile, live, activations, cotangent, *[packs[k] for k in g], *wait)

    def chip_sum(own, *wait):
        given = shift(own, "sub", subs, 1)
        sent = call(
            functools.partial(sum_kernel, 2, -1),
            in_specs=[VMEM] * 2 + after(wait),
            out_specs=VMEM,
            out_shape=jax.ShapeDtypeStruct(own.shape, bf16),
        )(own, given, *wait)
        return given, sent

    def slice_sum(own, given, others, held_parts, *wait):
        found = [own, given, *others]
        shapes = [jax.ShapeDtypeStruct(x.shape, x.dtype) for x in held_parts]
        return call(
            functools.partial(sum_kernel, len(found), -1 - len(shapes)),
            in_specs=[VMEM] * len(found) + after(held_parts) + after(wait),
            out_specs=[VMEM] + after(held_parts),
            out_shape=[jax.ShapeDtypeStruct(own.shape, bf16)] + shapes,
            input_output_aliases={len(found) + i: 1 + i for i in range(len(shapes))},
        )(*found, *held_parts, *wait)

    def adapter_terms(g, held, *wait):
        found = call(
            functools.partial(terms_kernel, g, cap),
            in_specs=[SMEM] + [VMEM] * 3 + after(wait),
            out_specs=[VMEM] * len(g),
            out_shape=[jax.ShapeDtypeStruct((2 * rank, features), bf16)] * len(g),
        )(tile, held, activations, cotangent, *wait)
        return dict(zip(g, found))

    later = extents[FIRST:]
    near, *rest = call(
        functools.partial(near_kernel, 1 + len(later)),
        flops=HEAVY,
        in_specs=[SMEM] + [VMEM] * 3 + after(direct[0]),
        out_specs=[VMEM] * (1 + len(later)),
        out_shape=[jax.ShapeDtypeStruct((rows, features), f32)]
        + [jax.ShapeDtypeStruct((e, features), bf16) for e in later],
    )(place, cotangent, pair, frozen_weight, *direct[0])
    parts = [*parts, *rest]

    first, second = groups
    packs = {0: pack} | {k: shift(pack, "adapter", n, k) for k in first}
    (pack_again,) = gate([pack_again], tile)
    packs |= {k: shift(pack_again, "adapter", n, k) for k in second if k}

    forwards = [forward(direct[0])]
    own = ranks(first, near)
    given, sent = chip_sum(own, tick(own), *forwards[0])
    mark = tick(sent)
    direct[1] = gate(direct[1], sent)
    forwards.append(forward(direct[1]))
    direct.append(across(*gate([parts[2]], mark)))
    (held,) = slice_sum(own, given, across(sent), [], mark, *forwards[1])
    sums = [held]
    own = ranks(second, held)
    terms = adapter_terms(first, held, own)
    arrived = {k: shift(terms[k], "adapter", n, -k) for k in first}

    given, sent = chip_sum(own, tick(own), terms[first[0]])
    mark = tick(sent)
    direct.append(across(*gate([parts[3]], mark)))
    (held,) = slice_sum(own, given, across(sent), [], mark)
    sums.append(held)
    terms |= adapter_terms(second, held)
    arrived |= {k: shift(terms[k], "adapter", n, -k) for k in second if k}
    direct[2] = gate(direct[2], held)
    forwards.append(forward(direct[2]))

    blocks = [x for c in range(3) for x in direct[c] + forwards[c]]
    count = len(blocks) // 3
    operands = [tile, place, *blocks, *sums, *[packs[k] for k in range(n)], near, frozen_weight]
    whole_shape = jax.ShapeDtypeStruct((rows, features), bf16)
    out, term = call(
        functools.partial(middle_kernel, groups, cap, count),
        mib=20,
        flops=HEAVY,
        in_specs=[SMEM] * 2 + [VMEM] * (len(operands) - 2) + [ANY] * 2,
        out_specs=[HBM, VMEM],
        out_shape=[whole_shape] * 2,
        scratch_shapes=[pltpu.VMEM((starts[3], features), bf16), pltpu.SemaphoreType.DMA],
    )(*operands, terms[second[-1]], tick(held))
    direct[3] = gate(direct[3], term)
    forwards.append(forward(direct[3]))
    maps_shape = jax.ShapeDtypeStruct((rank, features), bf16)
    down_grad, up_grad, token = call(
        functools.partial(final_kernel, n, (stored / rows) ** 0.5),
        flops=HEAVY,
        in_specs=[VMEM] * n,
        out_specs=[VMEM] * 3,
        out_shape=[maps_shape] * 2 + [jax.ShapeDtypeStruct((8, 128), f32)],
    )(terms[0], *[arrived[k] for k in range(1, n)])
    operands = [place, near, term, frozen_weight, *direct[3], *forwards[3]]
    out = call(
        functools.partial(far_kernel, count, starts[3]),
        mib=16,
        in_specs=[SMEM] + [VMEM] * (len(operands) - 1) + [HBM, VMEM],
        out_specs=HBM,
        out_shape=whole_shape,
        scratch_shapes=[pltpu.VMEM((rows - starts[3], features), bf16), pltpu.SemaphoreType.DMA],
        input_output_aliases={len(operands): 0},
    )(*operands, out, token)
    down_grad = jnp.swapaxes(down_grad.reshape(stored, rank, features), 1, 2)
    up_grad = up_grad.reshape(stored, rank, features)
    return (out, down_grad, up_grad)


def solution(mesh):
    return jax.shard_map(
        on_device,
        mesh=mesh,
        in_specs=(
            P(("groups", "adapter"), ("tensor", "sub")),
            P(("groups", "adapter"), ("tensor", "sub")),
            P(("tensor", "sub"), None),
            P(("groups", "adapter"), ("tensor", "sub"), None),
            P(("groups", "adapter"), None, ("tensor", "sub")),
            P("groups"),
            P("groups"),
            P("groups"),
        ),
        out_specs=(
            P(("groups", "adapter"), ("tensor", "sub")),
            P(("groups", "adapter"), ("tensor", "sub"), None),
            P(("groups", "adapter"), None, ("tensor", "sub")),
        ),
        check_vma=False,
    )
```

```python
import functools

import jax
import jax.numpy as jnp
from jax import lax
from jax.experimental import pallas as pl
from jax.experimental.pallas import tpu as pltpu
from jax.sharding import PartitionSpec as P

TILE = 128
HEAVY = 1 << 33
CHUNKS = (3, 4, 4, 5)
FIRST = 2
NT = (((1,), (1,)), ((), ()))
SMEM = pl.BlockSpec(memory_space=pltpu.SMEM)
VMEM = pl.BlockSpec(memory_space=pltpu.VMEM)
ANY = pl.BlockSpec(memory_space=pl.ANY)
HBM = pl.BlockSpec(memory_space=pltpu.HBM)


def shift(array, axis, size, by):
    return lax.ppermute(array, axis, [(i, (i + by) % size) for i in range(size)])


def call(body, mib=12, flops=0, **kwargs):
    params = pltpu.CompilerParams(vmem_limit_bytes=mib * 1024 * 1024)
    cost = pl.CostEstimate(flops=flops, bytes_accessed=0, transcendentals=0)
    name = getattr(body, "func", body).__name__
    return pl.pallas_call(body, compiler_params=params, cost_estimate=cost, name=name, **kwargs)


def dot(a, b, dims=(((1,), (0,)), ((), ()))):
    return lax.dot_general(a, b, dims, preferred_element_type=jnp.float32)


def tile_rows(index):
    return pl.ds(pl.multiple_of(index * TILE, TILE), TILE)


def slot_rows(data, tile, entries):
    return jnp.concatenate([data[tile_rows(tile[e]), :] for e in entries], axis=0)


def copy_all(pairs, sems):
    copies = [pltpu.make_async_copy(a, b, sems.at[i]) for i, (a, b) in enumerate(pairs)]
    for copy in copies:
        copy.start()
    return copies


def head_kernel(cot, down, up, *refs):
    *parts, pack, again, held, pack_held, sems = refs
    rank, rows, start = down.shape[0], [], 0
    for part in parts:
        rows.append(pl.ds(start, part.shape[0]))
        start += part.shape[0]
    pairs = [(cot.at[r, :], held.at[r, :]) for r in rows]
    pairs += [(down, pack_held.at[pl.ds(0, rank), :]), (up, pack_held.at[pl.ds(rank, rank), :])]
    loads = copy_all(pairs, sems.at[0])
    stores = []
    for i, part in enumerate(parts):
        loads[i].wait()
        stores.append(pltpu.make_async_copy(held.at[rows[i], :], part, sems.at[1, i]))
        stores[-1].start()
    for load in loads[-2:]:
        load.wait()
    stores += copy_all([(pack_held, pack), (pack_held, again)], sems.at[2])
    for store in stores:
        store.wait()


def plan_kernel(n, cap, tiles, ids, live_all, stored, me, tile, live, count):
    for k in range(n):
        count[k] = 0
    for e in range(n * cap):
        tile[e] = 0
        live[e] = 0
    for t in range(tiles):
        at = me[0] * tiles + t
        k = lax.rem(me[0] - stored[ids[at]] + n, n)
        e = jnp.minimum(k * cap + count[k], n * cap - 1)
        tile[e] = t
        live[e] = live_all[at]
        count[k] = count[k] + 1


def rank_kernel(slots, cap, tile, live, act, cot, *refs):
    packs, out = refs[: len(slots)], refs[-1]
    width = packs[0].shape[0]
    part = lax.broadcasted_iota(jnp.int32, packs[0].shape, 0) < width // 2
    row = lax.broadcasted_iota(jnp.int32, (TILE, width), 0)
    for i, (slot, pack) in enumerate(zip(slots, packs)):
        entries = range(slot * cap, (slot + 1) * cap)
        maps = pack[...]
        zero = jnp.zeros_like(maps)
        both = dot(slot_rows(act, tile, entries), jnp.where(part, maps, zero), NT)
        both += dot(slot_rows(cot, tile, entries), jnp.where(part, zero, maps), NT)
        for c, e in enumerate(entries):
            at = (i * cap + c) * TILE
            out[at : at + TILE, :] = jnp.where(
                row < live[e], both[c * TILE : (c + 1) * TILE], 0.0
            ).astype(jnp.bfloat16)


def sum_kernel(count, place, *refs):
    total = refs[0][...].astype(jnp.float32)
    for x in refs[1:count]:
        total += x[...].astype(jnp.float32)
    out = refs[place]
    out[...] = total.astype(out.dtype)


def gate_kernel(*refs):
    pass


def tick_kernel(*refs):
    refs[-1][...] = jnp.zeros_like(refs[-1])


def terms_kernel(slots, cap, tile, held, act, cot, *refs):
    terms = refs[-len(slots) :]
    rank = held.shape[1] // 2
    for i, slot in enumerate(slots):
        entries = range(slot * cap, (slot + 1) * cap)
        both = held[i * cap * TILE : (i + 1) * cap * TILE, :].astype(jnp.float32)
        both = both.T.astype(jnp.bfloat16)
        terms[i][:rank, :] = dot(both[rank:], slot_rows(act, tile, entries)).astype(jnp.bfloat16)
        terms[i][rank:, :] = dot(both[:rank], slot_rows(cot, tile, entries)).astype(jnp.bfloat16)


def weight_columns(weight, place):
    features = weight.shape[0]
    return weight[:, pl.ds(pl.multiple_of(place * features, 128), features)]


def near_kernel(count, place, own, pair, weight, *refs):
    out, *parts = refs[-count:]
    start = own.shape[0] - sum(part.shape[0] for part in parts)
    for part in parts:
        part[...] = own[start : start + part.shape[0], :]
        start += part.shape[0]
    out[...] = dot(own[...], weight_columns(weight, place[0]), NT)
    out[...] += dot(pair[...], weight_columns(weight, place[1]), NT)


def row_sums(start, count, place, near, term, weight, blocks, out, done, sem):
    at = 0
    for first in range(0, len(blocks), count):
        extent = blocks[first].shape[0]
        rows = slice(start + at, start + at + extent)
        total = near[rows, :] + term[rows, :].astype(jnp.float32)
        for i in range(count):
            total += dot(blocks[first + i][...], weight_columns(weight, place[2 + i]), NT)
        done[at : at + extent, :] = total.astype(jnp.bfloat16)
        at += extent
    copy = pltpu.make_async_copy(done, out.at[pl.ds(start, at), :], sem)
    copy.start()
    copy.wait()


def middle_kernel(groups, cap, count, tile, place, *refs):
    n = sum(len(g) for g in groups)
    blocks, refs = refs[: 3 * count], refs[3 * count :]
    sums, refs = refs[: len(groups)], refs[len(groups) :]
    packs, (near, weight), refs = refs[:n], refs[n : n + 2], refs[n + 2 :]
    out, term, done, sem = refs[-4:]
    term[...] = jnp.zeros_like(term)
    for g, slots in enumerate(groups):
        for i, slot in enumerate(slots):
            maps = packs[slot][...]
            rank = maps.shape[0] // 2
            maps = jnp.concatenate([jnp.zeros_like(maps[:rank]), maps[:rank]], axis=0)
            found = dot(sums[g][i * cap * TILE : (i + 1) * cap * TILE, :], maps)
            for c in range(cap):
                rows = tile_rows(tile[slot * cap + c])
                before = term[rows, :].astype(jnp.float32)
                term[rows, :] = (before + found[c * TILE : (c + 1) * TILE]).astype(term.dtype)
    row_sums(0, count, place, near, term, weight, blocks, out, done, sem)


def far_kernel(count, start, place, near, term, weight, *refs):
    out, done, sem = refs[-3:]
    row_sums(start, count, place, near, term, weight, refs[:count], out, done, sem)


def final_kernel(count, scale, *refs):
    down, up, token = refs[-3:]
    token[...] = jnp.zeros_like(token)
    rank = down.shape[0]
    for out, rows in ((down, slice(0, rank)), (up, slice(rank, 2 * rank))):
        total = refs[0][rows, :].astype(jnp.float32)
        for x in refs[1:count]:
            total += x[rows, :].astype(jnp.float32)
        out[...] = (total * scale).astype(out.dtype)


def on_device(
    activations,
    cotangent,
    frozen_weight,
    adapter_down_maps,
    adapter_up_maps,
    adapter_per_tile,
    live_per_tile,
    adapter_stored_row,
):
    rows, features = activations.shape
    tiles = rows // TILE
    stored, _, rank = adapter_down_maps.shape
    n = lax.axis_size("adapter")
    tensors = lax.axis_size("tensor")
    subs = lax.axis_size("sub")
    me = lax.axis_index("adapter")
    t_me, s_me = lax.axis_index("tensor"), lax.axis_index("sub")
    extents = [rows * c // sum(CHUNKS) for c in CHUNKS]
    starts = [sum(extents[:c]) for c in range(len(extents))]
    bf16, f32 = jnp.bfloat16, jnp.float32

    cap = -(-tiles // n)
    places = [t_me * subs + s_me, t_me * subs + (1 - s_me)]
    for s in (s_me, 1 - s_me):
        places += [jnp.remainder(t_me - k, tensors) * subs + s for k in range(1, tensors)]
    place = jnp.stack(places).astype(jnp.int32)

    groups = [[k for k in range(n) if 1 <= min(k, n - k) <= n // 4]]
    groups.append([k for k in range(n) if k not in groups[0]])

    down = jnp.swapaxes(adapter_down_maps, 1, 2).reshape(stored * rank, features)
    up = adapter_up_maps.reshape(stored * rank, features)
    pack_shape = jax.ShapeDtypeStruct((2 * rank, features), bf16)
    *parts, pack, pack_again = call(
        head_kernel,
        mib=56,
        in_specs=[ANY] * 3,
        out_specs=[ANY] * (FIRST + 2),
        out_shape=[jax.ShapeDtypeStruct((e, features), bf16) for e in extents[:FIRST]]
        + [pack_shape] * 2,
        scratch_shapes=[
            pltpu.VMEM((starts[FIRST], features), bf16),
            pltpu.VMEM(pack_shape.shape, bf16),
            pltpu.SemaphoreType.DMA((3, FIRST + 2)),
        ],
    )(cotangent, down, up)
    def across(part, aside=0):
        slice_axes, found = ("tensor", "sub"), []
        for k in range(1, tensors):
            to = [(t + k) % tensors * subs + (s + aside) % subs for t in range(tensors) for s in range(subs)]
            found.append(lax.ppermute(part, slice_axes, list(enumerate(to))))
        return found

    def forward(blocks):
        return [shift(x, "sub", subs, 1) for x in blocks]

    direct = [across(part) for part in parts]
    pair = shift(cotangent, "sub", subs, 1)
    table = jax.ShapeDtypeStruct((n * cap,), jnp.int32)
    tile, live = call(
        functools.partial(plan_kernel, n, cap, tiles),
        in_specs=[SMEM] * 4,
        out_specs=[SMEM] * 2,
        out_shape=[table] * 2,
        scratch_shapes=[pltpu.SMEM((n,), jnp.int32)],
    )(adapter_per_tile, live_per_tile, adapter_stored_row, me.astype(jnp.int32).reshape(1))

    def after(arrays):
        return [ANY] * len(arrays)

    def gate(blocks, ready):
        found = call(
            gate_kernel,
            in_specs=after(blocks) + [ANY],
            out_specs=after(blocks),
            out_shape=[jax.ShapeDtypeStruct(x.shape, x.dtype) for x in blocks],
            input_output_aliases={i: i for i in range(len(blocks))},
        )(*blocks, ready)
        return list(found)

    def tick(*ready):
        return call(
            tick_kernel,
            flops=HEAVY,
            in_specs=after(ready),
            out_specs=VMEM,
            out_shape=jax.ShapeDtypeStruct((8, 128), f32),
        )(*ready)

    def ranks(g, *wait):
        return call(
            functools.partial(rank_kernel, g, cap),
            in_specs=[SMEM] * 2 + [VMEM] * (2 + len(g)) + after(wait),
            out_specs=VMEM,
            out_shape=jax.ShapeDtypeStruct((len(g) * cap * TILE, 2 * rank), bf16),
        )(tile, live, activations, cotangent, *[packs[k] for k in g], *wait)

    def chip_sum(own, *wait):
        given = shift(own, "sub", subs, 1)
        sent = call(
            functools.partial(sum_kernel, 2, -1),
            in_specs=[VMEM] * 2 + after(wait),
            out_specs=VMEM,
            out_shape=jax.ShapeDtypeStruct(own.shape, bf16),
        )(own, given, *wait)
        return given, sent

    def slice_sum(own, given, others, held_parts, *wait):
        found = [own, given, *others]
        shapes = [jax.ShapeDtypeStruct(x.shape, x.dtype) for x in held_parts]
        return call(
            functools.partial(sum_kernel, len(found), -1 - len(shapes)),
            in_specs=[VMEM] * len(found) + after(held_parts) + after(wait),
            out_specs=[VMEM] + after(held_parts),
            out_shape=[jax.ShapeDtypeStruct(own.shape, bf16)] + shapes,
            input_output_aliases={len(found) + i: 1 + i for i in range(len(shapes))},
        )(*found, *held_parts, *wait)

    def adapter_terms(g, held, *wait):
        found = call(
            functools.partial(terms_kernel, g, cap),
            in_specs=[SMEM] + [VMEM] * 3 + after(wait),
            out_specs=[VMEM] * len(g),
            out_shape=[jax.ShapeDtypeStruct((2 * rank, features), bf16)] * len(g),
        )(tile, held, activations, cotangent, *wait)
        return dict(zip(g, found))

    later = extents[FIRST:]
    near, *rest = call(
        functools.partial(near_kernel, 1 + len(later)),
        flops=HEAVY,
        in_specs=[SMEM] + [VMEM] * 3 + after(direct[0]),
        out_specs=[VMEM] * (1 + len(later)),
        out_shape=[jax.ShapeDtypeStruct((rows, features), f32)]
        + [jax.ShapeDtypeStruct((e, features), bf16) for e in later],
    )(place, cotangent, pair, frozen_weight, *direct[0])
    parts = [*parts, *rest]

    first, second = groups
    packs = {0: pack} | {k: shift(pack, "adapter", n, k) for k in first}
    (pack_again,) = gate([pack_again], tile)
    packs |= {k: shift(pack_again, "adapter", n, k) for k in second if k}

    forwards = [forward(direct[0])]
    own = ranks(first, near)
    given, sent = chip_sum(own, tick(own), *forwards[0])
    mark = tick(sent)
    direct[1] = gate(direct[1], sent)
    forwards.append(forward(direct[1]))
    (held,) = slice_sum(own, given, across(sent), [], mark, *forwards[1])
    direct.append(across(*gate([parts[2]], held)))
    sums = [held]
    own = ranks(second, held)
    terms = adapter_terms(first, held, own)
    given, sent = chip_sum(own, tick(own), terms[first[0]])
    mark = tick(sent)
    leaving = gate([terms[k] for k in first], mark)
    arrived = {k: shift(x, "adapter", n, -k) for k, x in zip(first, leaving)}
    (held,) = slice_sum(own, given, across(sent), [], mark)
    direct.append(across(*gate([parts[3]], held)))
    sums.append(held)
    terms |= adapter_terms(second, held)
    arrived |= {k: shift(terms[k], "adapter", n, -k) for k in second if k}
    direct[2] = gate(direct[2], held)
    forwards.append(forward(direct[2]))

    blocks = [x for c in range(3) for x in direct[c] + forwards[c]]
    count = len(blocks) // 3
    operands = [tile, place, *blocks, *sums, *[packs[k] for k in range(n)], near, frozen_weight]
    whole_shape = jax.ShapeDtypeStruct((rows, features), bf16)
    out, term = call(
        functools.partial(middle_kernel, groups, cap, count),
        mib=20,
        flops=HEAVY,
        in_specs=[SMEM] * 2 + [VMEM] * (len(operands) - 2) + [ANY] * 2,
        out_specs=[HBM, VMEM],
        out_shape=[whole_shape] * 2,
        scratch_shapes=[pltpu.VMEM((starts[3], features), bf16), pltpu.SemaphoreType.DMA],
    )(*operands, terms[second[-1]], tick(held))
    direct[3] = gate(direct[3], term)
    forwards.append(forward(direct[3]))
    maps_shape = jax.ShapeDtypeStruct((rank, features), bf16)
    down_grad, up_grad, token = call(
        functools.partial(final_kernel, n, (stored / rows) ** 0.5),
        flops=HEAVY,
        in_specs=[VMEM] * n,
        out_specs=[VMEM] * 3,
        out_shape=[maps_shape] * 2 + [jax.ShapeDtypeStruct((8, 128), f32)],
    )(terms[0], *[arrived[k] for k in range(1, n)])
    operands = [place, near, term, frozen_weight, *direct[3], *forwards[3]]
    out = call(
        functools.partial(far_kernel, count, starts[3]),
        mib=16,
        in_specs=[SMEM] + [VMEM] * (len(operands) - 1) + [HBM, VMEM],
        out_specs=HBM,
        out_shape=whole_shape,
        scratch_shapes=[pltpu.VMEM((rows - starts[3], features), bf16), pltpu.SemaphoreType.DMA],
        input_output_aliases={len(operands): 0},
    )(*operands, out, token)
    down_grad = jnp.swapaxes(down_grad.reshape(stored, rank, features), 1, 2)
    up_grad = up_grad.reshape(stored, rank, features)
    return (out, down_grad, up_grad)


def solution(mesh):
    return jax.shard_map(
        on_device,
        mesh=mesh,
        in_specs=(
            P(("groups", "adapter"), ("tensor", "sub")),
            P(("groups", "adapter"), ("tensor", "sub")),
            P(("tensor", "sub"), None),
            P(("groups", "adapter"), ("tensor", "sub"), None),
            P(("groups", "adapter"), None, ("tensor", "sub")),
            P("groups"),
            P("groups"),
            P("groups"),
        ),
        out_specs=(
            P(("groups", "adapter"), ("tensor", "sub")),
            P(("groups", "adapter"), ("tensor", "sub"), None),
            P(("groups", "adapter"), None, ("tensor", "sub")),
        ),
        check_vma=False,
    )
```

```python
import functools

import jax
import jax.numpy as jnp
from jax import lax
from jax.experimental import pallas as pl
from jax.experimental.pallas import tpu as pltpu
from jax.sharding import PartitionSpec as P

TILE = 128
HEAVY = 1 << 33
CHUNKS = (3, 4, 4, 5)
FIRST = 2
NT = (((1,), (1,)), ((), ()))
SMEM = pl.BlockSpec(memory_space=pltpu.SMEM)
VMEM = pl.BlockSpec(memory_space=pltpu.VMEM)
ANY = pl.BlockSpec(memory_space=pl.ANY)
HBM = pl.BlockSpec(memory_space=pltpu.HBM)


def shift(array, axis, size, by):
    return lax.ppermute(array, axis, [(i, (i + by) % size) for i in range(size)])


def call(body, mib=12, flops=0, **kwargs):
    params = pltpu.CompilerParams(vmem_limit_bytes=mib * 1024 * 1024)
    cost = pl.CostEstimate(flops=flops, bytes_accessed=0, transcendentals=0)
    name = getattr(body, "func", body).__name__
    return pl.pallas_call(body, compiler_params=params, cost_estimate=cost, name=name, **kwargs)


def dot(a, b, dims=(((1,), (0,)), ((), ()))):
    return lax.dot_general(a, b, dims, preferred_element_type=jnp.float32)


def tile_rows(index):
    return pl.ds(pl.multiple_of(index * TILE, TILE), TILE)


def slot_rows(data, tile, entries):
    return jnp.concatenate([data[tile_rows(tile[e]), :] for e in entries], axis=0)


def copy_all(pairs, sems):
    copies = [pltpu.make_async_copy(a, b, sems.at[i]) for i, (a, b) in enumerate(pairs)]
    for copy in copies:
        copy.start()
    return copies


def head_kernel(cot, down, up, *refs):
    *parts, pack, again, held, pack_held, sems = refs
    rank, rows, start = down.shape[0], [], 0
    for part in parts:
        rows.append(pl.ds(start, part.shape[0]))
        start += part.shape[0]
    pairs = [(cot.at[r, :], held.at[r, :]) for r in rows]
    pairs += [(down, pack_held.at[pl.ds(0, rank), :]), (up, pack_held.at[pl.ds(rank, rank), :])]
    loads = copy_all(pairs, sems.at[0])
    stores = []
    for i, part in enumerate(parts):
        loads[i].wait()
        stores.append(pltpu.make_async_copy(held.at[rows[i], :], part, sems.at[1, i]))
        stores[-1].start()
    for load in loads[-2:]:
        load.wait()
    stores += copy_all([(pack_held, pack), (pack_held, again)], sems.at[2])
    for store in stores:
        store.wait()


def plan_kernel(n, cap, tiles, ids, live_all, stored, me, _, tile, live, count):
    for k in range(n):
        count[k] = 0
    for e in range(n * cap):
        tile[e] = 0
        live[e] = 0
    for t in range(tiles):
        at = me[0] * tiles + t
        k = lax.rem(me[0] - stored[ids[at]] + n, n)
        e = jnp.minimum(k * cap + count[k], n * cap - 1)
        tile[e] = t
        live[e] = live_all[at]
        count[k] = count[k] + 1


def rank_kernel(slots, cap, tile, live, act, cot, *refs):
    packs, out = refs[: len(slots)], refs[-1]
    width = packs[0].shape[0]
    part = lax.broadcasted_iota(jnp.int32, packs[0].shape, 0) < width // 2
    row = lax.broadcasted_iota(jnp.int32, (TILE, width), 0)
    for i, (slot, pack) in enumerate(zip(slots, packs)):
        entries = range(slot * cap, (slot + 1) * cap)
        maps = pack[...]
        zero = jnp.zeros_like(maps)
        both = dot(slot_rows(act, tile, entries), jnp.where(part, maps, zero), NT)
        both += dot(slot_rows(cot, tile, entries), jnp.where(part, zero, maps), NT)
        for c, e in enumerate(entries):
            at = (i * cap + c) * TILE
            out[at : at + TILE, :] = jnp.where(
                row < live[e], both[c * TILE : (c + 1) * TILE], 0.0
            ).astype(jnp.bfloat16)


def sum_kernel(count, place, *refs):
    total = refs[0][...].astype(jnp.float32)
    for x in refs[1:count]:
        total += x[...].astype(jnp.float32)
    out = refs[place]
    out[...] = total.astype(out.dtype)


def gate_kernel(*refs):
    pass


def tick_kernel(*refs):
    refs[-1][...] = jnp.zeros_like(refs[-1])


def terms_kernel(slots, cap, tile, held, act, cot, *refs):
    terms = refs[-len(slots) :]
    rank = held.shape[1] // 2
    for i, slot in enumerate(slots):
        entries = range(slot * cap, (slot + 1) * cap)
        both = held[i * cap * TILE : (i + 1) * cap * TILE, :].astype(jnp.float32)
        both = both.T.astype(jnp.bfloat16)
        terms[i][:rank, :] = dot(both[rank:], slot_rows(act, tile, entries)).astype(jnp.bfloat16)
        terms[i][rank:, :] = dot(both[:rank], slot_rows(cot, tile, entries)).astype(jnp.bfloat16)


def weight_columns(weight, place):
    features = weight.shape[0]
    return weight[:, pl.ds(pl.multiple_of(place * features, 128), features)]


def near_kernel(count, place, own, pair, weight, *refs):
    out, *parts = refs[-count:]
    start = own.shape[0] - sum(part.shape[0] for part in parts)
    for part in parts:
        part[...] = own[start : start + part.shape[0], :]
        start += part.shape[0]
    out[...] = dot(own[...], weight_columns(weight, place[0]), NT)
    out[...] += dot(pair[...], weight_columns(weight, place[1]), NT)


def row_sums(start, count, place, near, term, weight, blocks, out, done, sem):
    at = 0
    for first in range(0, len(blocks), count):
        extent = blocks[first].shape[0]
        rows = slice(start + at, start + at + extent)
        total = near[rows, :] + term[rows, :].astype(jnp.float32)
        for i in range(count):
            total += dot(blocks[first + i][...], weight_columns(weight, place[2 + i]), NT)
        done[at : at + extent, :] = total.astype(jnp.bfloat16)
        at += extent
    copy = pltpu.make_async_copy(done, out.at[pl.ds(start, at), :], sem)
    copy.start()
    copy.wait()


def middle_kernel(groups, cap, count, tile, place, *refs):
    n = sum(len(g) for g in groups)
    blocks, refs = refs[: 3 * count], refs[3 * count :]
    sums, refs = refs[: len(groups)], refs[len(groups) :]
    packs, (near, weight), refs = refs[:n], refs[n : n + 2], refs[n + 2 :]
    out, term, done, sem = refs[-4:]
    term[...] = jnp.zeros_like(term)
    for g, slots in enumerate(groups):
        for i, slot in enumerate(slots):
            maps = packs[slot][...]
            rank = maps.shape[0] // 2
            maps = jnp.concatenate([jnp.zeros_like(maps[:rank]), maps[:rank]], axis=0)
            found = dot(sums[g][i * cap * TILE : (i + 1) * cap * TILE, :], maps)
            for c in range(cap):
                rows = tile_rows(tile[slot * cap + c])
                before = term[rows, :].astype(jnp.float32)
                term[rows, :] = (before + found[c * TILE : (c + 1) * TILE]).astype(term.dtype)
    row_sums(0, count, place, near, term, weight, blocks, out, done, sem)


def far_kernel(count, start, place, near, term, weight, *refs):
    out, token, done, sem = refs[-4:]
    token[...] = jnp.zeros_like(token)
    row_sums(start, count, place, near, term, weight, refs[:count], out, done, sem)


def final_kernel(count, scale, *refs):
    down, up = refs[-2:]
    rank = down.shape[0]
    for out, rows in ((down, slice(0, rank)), (up, slice(rank, 2 * rank))):
        total = refs[0][rows, :].astype(jnp.float32)
        for x in refs[1:count]:
            total += x[rows, :].astype(jnp.float32)
        out[...] = (total * scale).astype(out.dtype)


def on_device(
    activations,
    cotangent,
    frozen_weight,
    adapter_down_maps,
    adapter_up_maps,
    adapter_per_tile,
    live_per_tile,
    adapter_stored_row,
):
    rows, features = activations.shape
    tiles = rows // TILE
    stored, _, rank = adapter_down_maps.shape
    n = lax.axis_size("adapter")
    tensors = lax.axis_size("tensor")
    subs = lax.axis_size("sub")
    me = lax.axis_index("adapter")
    t_me, s_me = lax.axis_index("tensor"), lax.axis_index("sub")
    extents = [rows * c // sum(CHUNKS) for c in CHUNKS]
    starts = [sum(extents[:c]) for c in range(len(extents))]
    bf16, f32 = jnp.bfloat16, jnp.float32

    cap = -(-tiles // n)
    places = [t_me * subs + s_me, t_me * subs + (1 - s_me)]
    for s in (s_me, 1 - s_me):
        places += [jnp.remainder(t_me - k, tensors) * subs + s for k in range(1, tensors)]
    place = jnp.stack(places).astype(jnp.int32)

    groups = [[k for k in range(n) if 1 <= min(k, n - k) <= n // 4]]
    groups.append([k for k in range(n) if k not in groups[0]])

    down = jnp.swapaxes(adapter_down_maps, 1, 2).reshape(stored * rank, features)
    up = adapter_up_maps.reshape(stored * rank, features)
    pack_shape = jax.ShapeDtypeStruct((2 * rank, features), bf16)
    *parts, pack, pack_again = call(
        head_kernel,
        mib=56,
        in_specs=[ANY] * 3,
        out_specs=[ANY] * (FIRST + 2),
        out_shape=[jax.ShapeDtypeStruct((e, features), bf16) for e in extents[:FIRST]]
        + [pack_shape] * 2,
        scratch_shapes=[
            pltpu.VMEM((starts[FIRST], features), bf16),
            pltpu.VMEM(pack_shape.shape, bf16),
            pltpu.SemaphoreType.DMA((3, FIRST + 2)),
        ],
    )(cotangent, down, up)
    def across(part, aside=0):
        slice_axes, found = ("tensor", "sub"), []
        for k in range(1, tensors):
            to = [(t + k) % tensors * subs + (s + aside) % subs for t in range(tensors) for s in range(subs)]
            found.append(lax.ppermute(part, slice_axes, list(enumerate(to))))
        return found

    def forward(blocks):
        return [shift(x, "sub", subs, 1) for x in blocks]

    direct = [across(part) for part in parts]
    pair = shift(cotangent, "sub", subs, 1)

    def tick(*ready):
        return call(
            tick_kernel,
            flops=HEAVY,
            in_specs=after(ready),
            out_specs=VMEM,
            out_shape=jax.ShapeDtypeStruct((8, 128), f32),
        )(*ready)

    def ranks(g, *wait):
        return call(
            functools.partial(rank_kernel, g, cap),
            in_specs=[SMEM] * 2 + [VMEM] * (2 + len(g)) + after(wait),
            out_specs=VMEM,
            out_shape=jax.ShapeDtypeStruct((len(g) * cap * TILE, 2 * rank), bf16),
        )(tile, live, activations, cotangent, *[packs[k] for k in g], *wait)

    def chip_sum(own, *wait):
        given = shift(own, "sub", subs, 1)
        sent = call(
            functools.partial(sum_kernel, 2, -1),
            in_specs=[VMEM] * 2 + after(wait),
            out_specs=VMEM,
            out_shape=jax.ShapeDtypeStruct(own.shape, bf16),
        )(own, given, *wait)
        return given, sent

    def slice_sum(own, given, others, held_parts, *wait):
        found = [own, given, *others]
        shapes = [jax.ShapeDtypeStruct(x.shape, x.dtype) for x in held_parts]
        return call(
            functools.partial(sum_kernel, len(found), -1 - len(shapes)),
            in_specs=[VMEM] * len(found) + after(held_parts) + after(wait),
            out_specs=[VMEM] + after(held_parts),
            out_shape=[jax.ShapeDtypeStruct(own.shape, bf16)] + shapes,
            input_output_aliases={len(found) + i: 1 + i for i in range(len(shapes))},
        )(*found, *held_parts, *wait)

    def adapter_terms(g, held, *wait):
        found = call(
            functools.partial(terms_kernel, g, cap),
            in_specs=[SMEM] + [VMEM] * 3 + after(wait),
            out_specs=[VMEM] * len(g),
            out_shape=[jax.ShapeDtypeStruct((2 * rank, features), bf16)] * len(g),
        )(tile, held, activations, cotangent, *wait)
        return dict(zip(g, found))

    def after(arrays):
        return [ANY] * len(arrays)

    def gate(blocks, ready):
        found = call(
            gate_kernel,
            in_specs=after(blocks) + [ANY],
            out_specs=after(blocks),
            out_shape=[jax.ShapeDtypeStruct(x.shape, x.dtype) for x in blocks],
            input_output_aliases={i: i for i in range(len(blocks))},
        )(*blocks, ready)
        return list(found)

    table = jax.ShapeDtypeStruct((n * cap,), jnp.int32)
    tile, live = call(
        functools.partial(plan_kernel, n, cap, tiles),
        in_specs=[SMEM] * 4 + [ANY],
        out_specs=[SMEM] * 2,
        out_shape=[table] * 2,
        scratch_shapes=[pltpu.SMEM((n,), jnp.int32)],
    )(adapter_per_tile, live_per_tile, adapter_stored_row, me.astype(jnp.int32).reshape(1), pair)
    (pack_again,) = gate([pack_again], tile)
    later = extents[FIRST:]
    near, *rest = call(
        functools.partial(near_kernel, 1 + len(later)),
        flops=HEAVY,
        in_specs=[SMEM] + [VMEM] * 3 + after(direct[0]) + [ANY],
        out_specs=[VMEM] * (1 + len(later)),
        out_shape=[jax.ShapeDtypeStruct((rows, features), f32)]
        + [jax.ShapeDtypeStruct((e, features), bf16) for e in later],
    )(place, cotangent, pair, frozen_weight, *direct[0], pack_again)
    parts = [*parts, *rest]

    first, second = groups
    packs = {0: pack} | {k: shift(pack, "adapter", n, k) for k in first}
    packs |= {k: shift(pack_again, "adapter", n, k) for k in second if k}

    forwards = [forward(direct[0])]
    own = ranks(first, near)
    given, sent = chip_sum(own, tick(own), *forwards[0])
    mark = tick(sent)
    direct[1] = gate(direct[1], sent)
    forwards.append(forward(direct[1]))
    direct.append(across(*gate([parts[2]], mark)))
    (held,) = slice_sum(own, given, across(sent), [], mark, *forwards[1])
    sums = [held]
    terms = adapter_terms(first, held)
    own = ranks(second, terms[first[0]])
    arrived = {k: shift(terms[k], "adapter", n, -k) for k in first}

    given, sent = chip_sum(own, tick(own))
    mark = tick(sent)
    direct.append(across(*gate([parts[3]], mark)))
    (held,) = slice_sum(own, given, across(sent), [], mark)
    sums.append(held)
    terms |= adapter_terms(second, held)
    arrived |= {k: shift(terms[k], "adapter", n, -k) for k in second if k}
    direct[2] = gate(direct[2], held)
    forwards.append(forward(direct[2]))

    blocks = [x for c in range(3) for x in direct[c] + forwards[c]]
    count = len(blocks) // 3
    operands = [tile, place, *blocks, *sums, *[packs[k] for k in range(n)], near, frozen_weight]
    whole_shape = jax.ShapeDtypeStruct((rows, features), bf16)
    out, term = call(
        functools.partial(middle_kernel, groups, cap, count),
        mib=20,
        flops=HEAVY,
        in_specs=[SMEM] * 2 + [VMEM] * (len(operands) - 2) + [ANY] * 2,
        out_specs=[HBM, VMEM],
        out_shape=[whole_shape] * 2,
        scratch_shapes=[pltpu.VMEM((starts[3], features), bf16), pltpu.SemaphoreType.DMA],
    )(*operands, terms[second[-1]], tick(held))
    direct[3] = gate(direct[3], term)
    forwards.append(forward(direct[3]))
    operands = [place, near, term, frozen_weight, *direct[3], *forwards[3]]
    out, token = call(
        functools.partial(far_kernel, count, starts[3]),
        mib=16,
        in_specs=[SMEM] + [VMEM] * (len(operands) - 1) + [HBM, ANY],
        out_specs=[HBM, VMEM],
        out_shape=[whole_shape, jax.ShapeDtypeStruct((8, 128), f32)],
        scratch_shapes=[pltpu.VMEM((rows - starts[3], features), bf16), pltpu.SemaphoreType.DMA],
        input_output_aliases={len(operands): 0},
    )(*operands, out, tick(held, terms[second[-1]]))
    maps_shape = jax.ShapeDtypeStruct((rank, features), bf16)
    down_grad, up_grad = call(
        functools.partial(final_kernel, n, (stored / rows) ** 0.5),
        in_specs=[VMEM] * n + [ANY],
        out_specs=[VMEM] * 2,
        out_shape=[maps_shape] * 2,
    )(terms[0], *[arrived[k] for k in range(1, n)], token)
    down_grad = jnp.swapaxes(down_grad.reshape(stored, rank, features), 1, 2)
    up_grad = up_grad.reshape(stored, rank, features)
    return (out, down_grad, up_grad)


def solution(mesh):
    return jax.shard_map(
        on_device,
        mesh=mesh,
        in_specs=(
            P(("groups", "adapter"), ("tensor", "sub")),
            P(("groups", "adapter"), ("tensor", "sub")),
            P(("tensor", "sub"), None),
            P(("groups", "adapter"), ("tensor", "sub"), None),
            P(("groups", "adapter"), None, ("tensor", "sub")),
            P("groups"),
            P("groups"),
            P("groups"),
        ),
        out_specs=(
            P(("groups", "adapter"), ("tensor", "sub")),
            P(("groups", "adapter"), ("tensor", "sub"), None),
            P(("groups", "adapter"), None, ("tensor", "sub")),
        ),
        check_vma=False,
    )
```

```python
import functools

import jax
import jax.numpy as jnp
from jax import lax
from jax.experimental import pallas as pl
from jax.experimental.pallas import tpu as pltpu
from jax.sharding import PartitionSpec as P

TILE = 128
HEAVY = 1 << 33
CHUNKS = (3, 4, 4, 5)
FIRST = 2
NT = (((1,), (1,)), ((), ()))
SMEM = pl.BlockSpec(memory_space=pltpu.SMEM)
VMEM = pl.BlockSpec(memory_space=pltpu.VMEM)
ANY = pl.BlockSpec(memory_space=pl.ANY)
HBM = pl.BlockSpec(memory_space=pltpu.HBM)


def shift(array, axis, size, by):
    return lax.ppermute(array, axis, [(i, (i + by) % size) for i in range(size)])


def call(body, mib=12, flops=0, **kwargs):
    params = pltpu.CompilerParams(vmem_limit_bytes=mib * 1024 * 1024)
    cost = pl.CostEstimate(flops=flops, bytes_accessed=0, transcendentals=0)
    name = getattr(body, "func", body).__name__
    return pl.pallas_call(body, compiler_params=params, cost_estimate=cost, name=name, **kwargs)


def dot(a, b, dims=(((1,), (0,)), ((), ()))):
    return lax.dot_general(a, b, dims, preferred_element_type=jnp.float32)


def tile_rows(index):
    return pl.ds(pl.multiple_of(index * TILE, TILE), TILE)


def slot_rows(data, tile, entries):
    return jnp.concatenate([data[tile_rows(tile[e]), :] for e in entries], axis=0)


def copy_all(pairs, sems):
    copies = [pltpu.make_async_copy(a, b, sems.at[i]) for i, (a, b) in enumerate(pairs)]
    for copy in copies:
        copy.start()
    return copies


def head_kernel(cot, down, up, *refs):
    *parts, pack, again, held, pack_held, sems = refs
    rank, rows, start = down.shape[0], [], 0
    for part in parts:
        rows.append(pl.ds(start, part.shape[0]))
        start += part.shape[0]
    pairs = [(cot.at[r, :], held.at[r, :]) for r in rows]
    pairs += [(down, pack_held.at[pl.ds(0, rank), :]), (up, pack_held.at[pl.ds(rank, rank), :])]
    loads = copy_all(pairs, sems.at[0])
    stores = []
    for i, part in enumerate(parts):
        loads[i].wait()
        stores.append(pltpu.make_async_copy(held.at[rows[i], :], part, sems.at[1, i]))
        stores[-1].start()
    for load in loads[-2:]:
        load.wait()
    stores += copy_all([(pack_held, pack), (pack_held, again)], sems.at[2])
    for store in stores:
        store.wait()


def plan_kernel(n, cap, tiles, ids, live_all, stored, me, tile, live, count):
    for k in range(n):
        count[k] = 0
    for e in range(n * cap):
        tile[e] = 0
        live[e] = 0
    for t in range(tiles):
        at = me[0] * tiles + t
        k = lax.rem(me[0] - stored[ids[at]] + n, n)
        e = jnp.minimum(k * cap + count[k], n * cap - 1)
        tile[e] = t
        live[e] = live_all[at]
        count[k] = count[k] + 1


def rank_kernel(slots, cap, tile, live, act, cot, *refs):
    packs, out = refs[: len(slots)], refs[-1]
    width = packs[0].shape[0]
    part = lax.broadcasted_iota(jnp.int32, packs[0].shape, 0) < width // 2
    row = lax.broadcasted_iota(jnp.int32, (TILE, width), 0)
    for i, (slot, pack) in enumerate(zip(slots, packs)):
        entries = range(slot * cap, (slot + 1) * cap)
        maps = pack[...]
        zero = jnp.zeros_like(maps)
        both = dot(slot_rows(act, tile, entries), jnp.where(part, maps, zero), NT)
        both += dot(slot_rows(cot, tile, entries), jnp.where(part, zero, maps), NT)
        for c, e in enumerate(entries):
            at = (i * cap + c) * TILE
            out[at : at + TILE, :] = jnp.where(
                row < live[e], both[c * TILE : (c + 1) * TILE], 0.0
            ).astype(jnp.bfloat16)


def sum_kernel(count, place, *refs):
    total = refs[0][...].astype(jnp.float32)
    for x in refs[1:count]:
        total += x[...].astype(jnp.float32)
    out = refs[place]
    out[...] = total.astype(out.dtype)


def gate_kernel(*refs):
    pass


def tick_kernel(*refs):
    refs[-1][...] = jnp.zeros_like(refs[-1])


def terms_kernel(slots, cap, tile, held, act, cot, *refs):
    terms = refs[-len(slots) :]
    rank = held.shape[1] // 2
    for i, slot in enumerate(slots):
        entries = range(slot * cap, (slot + 1) * cap)
        both = held[i * cap * TILE : (i + 1) * cap * TILE, :].astype(jnp.float32)
        both = both.T.astype(jnp.bfloat16)
        terms[i][:rank, :] = dot(both[rank:], slot_rows(act, tile, entries)).astype(jnp.bfloat16)
        terms[i][rank:, :] = dot(both[:rank], slot_rows(cot, tile, entries)).astype(jnp.bfloat16)


def weight_columns(weight, place):
    features = weight.shape[0]
    return weight[:, pl.ds(pl.multiple_of(place * features, 128), features)]


def near_kernel(count, place, own, pair, weight, *refs):
    out, *parts = refs[-count:]
    start = own.shape[0] - sum(part.shape[0] for part in parts)
    for part in parts:
        part[...] = own[start : start + part.shape[0], :]
        start += part.shape[0]
    out[...] = dot(own[...], weight_columns(weight, place[0]), NT)
    out[...] += dot(pair[...], weight_columns(weight, place[1]), NT)


def row_sums(start, count, place, near, term, weight, blocks, out, done, sem):
    at = 0
    for first in range(0, len(blocks), count):
        extent = blocks[first].shape[0]
        rows = slice(start + at, start + at + extent)
        total = near[rows, :] + term[rows, :].astype(jnp.float32)
        for i in range(count):
            total += dot(blocks[first + i][...], weight_columns(weight, place[2 + i]), NT)
        done[at : at + extent, :] = total.astype(jnp.bfloat16)
        at += extent
    copy = pltpu.make_async_copy(done, out.at[pl.ds(start, at), :], sem)
    copy.start()
    copy.wait()


def middle_kernel(groups, cap, count, tile, place, *refs):
    n = sum(len(g) for g in groups)
    blocks, refs = refs[: 3 * count], refs[3 * count :]
    sums, refs = refs[: len(groups)], refs[len(groups) :]
    packs, (near, weight), refs = refs[:n], refs[n : n + 2], refs[n + 2 :]
    out, term, done, sem = refs[-4:]
    term[...] = jnp.zeros_like(term)
    for g, slots in enumerate(groups):
        for i, slot in enumerate(slots):
            maps = packs[slot][...]
            rank = maps.shape[0] // 2
            maps = jnp.concatenate([jnp.zeros_like(maps[:rank]), maps[:rank]], axis=0)
            found = dot(sums[g][i * cap * TILE : (i + 1) * cap * TILE, :], maps)
            for c in range(cap):
                rows = tile_rows(tile[slot * cap + c])
                before = term[rows, :].astype(jnp.float32)
                term[rows, :] = (before + found[c * TILE : (c + 1) * TILE]).astype(term.dtype)
    row_sums(0, count, place, near, term, weight, blocks, out, done, sem)


def far_kernel(count, start, place, near, term, weight, *refs):
    out, token, done, sem = refs[-4:]
    token[...] = jnp.zeros_like(token)
    row_sums(start, count, place, near, term, weight, refs[:count], out, done, sem)


def final_kernel(count, scale, *refs):
    down, up = refs[-2:]
    rank = down.shape[0]
    for out, rows in ((down, slice(0, rank)), (up, slice(rank, 2 * rank))):
        total = refs[0][rows, :].astype(jnp.float32)
        for x in refs[1:count]:
            total += x[rows, :].astype(jnp.float32)
        out[...] = (total * scale).astype(out.dtype)


def on_device(
    activations,
    cotangent,
    frozen_weight,
    adapter_down_maps,
    adapter_up_maps,
    adapter_per_tile,
    live_per_tile,
    adapter_stored_row,
):
    rows, features = activations.shape
    tiles = rows // TILE
    stored, _, rank = adapter_down_maps.shape
    n = lax.axis_size("adapter")
    tensors = lax.axis_size("tensor")
    subs = lax.axis_size("sub")
    me = lax.axis_index("adapter")
    t_me, s_me = lax.axis_index("tensor"), lax.axis_index("sub")
    extents = [rows * c // sum(CHUNKS) for c in CHUNKS]
    starts = [sum(extents[:c]) for c in range(len(extents))]
    bf16, f32 = jnp.bfloat16, jnp.float32

    cap = -(-tiles // n)
    places = [t_me * subs + s_me, t_me * subs + (1 - s_me)]
    for s in (s_me, 1 - s_me):
        places += [jnp.remainder(t_me - k, tensors) * subs + s for k in range(1, tensors)]
    place = jnp.stack(places).astype(jnp.int32)

    groups = [[k for k in range(n) if 1 <= min(k, n - k) <= n // 4]]
    groups.append([k for k in range(n) if k not in groups[0]])

    down = jnp.swapaxes(adapter_down_maps, 1, 2).reshape(stored * rank, features)
    up = adapter_up_maps.reshape(stored * rank, features)
    pack_shape = jax.ShapeDtypeStruct((2 * rank, features), bf16)
    *parts, pack, pack_again = call(
        head_kernel,
        mib=56,
        in_specs=[ANY] * 3,
        out_specs=[ANY] * (FIRST + 2),
        out_shape=[jax.ShapeDtypeStruct((e, features), bf16) for e in extents[:FIRST]]
        + [pack_shape] * 2,
        scratch_shapes=[
            pltpu.VMEM((starts[FIRST], features), bf16),
            pltpu.VMEM(pack_shape.shape, bf16),
            pltpu.SemaphoreType.DMA((3, FIRST + 2)),
        ],
    )(cotangent, down, up)
    def across(part, aside=0):
        slice_axes, found = ("tensor", "sub"), []
        for k in range(1, tensors):
            to = [(t + k) % tensors * subs + (s + aside) % subs for t in range(tensors) for s in range(subs)]
            found.append(lax.ppermute(part, slice_axes, list(enumerate(to))))
        return found

    def forward(blocks):
        return [shift(x, "sub", subs, 1) for x in blocks]

    direct = [across(part) for part in parts]
    pair = shift(cotangent, "sub", subs, 1)
    table = jax.ShapeDtypeStruct((n * cap,), jnp.int32)
    tile, live = call(
        functools.partial(plan_kernel, n, cap, tiles),
        in_specs=[SMEM] * 4,
        out_specs=[SMEM] * 2,
        out_shape=[table] * 2,
        scratch_shapes=[pltpu.SMEM((n,), jnp.int32)],
    )(adapter_per_tile, live_per_tile, adapter_stored_row, me.astype(jnp.int32).reshape(1))

    def after(arrays):
        return [ANY] * len(arrays)

    def gate(blocks, ready):
        found = call(
            gate_kernel,
            in_specs=after(blocks) + [ANY],
            out_specs=after(blocks),
            out_shape=[jax.ShapeDtypeStruct(x.shape, x.dtype) for x in blocks],
            input_output_aliases={i: i for i in range(len(blocks))},
        )(*blocks, ready)
        return list(found)

    def tick(*ready):
        return call(
            tick_kernel,
            flops=HEAVY,
            in_specs=after(ready),
            out_specs=VMEM,
            out_shape=jax.ShapeDtypeStruct((8, 128), f32),
        )(*ready)

    def ranks(g, *wait):
        return call(
            functools.partial(rank_kernel, g, cap),
            in_specs=[SMEM] * 2 + [VMEM] * (2 + len(g)) + after(wait),
            out_specs=VMEM,
            out_shape=jax.ShapeDtypeStruct((len(g) * cap * TILE, 2 * rank), bf16),
        )(tile, live, activations, cotangent, *[packs[k] for k in g], *wait)

    def chip_sum(own, *wait):
        given = shift(own, "sub", subs, 1)
        sent = call(
            functools.partial(sum_kernel, 2, -1),
            in_specs=[VMEM] * 2 + after(wait),
            out_specs=VMEM,
            out_shape=jax.ShapeDtypeStruct(own.shape, bf16),
        )(own, given, *wait)
        return given, sent

    def slice_sum(own, given, others, held_parts, *wait):
        found = [own, given, *others]
        shapes = [jax.ShapeDtypeStruct(x.shape, x.dtype) for x in held_parts]
        return call(
            functools.partial(sum_kernel, len(found), -1 - len(shapes)),
            in_specs=[VMEM] * len(found) + after(held_parts) + after(wait),
            out_specs=[VMEM] + after(held_parts),
            out_shape=[jax.ShapeDtypeStruct(own.shape, bf16)] + shapes,
            input_output_aliases={len(found) + i: 1 + i for i in range(len(shapes))},
        )(*found, *held_parts, *wait)

    def adapter_terms(g, held, *wait):
        found = call(
            functools.partial(terms_kernel, g, cap),
            in_specs=[SMEM] + [VMEM] * 3 + after(wait),
            out_specs=[VMEM] * len(g),
            out_shape=[jax.ShapeDtypeStruct((2 * rank, features), bf16)] * len(g),
        )(tile, held, activations, cotangent, *wait)
        return dict(zip(g, found))

    later = extents[FIRST:]
    near, *rest = call(
        functools.partial(near_kernel, 1 + len(later)),
        flops=HEAVY,
        in_specs=[SMEM] + [VMEM] * 3 + after(direct[0]),
        out_specs=[VMEM] * (1 + len(later)),
        out_shape=[jax.ShapeDtypeStruct((rows, features), f32)]
        + [jax.ShapeDtypeStruct((e, features), bf16) for e in later],
    )(place, cotangent, pair, frozen_weight, *direct[0])
    parts = [*parts, *rest]

    first, second = groups
    packs = {0: pack} | {k: shift(pack, "adapter", n, k) for k in first}
    (pack_again,) = gate([pack_again], tile)
    packs |= {k: shift(pack_again, "adapter", n, k) for k in second if k}

    forwards = [forward(direct[0])]
    own = ranks(first, near)
    given, sent = chip_sum(own, tick(own), *forwards[0])
    mark = tick(sent)
    direct[1] = gate(direct[1], sent)
    forwards.append(forward(direct[1]))
    direct.append(across(*gate([parts[2]], mark)))
    (held,) = slice_sum(own, given, across(sent), [], mark, *forwards[1])
    sums = [held]
    own = ranks(second, held)
    terms = adapter_terms(first, held, own)
    given, sent = chip_sum(own, tick(own), terms[first[0]])
    mark = tick(sent)
    leaving = gate([terms[k] for k in first], mark)
    arrived = {k: shift(x, "adapter", n, -k) for k, x in zip(first, leaving)}
    direct.append(across(*gate([parts[3]], mark)))
    (held,) = slice_sum(own, given, across(sent), [], mark)
    sums.append(held)
    terms |= adapter_terms(second, held)
    arrived |= {k: shift(terms[k], "adapter", n, -k) for k in second if k}
    direct[2] = gate(direct[2], held)
    forwards.append(forward(direct[2]))

    blocks = [x for c in range(3) for x in direct[c] + forwards[c]]
    count = len(blocks) // 3
    operands = [tile, place, *blocks, *sums, *[packs[k] for k in range(n)], near, frozen_weight]
    whole_shape = jax.ShapeDtypeStruct((rows, features), bf16)
    out, term = call(
        functools.partial(middle_kernel, groups, cap, count),
        mib=20,
        flops=HEAVY,
        in_specs=[SMEM] * 2 + [VMEM] * (len(operands) - 2) + [ANY] * 2,
        out_specs=[HBM, VMEM],
        out_shape=[whole_shape] * 2,
        scratch_shapes=[pltpu.VMEM((starts[3], features), bf16), pltpu.SemaphoreType.DMA],
    )(*operands, terms[second[-1]], tick(held))
    direct[3] = gate(direct[3], term)
    forwards.append(forward(direct[3]))
    operands = [place, near, term, frozen_weight, *direct[3], *forwards[3]]
    out, token = call(
        functools.partial(far_kernel, count, starts[3]),
        mib=16,
        in_specs=[SMEM] + [VMEM] * (len(operands) - 1) + [HBM, ANY],
        out_specs=[HBM, VMEM],
        out_shape=[whole_shape, jax.ShapeDtypeStruct((8, 128), f32)],
        scratch_shapes=[pltpu.VMEM((rows - starts[3], features), bf16), pltpu.SemaphoreType.DMA],
        input_output_aliases={len(operands): 0},
    )(*operands, out, tick(held, terms[second[-1]]))
    maps_shape = jax.ShapeDtypeStruct((rank, features), bf16)
    down_grad, up_grad = call(
        functools.partial(final_kernel, n, (stored / rows) ** 0.5),
        in_specs=[VMEM] * n + [ANY],
        out_specs=[VMEM] * 2,
        out_shape=[maps_shape] * 2,
    )(terms[0], *[arrived[k] for k in range(1, n)], token)
    down_grad = jnp.swapaxes(down_grad.reshape(stored, rank, features), 1, 2)
    up_grad = up_grad.reshape(stored, rank, features)
    return (out, down_grad, up_grad)


def solution(mesh):
    return jax.shard_map(
        on_device,
        mesh=mesh,
        in_specs=(
            P(("groups", "adapter"), ("tensor", "sub")),
            P(("groups", "adapter"), ("tensor", "sub")),
            P(("tensor", "sub"), None),
            P(("groups", "adapter"), ("tensor", "sub"), None),
            P(("groups", "adapter"), None, ("tensor", "sub")),
            P("groups"),
            P("groups"),
            P("groups"),
        ),
        out_specs=(
            P(("groups", "adapter"), ("tensor", "sub")),
            P(("groups", "adapter"), ("tensor", "sub"), None),
            P(("groups", "adapter"), None, ("tensor", "sub")),
        ),
        check_vma=False,
    )
```

```python
import functools

import jax
import jax.numpy as jnp
from jax import lax
from jax.experimental import pallas as pl
from jax.experimental.pallas import tpu as pltpu
from jax.sharding import PartitionSpec as P

TILE = 128
HEAVY = 1 << 33
CHUNKS = (3, 5, 4, 4)
FIRST = 2
NT = (((1,), (1,)), ((), ()))
SMEM = pl.BlockSpec(memory_space=pltpu.SMEM)
VMEM = pl.BlockSpec(memory_space=pltpu.VMEM)
ANY = pl.BlockSpec(memory_space=pl.ANY)
HBM = pl.BlockSpec(memory_space=pltpu.HBM)


def shift(array, axis, size, by):
    return lax.ppermute(array, axis, [(i, (i + by) % size) for i in range(size)])


def call(body, mib=12, flops=0, **kwargs):
    params = pltpu.CompilerParams(vmem_limit_bytes=mib * 1024 * 1024)
    cost = pl.CostEstimate(flops=flops, bytes_accessed=0, transcendentals=0)
    name = getattr(body, "func", body).__name__
    return pl.pallas_call(body, compiler_params=params, cost_estimate=cost, name=name, **kwargs)


def dot(a, b, dims=(((1,), (0,)), ((), ()))):
    return lax.dot_general(a, b, dims, preferred_element_type=jnp.float32)


def tile_rows(index):
    return pl.ds(pl.multiple_of(index * TILE, TILE), TILE)


def slot_rows(data, tile, entries):
    return jnp.concatenate([data[tile_rows(tile[e]), :] for e in entries], axis=0)


def copy_all(pairs, sems):
    copies = [pltpu.make_async_copy(a, b, sems.at[i]) for i, (a, b) in enumerate(pairs)]
    for copy in copies:
        copy.start()
    return copies


def head_kernel(cot, down, up, *refs):
    *parts, pack, again, held, pack_held, sems = refs
    rank, rows, start = down.shape[0], [], 0
    for part in parts:
        rows.append(pl.ds(start, part.shape[0]))
        start += part.shape[0]
    pairs = [(cot.at[r, :], held.at[r, :]) for r in rows]
    pairs += [(down, pack_held.at[pl.ds(0, rank), :]), (up, pack_held.at[pl.ds(rank, rank), :])]
    loads = copy_all(pairs, sems.at[0])
    stores = []
    for i, part in enumerate(parts):
        loads[i].wait()
        stores.append(pltpu.make_async_copy(held.at[rows[i], :], part, sems.at[1, i]))
        stores[-1].start()
    for load in loads[-2:]:
        load.wait()
    stores += copy_all([(pack_held, pack), (pack_held, again)], sems.at[2])
    for store in stores:
        store.wait()


def plan_kernel(n, cap, tiles, ids, live_all, stored, me, own, tile, live, *refs):
    *parts, count = refs
    start = own.shape[0] - sum(part.shape[0] for part in parts)
    for part in parts:
        part[...] = own[start : start + part.shape[0], :]
        start += part.shape[0]
    for k in range(n):
        count[k] = 0
    for e in range(n * cap):
        tile[e] = 0
        live[e] = 0
    for t in range(tiles):
        at = me[0] * tiles + t
        k = lax.rem(me[0] - stored[ids[at]] + n, n)
        e = jnp.minimum(k * cap + count[k], n * cap - 1)
        tile[e] = t
        live[e] = live_all[at]
        count[k] = count[k] + 1


def rank_kernel(slots, cap, tile, live, act, cot, *refs):
    packs, out = refs[: len(slots)], refs[-1]
    width = packs[0].shape[0]
    part = lax.broadcasted_iota(jnp.int32, packs[0].shape, 0) < width // 2
    row = lax.broadcasted_iota(jnp.int32, (TILE, width), 0)
    for i, (slot, pack) in enumerate(zip(slots, packs)):
        entries = range(slot * cap, (slot + 1) * cap)
        maps = pack[...]
        zero = jnp.zeros_like(maps)
        both = dot(slot_rows(act, tile, entries), jnp.where(part, maps, zero), NT)
        both += dot(slot_rows(cot, tile, entries), jnp.where(part, zero, maps), NT)
        for c, e in enumerate(entries):
            at = (i * cap + c) * TILE
            out[at : at + TILE, :] = jnp.where(
                row < live[e], both[c * TILE : (c + 1) * TILE], 0.0
            ).astype(jnp.bfloat16)


def sum_kernel(count, place, *refs):
    total = refs[0][...].astype(jnp.float32)
    for x in refs[1:count]:
        total += x[...].astype(jnp.float32)
    out = refs[place]
    out[...] = total.astype(out.dtype)


def gate_kernel(*refs):
    pass


def tick_kernel(*refs):
    refs[-1][...] = jnp.zeros_like(refs[-1])


def terms_kernel(slots, cap, tile, held, act, cot, *refs):
    terms = refs[-len(slots) :]
    rank = held.shape[1] // 2
    for i, slot in enumerate(slots):
        entries = range(slot * cap, (slot + 1) * cap)
        both = held[i * cap * TILE : (i + 1) * cap * TILE, :].astype(jnp.float32)
        both = both.T.astype(jnp.bfloat16)
        terms[i][:rank, :] = dot(both[rank:], slot_rows(act, tile, entries)).astype(jnp.bfloat16)
        terms[i][rank:, :] = dot(both[:rank], slot_rows(cot, tile, entries)).astype(jnp.bfloat16)


def weight_columns(weight, place):
    features = weight.shape[0]
    return weight[:, pl.ds(pl.multiple_of(place * features, 128), features)]


def near_kernel(place, own, pair, weight, _, out):
    out[...] = dot(own[...], weight_columns(weight, place[0]), NT)
    out[...] += dot(pair[...], weight_columns(weight, place[1]), NT)


def row_sums(start, count, place, near, term, weight, blocks, out, done, sem):
    at = 0
    for first in range(0, len(blocks), count):
        extent = blocks[first].shape[0]
        rows = slice(start + at, start + at + extent)
        total = near[rows, :] + term[rows, :].astype(jnp.float32)
        for i in range(count):
            total += dot(blocks[first + i][...], weight_columns(weight, place[2 + i]), NT)
        done[at : at + extent, :] = total.astype(jnp.bfloat16)
        at += extent
    copy = pltpu.make_async_copy(done, out.at[pl.ds(start, at), :], sem)
    copy.start()
    copy.wait()


def middle_kernel(groups, cap, count, tile, place, *refs):
    n = sum(len(g) for g in groups)
    blocks, refs = refs[: 3 * count], refs[3 * count :]
    sums, refs = refs[: len(groups)], refs[len(groups) :]
    packs, (near, weight), refs = refs[:n], refs[n : n + 2], refs[n + 2 :]
    out, term, done, sem = refs[-4:]
    term[...] = jnp.zeros_like(term)
    for g, slots in enumerate(groups):
        for i, slot in enumerate(slots):
            maps = packs[slot][...]
            rank = maps.shape[0] // 2
            maps = jnp.concatenate([jnp.zeros_like(maps[:rank]), maps[:rank]], axis=0)
            found = dot(sums[g][i * cap * TILE : (i + 1) * cap * TILE, :], maps)
            for c in range(cap):
                rows = tile_rows(tile[slot * cap + c])
                before = term[rows, :].astype(jnp.float32)
                term[rows, :] = (before + found[c * TILE : (c + 1) * TILE]).astype(term.dtype)
    row_sums(0, count, place, near, term, weight, blocks, out, done, sem)


def far_kernel(count, start, place, near, term, weight, *refs):
    out, token, done, sem = refs[-4:]
    token[...] = jnp.zeros_like(token)
    row_sums(start, count, place, near, term, weight, refs[:count], out, done, sem)


def final_kernel(count, scale, *refs):
    down, up = refs[-2:]
    rank = down.shape[0]
    for out, rows in ((down, slice(0, rank)), (up, slice(rank, 2 * rank))):
        total = refs[0][rows, :].astype(jnp.float32)
        for x in refs[1:count]:
            total += x[rows, :].astype(jnp.float32)
        out[...] = (total * scale).astype(out.dtype)


def on_device(
    activations,
    cotangent,
    frozen_weight,
    adapter_down_maps,
    adapter_up_maps,
    adapter_per_tile,
    live_per_tile,
    adapter_stored_row,
):
    rows, features = activations.shape
    tiles = rows // TILE
    stored, _, rank = adapter_down_maps.shape
    n = lax.axis_size("adapter")
    tensors = lax.axis_size("tensor")
    subs = lax.axis_size("sub")
    me = lax.axis_index("adapter")
    t_me, s_me = lax.axis_index("tensor"), lax.axis_index("sub")
    extents = [rows * c // sum(CHUNKS) for c in CHUNKS]
    starts = [sum(extents[:c]) for c in range(len(extents))]
    bf16, f32 = jnp.bfloat16, jnp.float32

    cap = -(-tiles // n)
    places = [t_me * subs + s_me, t_me * subs + (1 - s_me)]
    for s in (s_me, 1 - s_me):
        places += [jnp.remainder(t_me - k, tensors) * subs + s for k in range(1, tensors)]
    place = jnp.stack(places).astype(jnp.int32)

    groups = [[k for k in range(n) if 1 <= min(k, n - k) <= n // 4]]
    groups.append([k for k in range(n) if k not in groups[0]])

    down = jnp.swapaxes(adapter_down_maps, 1, 2).reshape(stored * rank, features)
    up = adapter_up_maps.reshape(stored * rank, features)
    pack_shape = jax.ShapeDtypeStruct((2 * rank, features), bf16)
    *parts, pack, pack_again = call(
        head_kernel,
        mib=56,
        in_specs=[ANY] * 3,
        out_specs=[ANY] * (FIRST + 2),
        out_shape=[jax.ShapeDtypeStruct((e, features), bf16) for e in extents[:FIRST]]
        + [pack_shape] * 2,
        scratch_shapes=[
            pltpu.VMEM((starts[FIRST], features), bf16),
            pltpu.VMEM(pack_shape.shape, bf16),
            pltpu.SemaphoreType.DMA((3, FIRST + 2)),
        ],
    )(cotangent, down, up)
    def across(part, aside=0):
        slice_axes, found = ("tensor", "sub"), []
        for k in range(1, tensors):
            to = [(t + k) % tensors * subs + (s + aside) % subs for t in range(tensors) for s in range(subs)]
            found.append(lax.ppermute(part, slice_axes, list(enumerate(to))))
        return found

    def forward(blocks):
        return [shift(x, "sub", subs, 1) for x in blocks]

    direct = [across(part) for part in parts]
    pair = shift(cotangent, "sub", subs, 1)
    table = jax.ShapeDtypeStruct((n * cap,), jnp.int32)
    later = [jax.ShapeDtypeStruct((e, features), bf16) for e in extents[FIRST:]]
    tile, live, *rest = call(
        functools.partial(plan_kernel, n, cap, tiles),
        in_specs=[SMEM] * 4 + [VMEM],
        out_specs=[SMEM] * 2 + [VMEM] * len(later),
        out_shape=[table] * 2 + later,
        scratch_shapes=[pltpu.SMEM((n,), jnp.int32)],
    )(adapter_per_tile, live_per_tile, adapter_stored_row, me.astype(jnp.int32).reshape(1), cotangent)
    parts = [*parts, *rest]

    def after(arrays):
        return [ANY] * len(arrays)

    def gate(blocks, ready):
        found = call(
            gate_kernel,
            in_specs=after(blocks) + [ANY],
            out_specs=after(blocks),
            out_shape=[jax.ShapeDtypeStruct(x.shape, x.dtype) for x in blocks],
            input_output_aliases={i: i for i in range(len(blocks))},
        )(*blocks, ready)
        return list(found)

    def tick(*ready):
        return call(
            tick_kernel,
            flops=HEAVY,
            in_specs=after(ready),
            out_specs=VMEM,
            out_shape=jax.ShapeDtypeStruct((8, 128), f32),
        )(*ready)

    def ranks(g, *wait):
        return call(
            functools.partial(rank_kernel, g, cap),
            in_specs=[SMEM] * 2 + [VMEM] * (2 + len(g)) + after(wait),
            out_specs=VMEM,
            out_shape=jax.ShapeDtypeStruct((len(g) * cap * TILE, 2 * rank), bf16),
        )(tile, live, activations, cotangent, *[packs[k] for k in g], *wait)

    def chip_sum(own, *wait):
        given = shift(own, "sub", subs, 1)
        sent = call(
            functools.partial(sum_kernel, 2, -1),
            in_specs=[VMEM] * 2 + after(wait),
            out_specs=VMEM,
            out_shape=jax.ShapeDtypeStruct(own.shape, bf16),
        )(own, given, *wait)
        return given, sent

    def slice_sum(own, given, others, held_parts, *wait):
        found = [own, given, *others]
        shapes = [jax.ShapeDtypeStruct(x.shape, x.dtype) for x in held_parts]
        return call(
            functools.partial(sum_kernel, len(found), -1 - len(shapes)),
            in_specs=[VMEM] * len(found) + after(held_parts) + after(wait),
            out_specs=[VMEM] + after(held_parts),
            out_shape=[jax.ShapeDtypeStruct(own.shape, bf16)] + shapes,
            input_output_aliases={len(found) + i: 1 + i for i in range(len(shapes))},
        )(*found, *held_parts, *wait)

    def adapter_terms(g, held, *wait):
        found = call(
            functools.partial(terms_kernel, g, cap),
            in_specs=[SMEM] + [VMEM] * 3 + after(wait),
            out_specs=[VMEM] * len(g),
            out_shape=[jax.ShapeDtypeStruct((2 * rank, features), bf16)] * len(g),
        )(tile, held, activations, cotangent, *wait)
        return dict(zip(g, found))

    first, second = groups
    packs = {0: pack} | {k: shift(pack, "adapter", n, k) for k in first}
    (pack_again,) = gate([pack_again], tile)
    packs |= {k: shift(pack_again, "adapter", n, k) for k in second if k}

    forwards = [forward(direct[0])]
    own = ranks(first, tick(*direct[0], pair))
    given, sent = chip_sum(own, tick(own), *forwards[0])
    mark = tick(sent)
    direct[1] = gate(direct[1], sent)
    forwards.append(forward(direct[1]))
    direct.append(across(*gate([parts[2]], mark)))
    (held,) = slice_sum(own, given, across(sent), [], mark, *forwards[1])
    sums = [held]
    own = ranks(second, held)
    terms = adapter_terms(first, held, own)
    given, sent = chip_sum(own, tick(own), terms[first[0]])
    mark = tick(sent)
    leaving = gate([terms[k] for k in first], mark)
    arrived = {k: shift(x, "adapter", n, -k) for k, x in zip(first, leaving)}
    direct.append(across(*gate([parts[3]], mark)))
    (held,) = slice_sum(own, given, across(sent), [], mark)
    sums.append(held)
    terms |= adapter_terms(second, held)
    arrived |= {k: shift(terms[k], "adapter", n, -k) for k in second if k}
    direct[2] = gate(direct[2], held)
    forwards.append(forward(direct[2]))

    near = call(
        near_kernel,
        flops=HEAVY,
        in_specs=[SMEM] + [VMEM] * 3 + [ANY],
        out_specs=VMEM,
        out_shape=jax.ShapeDtypeStruct((rows, features), f32),
    )(place, cotangent, pair, frozen_weight, terms[second[-1]])
    blocks = [x for c in range(3) for x in direct[c] + forwards[c]]
    count = len(blocks) // 3
    operands = [tile, place, *blocks, *sums, *[packs[k] for k in range(n)], near, frozen_weight]
    whole_shape = jax.ShapeDtypeStruct((rows, features), bf16)
    out, term = call(
        functools.partial(middle_kernel, groups, cap, count),
        mib=20,
        flops=HEAVY,
        in_specs=[SMEM] * 2 + [VMEM] * (len(operands) - 2) + [ANY] * 2,
        out_specs=[HBM, VMEM],
        out_shape=[whole_shape] * 2,
        scratch_shapes=[pltpu.VMEM((starts[3], features), bf16), pltpu.SemaphoreType.DMA],
    )(*operands, terms[second[-1]], tick(held))
    direct[3] = gate(direct[3], term)
    forwards.append(forward(direct[3]))
    operands = [place, near, term, frozen_weight, *direct[3], *forwards[3]]
    out, token = call(
        functools.partial(far_kernel, count, starts[3]),
        mib=16,
        in_specs=[SMEM] + [VMEM] * (len(operands) - 1) + [HBM, ANY],
        out_specs=[HBM, VMEM],
        out_shape=[whole_shape, jax.ShapeDtypeStruct((8, 128), f32)],
        scratch_shapes=[pltpu.VMEM((rows - starts[3], features), bf16), pltpu.SemaphoreType.DMA],
        input_output_aliases={len(operands): 0},
    )(*operands, out, tick(held, terms[second[-1]]))
    maps_shape = jax.ShapeDtypeStruct((rank, features), bf16)
    down_grad, up_grad = call(
        functools.partial(final_kernel, n, (stored / rows) ** 0.5),
        in_specs=[VMEM] * n + [ANY],
        out_specs=[VMEM] * 2,
        out_shape=[maps_shape] * 2,
    )(terms[0], *[arrived[k] for k in range(1, n)], token)
    down_grad = jnp.swapaxes(down_grad.reshape(stored, rank, features), 1, 2)
    up_grad = up_grad.reshape(stored, rank, features)
    return (out, down_grad, up_grad)


def solution(mesh):
    return jax.shard_map(
        on_device,
        mesh=mesh,
        in_specs=(
            P(("groups", "adapter"), ("tensor", "sub")),
            P(("groups", "adapter"), ("tensor", "sub")),
            P(("tensor", "sub"), None),
            P(("groups", "adapter"), ("tensor", "sub"), None),
            P(("groups", "adapter"), None, ("tensor", "sub")),
            P("groups"),
            P("groups"),
            P("groups"),
        ),
        out_specs=(
            P(("groups", "adapter"), ("tensor", "sub")),
            P(("groups", "adapter"), ("tensor", "sub"), None),
            P(("groups", "adapter"), None, ("tensor", "sub")),
        ),
        check_vma=False,
    )
```

```python
import functools

import jax
import jax.numpy as jnp
from jax import lax
from jax.experimental import pallas as pl
from jax.experimental.pallas import tpu as pltpu
from jax.sharding import PartitionSpec as P

TILE = 128
HEAVY = 1 << 33
CHUNKS = (3, 5, 4, 4)
FIRST = 2
NT = (((1,), (1,)), ((), ()))
SMEM = pl.BlockSpec(memory_space=pltpu.SMEM)
VMEM = pl.BlockSpec(memory_space=pltpu.VMEM)
ANY = pl.BlockSpec(memory_space=pl.ANY)
HBM = pl.BlockSpec(memory_space=pltpu.HBM)


def shift(array, axis, size, by):
    return lax.ppermute(array, axis, [(i, (i + by) % size) for i in range(size)])


def call(body, mib=12, flops=0, **kwargs):
    params = pltpu.CompilerParams(vmem_limit_bytes=mib * 1024 * 1024)
    cost = pl.CostEstimate(flops=flops, bytes_accessed=0, transcendentals=0)
    name = getattr(body, "func", body).__name__
    return pl.pallas_call(body, compiler_params=params, cost_estimate=cost, name=name, **kwargs)


def dot(a, b, dims=(((1,), (0,)), ((), ()))):
    return lax.dot_general(a, b, dims, preferred_element_type=jnp.float32)


def tile_rows(index):
    return pl.ds(pl.multiple_of(index * TILE, TILE), TILE)


def slot_rows(data, tile, entries):
    return jnp.concatenate([data[tile_rows(tile[e]), :] for e in entries], axis=0)


def copy_all(pairs, sems):
    copies = [pltpu.make_async_copy(a, b, sems.at[i]) for i, (a, b) in enumerate(pairs)]
    for copy in copies:
        copy.start()
    return copies


def head_kernel(cot, down, up, *refs):
    *parts, pack, again, held, pack_held, sems = refs
    rank, rows, start = down.shape[0], [], 0
    for part in parts:
        rows.append(pl.ds(start, part.shape[0]))
        start += part.shape[0]
    pairs = [(cot.at[r, :], held.at[r, :]) for r in rows]
    pairs += [(down, pack_held.at[pl.ds(0, rank), :]), (up, pack_held.at[pl.ds(rank, rank), :])]
    loads = copy_all(pairs, sems.at[0])
    stores = []
    for i, part in enumerate(parts):
        loads[i].wait()
        stores.append(pltpu.make_async_copy(held.at[rows[i], :], part, sems.at[1, i]))
        stores[-1].start()
    for load in loads[-2:]:
        load.wait()
    stores += copy_all([(pack_held, pack), (pack_held, again)], sems.at[2])
    for store in stores:
        store.wait()


def plan_kernel(n, cap, tiles, ids, live_all, stored, me, own, tile, live, *refs):
    *parts, count = refs
    start = own.shape[0] - sum(part.shape[0] for part in parts)
    for part in parts:
        part[...] = own[start : start + part.shape[0], :]
        start += part.shape[0]
    for k in range(n):
        count[k] = 0
    for e in range(n * cap):
        tile[e] = 0
        live[e] = 0
    for t in range(tiles):
        at = me[0] * tiles + t
        k = lax.rem(me[0] - stored[ids[at]] + n, n)
        e = jnp.minimum(k * cap + count[k], n * cap - 1)
        tile[e] = t
        live[e] = live_all[at]
        count[k] = count[k] + 1


def rank_kernel(slots, cap, tile, live, act, cot, *refs):
    packs, out = refs[: len(slots)], refs[-1]
    width = packs[0].shape[0]
    part = lax.broadcasted_iota(jnp.int32, packs[0].shape, 0) < width // 2
    row = lax.broadcasted_iota(jnp.int32, (TILE, width), 0)
    for i, (slot, pack) in enumerate(zip(slots, packs)):
        entries = range(slot * cap, (slot + 1) * cap)
        maps = pack[...]
        zero = jnp.zeros_like(maps)
        both = dot(slot_rows(act, tile, entries), jnp.where(part, maps, zero), NT)
        both += dot(slot_rows(cot, tile, entries), jnp.where(part, zero, maps), NT)
        for c, e in enumerate(entries):
            at = (i * cap + c) * TILE
            out[at : at + TILE, :] = jnp.where(
                row < live[e], both[c * TILE : (c + 1) * TILE], 0.0
            ).astype(jnp.bfloat16)


def sum_kernel(count, place, *refs):
    total = refs[0][...].astype(jnp.float32)
    for x in refs[1:count]:
        total += x[...].astype(jnp.float32)
    out = refs[place]
    out[...] = total.astype(out.dtype)


def gate_kernel(*refs):
    pass


def tick_kernel(*refs):
    refs[-1][...] = jnp.zeros_like(refs[-1])


def terms_kernel(slots, cap, tile, held, act, cot, *refs):
    terms = refs[-len(slots) :]
    rank = held.shape[1] // 2
    for i, slot in enumerate(slots):
        entries = range(slot * cap, (slot + 1) * cap)
        both = held[i * cap * TILE : (i + 1) * cap * TILE, :].astype(jnp.float32)
        both = both.T.astype(jnp.bfloat16)
        terms[i][:rank, :] = dot(both[rank:], slot_rows(act, tile, entries)).astype(jnp.bfloat16)
        terms[i][rank:, :] = dot(both[:rank], slot_rows(cot, tile, entries)).astype(jnp.bfloat16)


def weight_columns(weight, place):
    features = weight.shape[0]
    return weight[:, pl.ds(pl.multiple_of(place * features, 128), features)]


def near_kernel(which, place, data, weight, *refs):
    total = dot(data[...], weight_columns(weight, place[which]), NT)
    refs[-1][...] = total if which == 0 else refs[0][...] + total


def row_sums(start, count, place, near, term, weight, blocks, out, done, sem):
    at = 0
    for first in range(0, len(blocks), count):
        extent = blocks[first].shape[0]
        rows = slice(start + at, start + at + extent)
        total = near[rows, :] + term[rows, :].astype(jnp.float32)
        for i in range(count):
            total += dot(blocks[first + i][...], weight_columns(weight, place[2 + i]), NT)
        done[at : at + extent, :] = total.astype(jnp.bfloat16)
        at += extent
    copy = pltpu.make_async_copy(done, out.at[pl.ds(start, at), :], sem)
    copy.start()
    copy.wait()


def middle_kernel(groups, cap, count, tile, place, *refs):
    n = sum(len(g) for g in groups)
    blocks, refs = refs[: 3 * count], refs[3 * count :]
    sums, refs = refs[: len(groups)], refs[len(groups) :]
    packs, (near, weight), refs = refs[:n], refs[n : n + 2], refs[n + 2 :]
    out, term, done, sem = refs[-4:]
    term[...] = jnp.zeros_like(term)
    for g, slots in enumerate(groups):
        for i, slot in enumerate(slots):
            maps = packs[slot][...]
            rank = maps.shape[0] // 2
            maps = jnp.concatenate([jnp.zeros_like(maps[:rank]), maps[:rank]], axis=0)
            found = dot(sums[g][i * cap * TILE : (i + 1) * cap * TILE, :], maps)
            for c in range(cap):
                rows = tile_rows(tile[slot * cap + c])
                before = term[rows, :].astype(jnp.float32)
                term[rows, :] = (before + found[c * TILE : (c + 1) * TILE]).astype(term.dtype)
    row_sums(0, count, place, near, term, weight, blocks, out, done, sem)


def far_kernel(count, start, place, near, term, weight, *refs):
    out, token, done, sem = refs[-4:]
    token[...] = jnp.zeros_like(token)
    row_sums(start, count, place, near, term, weight, refs[:count], out, done, sem)


def final_kernel(count, scale, *refs):
    down, up = refs[-2:]
    rank = down.shape[0]
    for out, rows in ((down, slice(0, rank)), (up, slice(rank, 2 * rank))):
        total = refs[0][rows, :].astype(jnp.float32)
        for x in refs[1:count]:
            total += x[rows, :].astype(jnp.float32)
        out[...] = (total * scale).astype(out.dtype)


def on_device(
    activations,
    cotangent,
    frozen_weight,
    adapter_down_maps,
    adapter_up_maps,
    adapter_per_tile,
    live_per_tile,
    adapter_stored_row,
):
    rows, features = activations.shape
    tiles = rows // TILE
    stored, _, rank = adapter_down_maps.shape
    n = lax.axis_size("adapter")
    tensors = lax.axis_size("tensor")
    subs = lax.axis_size("sub")
    me = lax.axis_index("adapter")
    t_me, s_me = lax.axis_index("tensor"), lax.axis_index("sub")
    extents = [rows * c // sum(CHUNKS) for c in CHUNKS]
    starts = [sum(extents[:c]) for c in range(len(extents))]
    bf16, f32 = jnp.bfloat16, jnp.float32

    cap = -(-tiles // n)
    places = [t_me * subs + s_me, t_me * subs + (1 - s_me)]
    for s in (s_me, 1 - s_me):
        places += [jnp.remainder(t_me - k, tensors) * subs + s for k in range(1, tensors)]
    place = jnp.stack(places).astype(jnp.int32)

    groups = [[k for k in range(n) if 1 <= min(k, n - k) <= n // 4]]
    groups.append([k for k in range(n) if k not in groups[0]])

    down = jnp.swapaxes(adapter_down_maps, 1, 2).reshape(stored * rank, features)
    up = adapter_up_maps.reshape(stored * rank, features)
    pack_shape = jax.ShapeDtypeStruct((2 * rank, features), bf16)
    *parts, pack, pack_again = call(
        head_kernel,
        mib=56,
        in_specs=[ANY] * 3,
        out_specs=[ANY] * (FIRST + 2),
        out_shape=[jax.ShapeDtypeStruct((e, features), bf16) for e in extents[:FIRST]]
        + [pack_shape] * 2,
        scratch_shapes=[
            pltpu.VMEM((starts[FIRST], features), bf16),
            pltpu.VMEM(pack_shape.shape, bf16),
            pltpu.SemaphoreType.DMA((3, FIRST + 2)),
        ],
    )(cotangent, down, up)
    def across(part, aside=0):
        slice_axes, found = ("tensor", "sub"), []
        for k in range(1, tensors):
            to = [(t + k) % tensors * subs + (s + aside) % subs for t in range(tensors) for s in range(subs)]
            found.append(lax.ppermute(part, slice_axes, list(enumerate(to))))
        return found

    def forward(blocks):
        return [shift(x, "sub", subs, 1) for x in blocks]

    direct = [across(part) for part in parts]
    pair = shift(cotangent, "sub", subs, 1)
    table = jax.ShapeDtypeStruct((n * cap,), jnp.int32)
    later = [jax.ShapeDtypeStruct((e, features), bf16) for e in extents[FIRST:]]
    tile, live, *rest = call(
        functools.partial(plan_kernel, n, cap, tiles),
        in_specs=[SMEM] * 4 + [VMEM],
        out_specs=[SMEM] * 2 + [VMEM] * len(later),
        out_shape=[table] * 2 + later,
        scratch_shapes=[pltpu.SMEM((n,), jnp.int32)],
    )(adapter_per_tile, live_per_tile, adapter_stored_row, me.astype(jnp.int32).reshape(1), cotangent)
    parts = [*parts, *rest]

    def after(arrays):
        return [ANY] * len(arrays)

    def gate(blocks, ready):
        found = call(
            gate_kernel,
            in_specs=after(blocks) + [ANY],
            out_specs=after(blocks),
            out_shape=[jax.ShapeDtypeStruct(x.shape, x.dtype) for x in blocks],
            input_output_aliases={i: i for i in range(len(blocks))},
        )(*blocks, ready)
        return list(found)

    def near_part(which, data, ready, *before):
        return call(
            functools.partial(near_kernel, which),
            flops=HEAVY,
            in_specs=[SMEM] + [VMEM] * (2 + len(before)) + [ANY],
            out_specs=VMEM,
            out_shape=jax.ShapeDtypeStruct((rows, features), f32),
            input_output_aliases={3: 0} if before else {},
        )(place, data, frozen_weight, *before, ready)

    def tick(*ready):
        return call(
            tick_kernel,
            flops=HEAVY,
            in_specs=after(ready),
            out_specs=VMEM,
            out_shape=jax.ShapeDtypeStruct((8, 128), f32),
        )(*ready)

    def ranks(g, *wait):
        return call(
            functools.partial(rank_kernel, g, cap),
            in_specs=[SMEM] * 2 + [VMEM] * (2 + len(g)) + after(wait),
            out_specs=VMEM,
            out_shape=jax.ShapeDtypeStruct((len(g) * cap * TILE, 2 * rank), bf16),
        )(tile, live, activations, cotangent, *[packs[k] for k in g], *wait)

    def chip_sum(own, *wait):
        given = shift(own, "sub", subs, 1)
        sent = call(
            functools.partial(sum_kernel, 2, -1),
            in_specs=[VMEM] * 2 + after(wait),
            out_specs=VMEM,
            out_shape=jax.ShapeDtypeStruct(own.shape, bf16),
        )(own, given, *wait)
        return given, sent

    def slice_sum(own, given, others, held_parts, *wait):
        found = [own, given, *others]
        shapes = [jax.ShapeDtypeStruct(x.shape, x.dtype) for x in held_parts]
        return call(
            functools.partial(sum_kernel, len(found), -1 - len(shapes)),
            in_specs=[VMEM] * len(found) + after(held_parts) + after(wait),
            out_specs=[VMEM] + after(held_parts),
            out_shape=[jax.ShapeDtypeStruct(own.shape, bf16)] + shapes,
            input_output_aliases={len(found) + i: 1 + i for i in range(len(shapes))},
        )(*found, *held_parts, *wait)

    def adapter_terms(g, held, *wait):
        found = call(
            functools.partial(terms_kernel, g, cap),
            in_specs=[SMEM] + [VMEM] * 3 + after(wait),
            out_specs=[VMEM] * len(g),
            out_shape=[jax.ShapeDtypeStruct((2 * rank, features), bf16)] * len(g),
        )(tile, held, activations, cotangent, *wait)
        return dict(zip(g, found))

    first, second = groups
    packs = {0: pack} | {k: shift(pack, "adapter", n, k) for k in first}
    (pack_again,) = gate([pack_again], tile)
    packs |= {k: shift(pack_again, "adapter", n, k) for k in second if k}

    forwards = [forward(direct[0])]
    own = ranks(first, tick(*direct[0], pair))
    given, sent = chip_sum(own, tick(own), *forwards[0])
    mark = tick(sent)
    direct.append(across(*gate([parts[2]], mark)))
    near = near_part(0, cotangent, mark)
    (held,) = slice_sum(own, given, across(sent), [], near)
    direct[1] = gate(direct[1], held)
    forwards.insert(1, forward(direct[1]))
    sums = [held]
    own = ranks(second, held)
    terms = adapter_terms(first, held, own)
    given, sent = chip_sum(own, tick(own), terms[first[0]], *forwards[1])
    mark = tick(sent)
    leaving = gate([terms[k] for k in first], mark)
    arrived = {k: shift(x, "adapter", n, -k) for k, x in zip(first, leaving)}
    direct.append(across(*gate([parts[3]], mark)))
    near = near_part(1, pair, mark, near)
    (held,) = slice_sum(own, given, across(sent), [], near)
    sums.append(held)
    terms |= adapter_terms(second, held)
    arrived |= {k: shift(terms[k], "adapter", n, -k) for k in second if k}
    direct[2] = gate(direct[2], held)
    forwards.append(forward(direct[2]))

    blocks = [x for c in range(3) for x in direct[c] + forwards[c]]
    count = len(blocks) // 3
    operands = [tile, place, *blocks, *sums, *[packs[k] for k in range(n)], near, frozen_weight]
    whole_shape = jax.ShapeDtypeStruct((rows, features), bf16)
    out, term = call(
        functools.partial(middle_kernel, groups, cap, count),
        mib=20,
        flops=HEAVY,
        in_specs=[SMEM] * 2 + [VMEM] * (len(operands) - 2) + [ANY] * 2,
        out_specs=[HBM, VMEM],
        out_shape=[whole_shape] * 2,
        scratch_shapes=[pltpu.VMEM((starts[3], features), bf16), pltpu.SemaphoreType.DMA],
    )(*operands, terms[second[-1]], tick(held))
    direct[3] = gate(direct[3], term)
    forwards.append(forward(direct[3]))
    operands = [place, near, term, frozen_weight, *direct[3], *forwards[3]]
    out, token = call(
        functools.partial(far_kernel, count, starts[3]),
        mib=16,
        in_specs=[SMEM] + [VMEM] * (len(operands) - 1) + [HBM, ANY],
        out_specs=[HBM, VMEM],
        out_shape=[whole_shape, jax.ShapeDtypeStruct((8, 128), f32)],
        scratch_shapes=[pltpu.VMEM((rows - starts[3], features), bf16), pltpu.SemaphoreType.DMA],
        input_output_aliases={len(operands): 0},
    )(*operands, out, tick(held, terms[second[-1]]))
    maps_shape = jax.ShapeDtypeStruct((rank, features), bf16)
    down_grad, up_grad = call(
        functools.partial(final_kernel, n, (stored / rows) ** 0.5),
        in_specs=[VMEM] * n + [ANY],
        out_specs=[VMEM] * 2,
        out_shape=[maps_shape] * 2,
    )(terms[0], *[arrived[k] for k in range(1, n)], token)
    down_grad = jnp.swapaxes(down_grad.reshape(stored, rank, features), 1, 2)
    up_grad = up_grad.reshape(stored, rank, features)
    return (out, down_grad, up_grad)


def solution(mesh):
    return jax.shard_map(
        on_device,
        mesh=mesh,
        in_specs=(
            P(("groups", "adapter"), ("tensor", "sub")),
            P(("groups", "adapter"), ("tensor", "sub")),
            P(("tensor", "sub"), None),
            P(("groups", "adapter"), ("tensor", "sub"), None),
            P(("groups", "adapter"), None, ("tensor", "sub")),
            P("groups"),
            P("groups"),
            P("groups"),
        ),
        out_specs=(
            P(("groups", "adapter"), ("tensor", "sub")),
            P(("groups", "adapter"), ("tensor", "sub"), None),
            P(("groups", "adapter"), None, ("tensor", "sub")),
        ),
        check_vma=False,
    )
```

```python
import functools

import jax
import jax.numpy as jnp
from jax import lax
from jax.experimental import pallas as pl
from jax.experimental.pallas import tpu as pltpu
from jax.sharding import PartitionSpec as P

TILE = 128
HEAVY = 1 << 33
CHUNKS = (6, 5, 5)
FIRST = 1
NT = (((1,), (1,)), ((), ()))
SMEM = pl.BlockSpec(memory_space=pltpu.SMEM)
VMEM = pl.BlockSpec(memory_space=pltpu.VMEM)
ANY = pl.BlockSpec(memory_space=pl.ANY)
HBM = pl.BlockSpec(memory_space=pltpu.HBM)


def shift(array, axis, size, by):
    return lax.ppermute(array, axis, [(i, (i + by) % size) for i in range(size)])


def call(body, mib=12, flops=0, **kwargs):
    params = pltpu.CompilerParams(vmem_limit_bytes=mib * 1024 * 1024)
    cost = pl.CostEstimate(flops=flops, bytes_accessed=0, transcendentals=0)
    name = getattr(body, "func", body).__name__
    return pl.pallas_call(body, compiler_params=params, cost_estimate=cost, name=name, **kwargs)


def dot(a, b, dims=(((1,), (0,)), ((), ()))):
    return lax.dot_general(a, b, dims, preferred_element_type=jnp.float32)


def tile_rows(index):
    return pl.ds(pl.multiple_of(index * TILE, TILE), TILE)


def slot_rows(data, tile, entries):
    return jnp.concatenate([data[tile_rows(tile[e]), :] for e in entries], axis=0)


def copy_all(pairs, sems):
    copies = [pltpu.make_async_copy(a, b, sems.at[i]) for i, (a, b) in enumerate(pairs)]
    for copy in copies:
        copy.start()
    return copies


def head_kernel(cot, down, up, *refs):
    *parts, pack, again, held, pack_held, sems = refs
    rank, rows, start = down.shape[0], [], 0
    for part in parts:
        rows.append(pl.ds(start, part.shape[0]))
        start += part.shape[0]
    pairs = [(cot.at[r, :], held.at[r, :]) for r in rows]
    pairs += [(down, pack_held.at[pl.ds(0, rank), :]), (up, pack_held.at[pl.ds(rank, rank), :])]
    loads = copy_all(pairs, sems.at[0])
    stores = []
    for i, part in enumerate(parts):
        loads[i].wait()
        stores.append(pltpu.make_async_copy(held.at[rows[i], :], part, sems.at[1, i]))
        stores[-1].start()
    for load in loads[-2:]:
        load.wait()
    stores += copy_all([(pack_held, pack), (pack_held, again)], sems.at[2])
    for store in stores:
        store.wait()


def plan_kernel(n, cap, tiles, ids, live_all, stored, me, own, tile, live, *refs):
    *parts, count = refs
    start = own.shape[0] - sum(part.shape[0] for part in parts)
    for part in parts:
        part[...] = own[start : start + part.shape[0], :]
        start += part.shape[0]
    for k in range(n):
        count[k] = 0
    for e in range(n * cap):
        tile[e] = 0
        live[e] = 0
    for t in range(tiles):
        at = me[0] * tiles + t
        k = lax.rem(me[0] - stored[ids[at]] + n, n)
        e = jnp.minimum(k * cap + count[k], n * cap - 1)
        tile[e] = t
        live[e] = live_all[at]
        count[k] = count[k] + 1


def rank_kernel(slots, cap, tile, live, act, cot, *refs):
    packs, out = refs[: len(slots)], refs[-1]
    width = packs[0].shape[0]
    part = lax.broadcasted_iota(jnp.int32, packs[0].shape, 0) < width // 2
    row = lax.broadcasted_iota(jnp.int32, (TILE, width), 0)
    for i, (slot, pack) in enumerate(zip(slots, packs)):
        entries = range(slot * cap, (slot + 1) * cap)
        maps = pack[...]
        zero = jnp.zeros_like(maps)
        both = dot(slot_rows(act, tile, entries), jnp.where(part, maps, zero), NT)
        both += dot(slot_rows(cot, tile, entries), jnp.where(part, zero, maps), NT)
        for c, e in enumerate(entries):
            at = (i * cap + c) * TILE
            out[at : at + TILE, :] = jnp.where(
                row < live[e], both[c * TILE : (c + 1) * TILE], 0.0
            ).astype(jnp.bfloat16)


def sum_kernel(count, place, *refs):
    total = refs[0][...].astype(jnp.float32)
    for x in refs[1:count]:
        total += x[...].astype(jnp.float32)
    out = refs[place]
    out[...] = total.astype(out.dtype)


def gate_kernel(*refs):
    pass


def tick_kernel(*refs):
    refs[-1][...] = jnp.zeros_like(refs[-1])


def terms_kernel(slots, cap, tile, held, act, cot, *refs):
    terms = refs[-len(slots) :]
    rank = held.shape[1] // 2
    for i, slot in enumerate(slots):
        entries = range(slot * cap, (slot + 1) * cap)
        both = held[i * cap * TILE : (i + 1) * cap * TILE, :].astype(jnp.float32)
        both = both.T.astype(jnp.bfloat16)
        terms[i][:rank, :] = dot(both[rank:], slot_rows(act, tile, entries)).astype(jnp.bfloat16)
        terms[i][rank:, :] = dot(both[:rank], slot_rows(cot, tile, entries)).astype(jnp.bfloat16)


def weight_columns(weight, place):
    features = weight.shape[0]
    return weight[:, pl.ds(pl.multiple_of(place * features, 128), features)]


def near_kernel(which, place, data, weight, *refs):
    total = dot(data[...], weight_columns(weight, place[which]), NT)
    refs[-1][...] = total if which == 0 else refs[0][...] + total


def row_sums(start, count, place, near, term, weight, blocks, out, done, sem):
    at = 0
    for first in range(0, len(blocks), count):
        extent = blocks[first].shape[0]
        rows = slice(start + at, start + at + extent)
        total = near[rows, :] + term[rows, :].astype(jnp.float32)
        for i in range(count):
            total += dot(blocks[first + i][...], weight_columns(weight, place[2 + i]), NT)
        done[at : at + extent, :] = total.astype(jnp.bfloat16)
        at += extent
    copy = pltpu.make_async_copy(done, out.at[pl.ds(start, at), :], sem)
    copy.start()
    copy.wait()


def middle_kernel(groups, cap, count, tile, place, *refs):
    n = sum(len(g) for g in groups)
    blocks, refs = refs[: 2 * count], refs[2 * count :]
    sums, refs = refs[: len(groups)], refs[len(groups) :]
    packs, (near, weight), refs = refs[:n], refs[n : n + 2], refs[n + 2 :]
    out, term, done, sem = refs[-4:]
    term[...] = jnp.zeros_like(term)
    for g, slots in enumerate(groups):
        for i, slot in enumerate(slots):
            maps = packs[slot][...]
            rank = maps.shape[0] // 2
            maps = jnp.concatenate([jnp.zeros_like(maps[:rank]), maps[:rank]], axis=0)
            found = dot(sums[g][i * cap * TILE : (i + 1) * cap * TILE, :], maps)
            for c in range(cap):
                rows = tile_rows(tile[slot * cap + c])
                before = term[rows, :].astype(jnp.float32)
                term[rows, :] = (before + found[c * TILE : (c + 1) * TILE]).astype(term.dtype)
    row_sums(0, count, place, near, term, weight, blocks, out, done, sem)


def far_kernel(count, start, place, near, term, weight, *refs):
    out, token, done, sem = refs[-4:]
    token[...] = jnp.zeros_like(token)
    row_sums(start, count, place, near, term, weight, refs[:count], out, done, sem)


def final_kernel(count, scale, *refs):
    down, up = refs[-2:]
    rank = down.shape[0]
    for out, rows in ((down, slice(0, rank)), (up, slice(rank, 2 * rank))):
        total = refs[0][rows, :].astype(jnp.float32)
        for x in refs[1:count]:
            total += x[rows, :].astype(jnp.float32)
        out[...] = (total * scale).astype(out.dtype)


def on_device(
    activations,
    cotangent,
    frozen_weight,
    adapter_down_maps,
    adapter_up_maps,
    adapter_per_tile,
    live_per_tile,
    adapter_stored_row,
):
    rows, features = activations.shape
    tiles = rows // TILE
    stored, _, rank = adapter_down_maps.shape
    n = lax.axis_size("adapter")
    tensors = lax.axis_size("tensor")
    subs = lax.axis_size("sub")
    me = lax.axis_index("adapter")
    t_me, s_me = lax.axis_index("tensor"), lax.axis_index("sub")
    extents = [rows * c // sum(CHUNKS) for c in CHUNKS]
    starts = [sum(extents[:c]) for c in range(len(extents))]
    bf16, f32 = jnp.bfloat16, jnp.float32

    cap = -(-tiles // n)
    places = [t_me * subs + s_me, t_me * subs + (1 - s_me)]
    for s in (s_me, 1 - s_me):
        places += [jnp.remainder(t_me - k, tensors) * subs + s for k in range(1, tensors)]
    place = jnp.stack(places).astype(jnp.int32)

    groups = [[k for k in range(n) if 1 <= min(k, n - k) <= n // 4]]
    groups.append([k for k in range(n) if k not in groups[0]])

    down = jnp.swapaxes(adapter_down_maps, 1, 2).reshape(stored * rank, features)
    up = adapter_up_maps.reshape(stored * rank, features)
    pack_shape = jax.ShapeDtypeStruct((2 * rank, features), bf16)
    *parts, pack, pack_again = call(
        head_kernel,
        mib=56,
        in_specs=[ANY] * 3,
        out_specs=[ANY] * (FIRST + 2),
        out_shape=[jax.ShapeDtypeStruct((e, features), bf16) for e in extents[:FIRST]]
        + [pack_shape] * 2,
        scratch_shapes=[
            pltpu.VMEM((starts[FIRST], features), bf16),
            pltpu.VMEM(pack_shape.shape, bf16),
            pltpu.SemaphoreType.DMA((3, FIRST + 2)),
        ],
    )(cotangent, down, up)
    def across(part, aside=0):
        slice_axes, found = ("tensor", "sub"), []
        for k in range(1, tensors):
            to = [(t + k) % tensors * subs + (s + aside) % subs for t in range(tensors) for s in range(subs)]
            found.append(lax.ppermute(part, slice_axes, list(enumerate(to))))
        return found

    def forward(blocks):
        return [shift(x, "sub", subs, 1) for x in blocks]

    direct = [across(part) for part in parts]
    pair = shift(cotangent, "sub", subs, 1)
    table = jax.ShapeDtypeStruct((n * cap,), jnp.int32)
    later = [jax.ShapeDtypeStruct((e, features), bf16) for e in extents[FIRST:]]
    tile, live, *rest = call(
        functools.partial(plan_kernel, n, cap, tiles),
        in_specs=[SMEM] * 4 + [VMEM],
        out_specs=[SMEM] * 2 + [VMEM] * len(later),
        out_shape=[table] * 2 + later,
        scratch_shapes=[pltpu.SMEM((n,), jnp.int32)],
    )(adapter_per_tile, live_per_tile, adapter_stored_row, me.astype(jnp.int32).reshape(1), cotangent)
    parts = [*parts, *rest]

    def after(arrays):
        return [ANY] * len(arrays)

    def gate(blocks, ready):
        found = call(
            gate_kernel,
            in_specs=after(blocks) + [ANY],
            out_specs=after(blocks),
            out_shape=[jax.ShapeDtypeStruct(x.shape, x.dtype) for x in blocks],
            input_output_aliases={i: i for i in range(len(blocks))},
        )(*blocks, ready)
        return list(found)

    def near_part(which, data, ready, *before):
        return call(
            functools.partial(near_kernel, which),
            flops=HEAVY,
            in_specs=[SMEM] + [VMEM] * (2 + len(before)) + [ANY],
            out_specs=VMEM,
            out_shape=jax.ShapeDtypeStruct((rows, features), f32),
            input_output_aliases={3: 0} if before else {},
        )(place, data, frozen_weight, *before, ready)

    def tick(*ready):
        return call(
            tick_kernel,
            flops=HEAVY,
            in_specs=after(ready),
            out_specs=VMEM,
            out_shape=jax.ShapeDtypeStruct((8, 128), f32),
        )(*ready)

    def ranks(g, *wait):
        return call(
            functools.partial(rank_kernel, g, cap),
            in_specs=[SMEM] * 2 + [VMEM] * (2 + len(g)) + after(wait),
            out_specs=VMEM,
            out_shape=jax.ShapeDtypeStruct((len(g) * cap * TILE, 2 * rank), bf16),
        )(tile, live, activations, cotangent, *[packs[k] for k in g], *wait)

    def chip_sum(own, *wait):
        given = shift(own, "sub", subs, 1)
        sent = call(
            functools.partial(sum_kernel, 2, -1),
            in_specs=[VMEM] * 2 + after(wait),
            out_specs=VMEM,
            out_shape=jax.ShapeDtypeStruct(own.shape, bf16),
        )(own, given, *wait)
        return given, sent

    def slice_sum(own, given, others, held_parts, *wait):
        found = [own, given, *others]
        shapes = [jax.ShapeDtypeStruct(x.shape, x.dtype) for x in held_parts]
        return call(
            functools.partial(sum_kernel, len(found), -1 - len(shapes)),
            in_specs=[VMEM] * len(found) + after(held_parts) + after(wait),
            out_specs=[VMEM] + after(held_parts),
            out_shape=[jax.ShapeDtypeStruct(own.shape, bf16)] + shapes,
            input_output_aliases={len(found) + i: 1 + i for i in range(len(shapes))},
        )(*found, *held_parts, *wait)

    def adapter_terms(g, held, *wait):
        found = call(
            functools.partial(terms_kernel, g, cap),
            in_specs=[SMEM] + [VMEM] * 3 + after(wait),
            out_specs=[VMEM] * len(g),
            out_shape=[jax.ShapeDtypeStruct((2 * rank, features), bf16)] * len(g),
        )(tile, held, activations, cotangent, *wait)
        return dict(zip(g, found))

    first, second = groups
    packs = {0: pack} | {k: shift(pack, "adapter", n, k) for k in first}
    (pack_again,) = gate([pack_again], tile)
    packs |= {k: shift(pack_again, "adapter", n, k) for k in second if k}

    forwards = [forward(direct[0])]
    own = ranks(first, tick(*direct[0], pair))
    given, sent = chip_sum(own, tick(own), *forwards[0])
    mark = tick(sent)
    direct.append(across(*gate([parts[1]], mark)))
    near = near_part(0, cotangent, mark)
    (held,) = slice_sum(own, given, across(sent), [], near)
    sums = [held]
    own = ranks(second, held)
    terms = adapter_terms(first, held, own)
    given, sent = chip_sum(own, tick(own), terms[first[0]])
    mark = tick(sent)
    leaving = gate([terms[k] for k in first], mark)
    arrived = {k: shift(x, "adapter", n, -k) for k, x in zip(first, leaving)}
    direct.append(across(*gate([parts[2]], mark)))
    near = near_part(1, pair, mark, near)
    (held,) = slice_sum(own, given, across(sent), [], near)
    sums.append(held)
    terms |= adapter_terms(second, held)
    arrived |= {k: shift(terms[k], "adapter", n, -k) for k in second if k}
    direct[1] = gate(direct[1], held)
    forwards.append(forward(direct[1]))

    blocks = [x for c in range(2) for x in direct[c] + forwards[c]]
    count = len(blocks) // 2
    operands = [tile, place, *blocks, *sums, *[packs[k] for k in range(n)], near, frozen_weight]
    whole_shape = jax.ShapeDtypeStruct((rows, features), bf16)
    out, term = call(
        functools.partial(middle_kernel, groups, cap, count),
        mib=20,
        flops=HEAVY,
        in_specs=[SMEM] * 2 + [VMEM] * (len(operands) - 2) + [ANY] * 2,
        out_specs=[HBM, VMEM],
        out_shape=[whole_shape] * 2,
        scratch_shapes=[pltpu.VMEM((starts[2], features), bf16), pltpu.SemaphoreType.DMA],
    )(*operands, terms[second[-1]], tick(held))
    direct[2] = gate(direct[2], term)
    forwards.append(forward(direct[2]))
    operands = [place, near, term, frozen_weight, *direct[2], *forwards[2]]
    out, token = call(
        functools.partial(far_kernel, count, starts[2]),
        mib=16,
        in_specs=[SMEM] + [VMEM] * (len(operands) - 1) + [HBM, ANY],
        out_specs=[HBM, VMEM],
        out_shape=[whole_shape, jax.ShapeDtypeStruct((8, 128), f32)],
        scratch_shapes=[pltpu.VMEM((rows - starts[2], features), bf16), pltpu.SemaphoreType.DMA],
        input_output_aliases={len(operands): 0},
    )(*operands, out, tick(held, terms[second[-1]]))
    maps_shape = jax.ShapeDtypeStruct((rank, features), bf16)
    down_grad, up_grad = call(
        functools.partial(final_kernel, n, (stored / rows) ** 0.5),
        in_specs=[VMEM] * n + [ANY],
        out_specs=[VMEM] * 2,
        out_shape=[maps_shape] * 2,
    )(terms[0], *[arrived[k] for k in range(1, n)], token)
    down_grad = jnp.swapaxes(down_grad.reshape(stored, rank, features), 1, 2)
    up_grad = up_grad.reshape(stored, rank, features)
    return (out, down_grad, up_grad)


def solution(mesh):
    return jax.shard_map(
        on_device,
        mesh=mesh,
        in_specs=(
            P(("groups", "adapter"), ("tensor", "sub")),
            P(("groups", "adapter"), ("tensor", "sub")),
            P(("tensor", "sub"), None),
            P(("groups", "adapter"), ("tensor", "sub"), None),
            P(("groups", "adapter"), None, ("tensor", "sub")),
            P("groups"),
            P("groups"),
            P("groups"),
        ),
        out_specs=(
            P(("groups", "adapter"), ("tensor", "sub")),
            P(("groups", "adapter"), ("tensor", "sub"), None),
            P(("groups", "adapter"), None, ("tensor", "sub")),
        ),
        check_vma=False,
    )
```

```python
import functools

import jax
import jax.numpy as jnp
from jax import lax
from jax.experimental import pallas as pl
from jax.experimental.pallas import tpu as pltpu
from jax.sharding import PartitionSpec as P

TILE = 128
HEAVY = 1 << 33
CHUNKS = (6, 6, 4)
FIRST = 1
NT = (((1,), (1,)), ((), ()))
SMEM = pl.BlockSpec(memory_space=pltpu.SMEM)
VMEM = pl.BlockSpec(memory_space=pltpu.VMEM)
ANY = pl.BlockSpec(memory_space=pl.ANY)
HBM = pl.BlockSpec(memory_space=pltpu.HBM)


def shift(array, axis, size, by):
    return lax.ppermute(array, axis, [(i, (i + by) % size) for i in range(size)])


def call(body, mib=12, flops=0, **kwargs):
    params = pltpu.CompilerParams(vmem_limit_bytes=mib * 1024 * 1024)
    cost = pl.CostEstimate(flops=flops, bytes_accessed=0, transcendentals=0)
    name = getattr(body, "func", body).__name__
    return pl.pallas_call(body, compiler_params=params, cost_estimate=cost, name=name, **kwargs)


def dot(a, b, dims=(((1,), (0,)), ((), ()))):
    return lax.dot_general(a, b, dims, preferred_element_type=jnp.float32)


def tile_rows(index):
    return pl.ds(pl.multiple_of(index * TILE, TILE), TILE)


def slot_rows(data, tile, entries):
    return jnp.concatenate([data[tile_rows(tile[e]), :] for e in entries], axis=0)


def copy_all(pairs, sems):
    copies = [pltpu.make_async_copy(a, b, sems.at[i]) for i, (a, b) in enumerate(pairs)]
    for copy in copies:
        copy.start()
    return copies


def head_kernel(cot, down, up, *refs):
    *parts, pack, again, held, pack_held, sems = refs
    rank, rows, start = down.shape[0], [], 0
    for part in parts:
        rows.append(pl.ds(start, part.shape[0]))
        start += part.shape[0]
    pairs = [(cot.at[r, :], held.at[r, :]) for r in rows]
    pairs += [(down, pack_held.at[pl.ds(0, rank), :]), (up, pack_held.at[pl.ds(rank, rank), :])]
    loads = copy_all(pairs, sems.at[0])
    stores = []
    for i, part in enumerate(parts):
        loads[i].wait()
        stores.append(pltpu.make_async_copy(held.at[rows[i], :], part, sems.at[1, i]))
        stores[-1].start()
    for load in loads[-2:]:
        load.wait()
    stores += copy_all([(pack_held, pack), (pack_held, again)], sems.at[2])
    for store in stores:
        store.wait()


def plan_kernel(n, cap, tiles, ids, live_all, stored, me, own, tile, live, *refs):
    *parts, count = refs
    start = own.shape[0] - sum(part.shape[0] for part in parts)
    for part in parts:
        part[...] = own[start : start + part.shape[0], :]
        start += part.shape[0]
    for k in range(n):
        count[k] = 0
    for e in range(n * cap):
        tile[e] = 0
        live[e] = 0
    for t in range(tiles):
        at = me[0] * tiles + t
        k = lax.rem(me[0] - stored[ids[at]] + n, n)
        e = jnp.minimum(k * cap + count[k], n * cap - 1)
        tile[e] = t
        live[e] = live_all[at]
        count[k] = count[k] + 1


def rank_kernel(slots, cap, tile, live, act, cot, *refs):
    packs, out = refs[: len(slots)], refs[-1]
    width = packs[0].shape[0]
    part = lax.broadcasted_iota(jnp.int32, packs[0].shape, 0) < width // 2
    row = lax.broadcasted_iota(jnp.int32, (TILE, width), 0)
    for i, (slot, pack) in enumerate(zip(slots, packs)):
        entries = range(slot * cap, (slot + 1) * cap)
        maps = pack[...]
        zero = jnp.zeros_like(maps)
        both = dot(slot_rows(act, tile, entries), jnp.where(part, maps, zero), NT)
        both += dot(slot_rows(cot, tile, entries), jnp.where(part, zero, maps), NT)
        for c, e in enumerate(entries):
            at = (i * cap + c) * TILE
            out[at : at + TILE, :] = jnp.where(
                row < live[e], both[c * TILE : (c + 1) * TILE], 0.0
            ).astype(jnp.bfloat16)


def sum_kernel(count, place, *refs):
    total = refs[0][...].astype(jnp.float32)
    for x in refs[1:count]:
        total += x[...].astype(jnp.float32)
    out = refs[place]
    out[...] = total.astype(out.dtype)


def gate_kernel(*refs):
    pass


def tick_kernel(*refs):
    refs[-1][...] = jnp.zeros_like(refs[-1])


def terms_kernel(slots, cap, tile, held, act, cot, *refs):
    terms = refs[-len(slots) :]
    rank = held.shape[1] // 2
    for i, slot in enumerate(slots):
        entries = range(slot * cap, (slot + 1) * cap)
        both = held[i * cap * TILE : (i + 1) * cap * TILE, :].astype(jnp.float32)
        both = both.T.astype(jnp.bfloat16)
        terms[i][:rank, :] = dot(both[rank:], slot_rows(act, tile, entries)).astype(jnp.bfloat16)
        terms[i][rank:, :] = dot(both[:rank], slot_rows(cot, tile, entries)).astype(jnp.bfloat16)


def weight_columns(weight, place):
    features = weight.shape[0]
    return weight[:, pl.ds(pl.multiple_of(place * features, 128), features)]


def near_kernel(which, place, data, weight, *refs):
    total = dot(data[...], weight_columns(weight, place[which]), NT)
    refs[-1][...] = total if which == 0 else refs[0][...] + total


def turn_kernel(place, weight, out):
    features = weight.shape[0]
    for i in range(out.shape[0] // features):
        out[i * features : (i + 1) * features, :] = weight_columns(weight, place[2 + i]).T


def row_sums(start, count, near, term, turned, blocks, out, done, sem):
    at = 0
    for first in range(0, len(blocks), count):
        extent = blocks[first].shape[0]
        rows = slice(start + at, start + at + extent)
        total = near[rows, :] + term[rows, :].astype(jnp.float32)
        for i in range(count):
            features = turned.shape[1]
            total += dot(blocks[first + i][...], turned[i * features : (i + 1) * features, :])
        done[at : at + extent, :] = total.astype(jnp.bfloat16)
        at += extent
    copy = pltpu.make_async_copy(done, out.at[pl.ds(start, at), :], sem)
    copy.start()
    copy.wait()


def middle_kernel(groups, cap, count, tile, *refs):
    n = sum(len(g) for g in groups)
    blocks, refs = refs[: 2 * count], refs[2 * count :]
    sums, refs = refs[: len(groups)], refs[len(groups) :]
    packs, (near, turned), refs = refs[:n], refs[n : n + 2], refs[n + 2 :]
    out, term, done, sem = refs[-4:]
    term[...] = jnp.zeros_like(term)
    for g, slots in enumerate(groups):
        for i, slot in enumerate(slots):
            maps = packs[slot][...]
            rank = maps.shape[0] // 2
            maps = jnp.concatenate([jnp.zeros_like(maps[:rank]), maps[:rank]], axis=0)
            found = dot(sums[g][i * cap * TILE : (i + 1) * cap * TILE, :], maps)
            for c in range(cap):
                rows = tile_rows(tile[slot * cap + c])
                before = term[rows, :].astype(jnp.float32)
                term[rows, :] = (before + found[c * TILE : (c + 1) * TILE]).astype(term.dtype)
    row_sums(0, count, near, term, turned, blocks, out, done, sem)


def far_kernel(count, start, near, term, turned, *refs):
    out, token, done, sem = refs[-4:]
    token[...] = jnp.zeros_like(token)
    row_sums(start, count, near, term, turned, refs[:count], out, done, sem)


def final_kernel(count, scale, *refs):
    down, up = refs[-2:]
    rank = down.shape[0]
    for out, rows in ((down, slice(0, rank)), (up, slice(rank, 2 * rank))):
        total = refs[0][rows, :].astype(jnp.float32)
        for x in refs[1:count]:
            total += x[rows, :].astype(jnp.float32)
        out[...] = (total * scale).astype(out.dtype)


def on_device(
    activations,
    cotangent,
    frozen_weight,
    adapter_down_maps,
    adapter_up_maps,
    adapter_per_tile,
    live_per_tile,
    adapter_stored_row,
):
    rows, features = activations.shape
    tiles = rows // TILE
    stored, _, rank = adapter_down_maps.shape
    n = lax.axis_size("adapter")
    tensors = lax.axis_size("tensor")
    subs = lax.axis_size("sub")
    me = lax.axis_index("adapter")
    t_me, s_me = lax.axis_index("tensor"), lax.axis_index("sub")
    extents = [rows * c // sum(CHUNKS) for c in CHUNKS]
    starts = [sum(extents[:c]) for c in range(len(extents))]
    bf16, f32 = jnp.bfloat16, jnp.float32

    cap = -(-tiles // n)
    places = [t_me * subs + s_me, t_me * subs + (1 - s_me)]
    for s in (s_me, 1 - s_me):
        places += [jnp.remainder(t_me - k, tensors) * subs + s for k in range(1, tensors)]
    place = jnp.stack(places).astype(jnp.int32)

    groups = [[k for k in range(n) if 1 <= min(k, n - k) <= n // 4]]
    groups.append([k for k in range(n) if k not in groups[0]])

    down = jnp.swapaxes(adapter_down_maps, 1, 2).reshape(stored * rank, features)
    up = adapter_up_maps.reshape(stored * rank, features)
    pack_shape = jax.ShapeDtypeStruct((2 * rank, features), bf16)
    *parts, pack, pack_again = call(
        head_kernel,
        mib=56,
        in_specs=[ANY] * 3,
        out_specs=[ANY] * (FIRST + 2),
        out_shape=[jax.ShapeDtypeStruct((e, features), bf16) for e in extents[:FIRST]]
        + [pack_shape] * 2,
        scratch_shapes=[
            pltpu.VMEM((starts[FIRST], features), bf16),
            pltpu.VMEM(pack_shape.shape, bf16),
            pltpu.SemaphoreType.DMA((3, FIRST + 2)),
        ],
    )(cotangent, down, up)
    def across(part, aside=0):
        slice_axes, found = ("tensor", "sub"), []
        for k in range(1, tensors):
            to = [(t + k) % tensors * subs + (s + aside) % subs for t in range(tensors) for s in range(subs)]
            found.append(lax.ppermute(part, slice_axes, list(enumerate(to))))
        return found

    def forward(blocks):
        return [shift(x, "sub", subs, 1) for x in blocks]

    direct = [across(part) for part in parts]
    pair = shift(cotangent, "sub", subs, 1)
    table = jax.ShapeDtypeStruct((n * cap,), jnp.int32)
    later = [jax.ShapeDtypeStruct((e, features), bf16) for e in extents[FIRST:]]
    tile, live, *rest = call(
        functools.partial(plan_kernel, n, cap, tiles),
        in_specs=[SMEM] * 4 + [VMEM],
        out_specs=[SMEM] * 2 + [VMEM] * len(later),
        out_shape=[table] * 2 + later,
        scratch_shapes=[pltpu.SMEM((n,), jnp.int32)],
    )(adapter_per_tile, live_per_tile, adapter_stored_row, me.astype(jnp.int32).reshape(1), cotangent)
    parts = [*parts, *rest]

    def after(arrays):
        return [ANY] * len(arrays)

    def gate(blocks, ready):
        found = call(
            gate_kernel,
            in_specs=after(blocks) + [ANY],
            out_specs=after(blocks),
            out_shape=[jax.ShapeDtypeStruct(x.shape, x.dtype) for x in blocks],
            input_output_aliases={i: i for i in range(len(blocks))},
        )(*blocks, ready)
        return list(found)

    def near_part(which, data, ready, *before):
        return call(
            functools.partial(near_kernel, which),
            flops=HEAVY,
            in_specs=[SMEM] + [VMEM] * (2 + len(before)) + [ANY],
            out_specs=VMEM,
            out_shape=jax.ShapeDtypeStruct((rows, features), f32),
            input_output_aliases={3: 0} if before else {},
        )(place, data, frozen_weight, *before, ready)

    def tick(*ready):
        return call(
            tick_kernel,
            flops=HEAVY,
            in_specs=after(ready),
            out_specs=VMEM,
            out_shape=jax.ShapeDtypeStruct((8, 128), f32),
        )(*ready)

    def ranks(g, *wait):
        return call(
            functools.partial(rank_kernel, g, cap),
            in_specs=[SMEM] * 2 + [VMEM] * (2 + len(g)) + after(wait),
            out_specs=VMEM,
            out_shape=jax.ShapeDtypeStruct((len(g) * cap * TILE, 2 * rank), bf16),
        )(tile, live, activations, cotangent, *[packs[k] for k in g], *wait)

    def chip_sum(own, *wait):
        given = shift(own, "sub", subs, 1)
        sent = call(
            functools.partial(sum_kernel, 2, -1),
            in_specs=[VMEM] * 2 + after(wait),
            out_specs=VMEM,
            out_shape=jax.ShapeDtypeStruct(own.shape, bf16),
        )(own, given, *wait)
        return given, sent

    def slice_sum(own, given, others, held_parts, *wait):
        found = [own, given, *others]
        shapes = [jax.ShapeDtypeStruct(x.shape, x.dtype) for x in held_parts]
        return call(
            functools.partial(sum_kernel, len(found), -1 - len(shapes)),
            in_specs=[VMEM] * len(found) + after(held_parts) + after(wait),
            out_specs=[VMEM] + after(held_parts),
            out_shape=[jax.ShapeDtypeStruct(own.shape, bf16)] + shapes,
            input_output_aliases={len(found) + i: 1 + i for i in range(len(shapes))},
        )(*found, *held_parts, *wait)

    def adapter_terms(g, held, *wait):
        found = call(
            functools.partial(terms_kernel, g, cap),
            in_specs=[SMEM] + [VMEM] * 3 + after(wait),
            out_specs=[VMEM] * len(g),
            out_shape=[jax.ShapeDtypeStruct((2 * rank, features), bf16)] * len(g),
        )(tile, held, activations, cotangent, *wait)
        return dict(zip(g, found))

    first, second = groups
    packs = {0: pack} | {k: shift(pack, "adapter", n, k) for k in first}
    (pack_again,) = gate([pack_again], tile)
    packs |= {k: shift(pack_again, "adapter", n, k) for k in second if k}

    forwards = [forward(direct[0])]
    turned = call(
        turn_kernel,
        in_specs=[SMEM, VMEM],
        out_specs=VMEM,
        out_shape=jax.ShapeDtypeStruct((2 * (tensors - 1) * features, features), bf16),
    )(place, frozen_weight)
    own = ranks(first, tick(*direct[0], pair, turned))
    given, sent = chip_sum(own, tick(own), *forwards[0])
    mark = tick(sent)
    opened = gate([parts[1]], mark)
    direct.append(across(*opened))
    near = near_part(0, cotangent, opened[0])
    (held,) = slice_sum(own, given, across(sent), [], near)
    sums = [held]
    own = ranks(second, held)
    terms = adapter_terms(first, held, own)
    given, sent = chip_sum(own, tick(own), terms[first[0]])
    mark = tick(sent)
    leaving = gate([terms[k] for k in first], mark)
    arrived = {k: shift(x, "adapter", n, -k) for k, x in zip(first, leaving)}
    direct.append(across(*gate([parts[2]], mark)))
    near = near_part(1, pair, mark, near)
    direct[1] = gate(direct[1], near)
    forwards.append(forward(direct[1]))
    (held,) = slice_sum(own, given, across(sent), [], near)
    sums.append(held)
    terms |= adapter_terms(second, held, *direct[1])
    arrived |= {k: shift(terms[k], "adapter", n, -k) for k in second if k}

    blocks = [x for c in range(2) for x in direct[c] + forwards[c]]
    count = len(blocks) // 2
    operands = [tile, *blocks, *sums, *[packs[k] for k in range(n)], near, turned]
    whole_shape = jax.ShapeDtypeStruct((rows, features), bf16)
    out, term = call(
        functools.partial(middle_kernel, groups, cap, count),
        mib=20,
        flops=HEAVY,
        in_specs=[SMEM] + [VMEM] * (len(operands) - 1) + [ANY] * 2,
        out_specs=[HBM, VMEM],
        out_shape=[whole_shape] * 2,
        scratch_shapes=[pltpu.VMEM((starts[2], features), bf16), pltpu.SemaphoreType.DMA],
    )(*operands, terms[second[-1]], tick(held))
    direct[2] = gate(direct[2], term)
    forwards.append(forward(direct[2]))
    operands = [near, term, turned, *direct[2], *forwards[2]]
    out, token = call(
        functools.partial(far_kernel, count, starts[2]),
        mib=16,
        in_specs=[VMEM] * len(operands) + [HBM, ANY],
        out_specs=[HBM, VMEM],
        out_shape=[whole_shape, jax.ShapeDtypeStruct((8, 128), f32)],
        scratch_shapes=[pltpu.VMEM((rows - starts[2], features), bf16), pltpu.SemaphoreType.DMA],
        input_output_aliases={len(operands): 0},
    )(*operands, out, tick(held, terms[second[-1]]))
    maps_shape = jax.ShapeDtypeStruct((rank, features), bf16)
    down_grad, up_grad = call(
        functools.partial(final_kernel, n, (stored / rows) ** 0.5),
        in_specs=[VMEM] * n + [ANY],
        out_specs=[VMEM] * 2,
        out_shape=[maps_shape] * 2,
    )(terms[0], *[arrived[k] for k in range(1, n)], token)
    down_grad = jnp.swapaxes(down_grad.reshape(stored, rank, features), 1, 2)
    up_grad = up_grad.reshape(stored, rank, features)
    return (out, down_grad, up_grad)


def solution(mesh):
    return jax.shard_map(
        on_device,
        mesh=mesh,
        in_specs=(
            P(("groups", "adapter"), ("tensor", "sub")),
            P(("groups", "adapter"), ("tensor", "sub")),
            P(("tensor", "sub"), None),
            P(("groups", "adapter"), ("tensor", "sub"), None),
            P(("groups", "adapter"), None, ("tensor", "sub")),
            P("groups"),
            P("groups"),
            P("groups"),
        ),
        out_specs=(
            P(("groups", "adapter"), ("tensor", "sub")),
            P(("groups", "adapter"), ("tensor", "sub"), None),
            P(("groups", "adapter"), None, ("tensor", "sub")),
        ),
        check_vma=False,
    )
```

```python
import functools

import jax
import jax.numpy as jnp
from jax import lax
from jax.experimental import pallas as pl
from jax.experimental.pallas import tpu as pltpu
from jax.sharding import PartitionSpec as P

TILE = 128
HEAVY = 1 << 33
CHUNKS = (6, 5, 5)
FIRST = 1
NT = (((1,), (1,)), ((), ()))
SMEM = pl.BlockSpec(memory_space=pltpu.SMEM)
VMEM = pl.BlockSpec(memory_space=pltpu.VMEM)
ANY = pl.BlockSpec(memory_space=pl.ANY)
HBM = pl.BlockSpec(memory_space=pltpu.HBM)


def shift(array, axis, size, by):
    return lax.ppermute(array, axis, [(i, (i + by) % size) for i in range(size)])


def call(body, mib=12, flops=0, **kwargs):
    params = pltpu.CompilerParams(vmem_limit_bytes=mib * 1024 * 1024)
    cost = pl.CostEstimate(flops=flops, bytes_accessed=0, transcendentals=0)
    name = getattr(body, "func", body).__name__
    return pl.pallas_call(body, compiler_params=params, cost_estimate=cost, name=name, **kwargs)


def dot(a, b, dims=(((1,), (0,)), ((), ()))):
    return lax.dot_general(a, b, dims, preferred_element_type=jnp.float32)


def tile_rows(index):
    return pl.ds(pl.multiple_of(index * TILE, TILE), TILE)


def slot_rows(data, tile, entries):
    return jnp.concatenate([data[tile_rows(tile[e]), :] for e in entries], axis=0)


def copy_all(pairs, sems):
    copies = [pltpu.make_async_copy(a, b, sems.at[i]) for i, (a, b) in enumerate(pairs)]
    for copy in copies:
        copy.start()
    return copies


def head_kernel(cot, down, up, *refs):
    *parts, pack, again, held, pack_held, sems = refs
    rank, rows, start = down.shape[0], [], 0
    for part in parts:
        rows.append(pl.ds(start, part.shape[0]))
        start += part.shape[0]
    pairs = [(cot.at[r, :], held.at[r, :]) for r in rows]
    pairs += [(down, pack_held.at[pl.ds(0, rank), :]), (up, pack_held.at[pl.ds(rank, rank), :])]
    loads = copy_all(pairs, sems.at[0])
    stores = []
    for i, part in enumerate(parts):
        loads[i].wait()
        stores.append(pltpu.make_async_copy(held.at[rows[i], :], part, sems.at[1, i]))
        stores[-1].start()
    for load in loads[-2:]:
        load.wait()
    stores += copy_all([(pack_held, pack), (pack_held, again)], sems.at[2])
    for store in stores:
        store.wait()


def plan_kernel(n, cap, tiles, ids, live_all, stored, me, own, tile, live, *refs):
    *parts, count = refs
    start = own.shape[0] - sum(part.shape[0] for part in parts)
    for part in parts:
        part[...] = own[start : start + part.shape[0], :]
        start += part.shape[0]
    for k in range(n):
        count[k] = 0
    for e in range(n * cap):
        tile[e] = 0
        live[e] = 0
    for t in range(tiles):
        at = me[0] * tiles + t
        k = lax.rem(me[0] - stored[ids[at]] + n, n)
        e = jnp.minimum(k * cap + count[k], n * cap - 1)
        tile[e] = t
        live[e] = live_all[at]
        count[k] = count[k] + 1


def rank_kernel(slots, cap, tile, live, act, cot, *refs):
    packs, out = refs[: len(slots)], refs[-1]
    width = packs[0].shape[0]
    part = lax.broadcasted_iota(jnp.int32, packs[0].shape, 0) < width // 2
    row = lax.broadcasted_iota(jnp.int32, (TILE, width), 0)
    for i, (slot, pack) in enumerate(zip(slots, packs)):
        entries = range(slot * cap, (slot + 1) * cap)
        maps = pack[...]
        zero = jnp.zeros_like(maps)
        both = dot(slot_rows(act, tile, entries), jnp.where(part, maps, zero), NT)
        both += dot(slot_rows(cot, tile, entries), jnp.where(part, zero, maps), NT)
        for c, e in enumerate(entries):
            at = (i * cap + c) * TILE
            out[at : at + TILE, :] = jnp.where(
                row < live[e], both[c * TILE : (c + 1) * TILE], 0.0
            ).astype(jnp.bfloat16)


def sum_kernel(count, place, *refs):
    total = refs[0][...].astype(jnp.float32)
    for x in refs[1:count]:
        total += x[...].astype(jnp.float32)
    out = refs[place]
    out[...] = total.astype(out.dtype)


def gate_kernel(*refs):
    pass


def tick_kernel(*refs):
    refs[-1][...] = jnp.zeros_like(refs[-1])


def terms_kernel(slots, cap, tile, held, act, cot, *refs):
    terms = refs[-len(slots) :]
    rank = held.shape[1] // 2
    for i, slot in enumerate(slots):
        entries = range(slot * cap, (slot + 1) * cap)
        both = held[i * cap * TILE : (i + 1) * cap * TILE, :].astype(jnp.float32)
        both = both.T.astype(jnp.bfloat16)
        terms[i][:rank, :] = dot(both[rank:], slot_rows(act, tile, entries)).astype(jnp.bfloat16)
        terms[i][rank:, :] = dot(both[:rank], slot_rows(cot, tile, entries)).astype(jnp.bfloat16)


def weight_columns(weight, place):
    features = weight.shape[0]
    return weight[:, pl.ds(pl.multiple_of(place * features, 128), features)]


def near_kernel(which, place, data, weight, *refs):
    total = dot(data[...], weight_columns(weight, place[which]), NT)
    refs[-1][...] = total if which == 0 else refs[0][...] + total


def turn_kernel(place, weight, out):
    features = weight.shape[0]
    for i in range(out.shape[0] // features):
        out[i * features : (i + 1) * features, :] = weight_columns(weight, place[2 + i]).T


def row_sums(start, count, near, term, turned, blocks, out, done, sem):
    at = 0
    for first in range(0, len(blocks), count):
        extent = blocks[first].shape[0]
        rows = slice(start + at, start + at + extent)
        total = near[rows, :] + term[rows, :].astype(jnp.float32)
        for i in range(count):
            features = turned.shape[1]
            total += dot(blocks[first + i][...], turned[i * features : (i + 1) * features, :])
        done[at : at + extent, :] = total.astype(jnp.bfloat16)
        at += extent
    copy = pltpu.make_async_copy(done, out.at[pl.ds(start, at), :], sem)
    copy.start()
    copy.wait()


def middle_kernel(groups, cap, count, tile, *refs):
    n = sum(len(g) for g in groups)
    blocks, refs = refs[: 2 * count], refs[2 * count :]
    sums, refs = refs[: len(groups)], refs[len(groups) :]
    packs, (near, turned), refs = refs[:n], refs[n : n + 2], refs[n + 2 :]
    out, term, done, sem = refs[-4:]
    term[...] = jnp.zeros_like(term)
    for g, slots in enumerate(groups):
        for i, slot in enumerate(slots):
            maps = packs[slot][...]
            rank = maps.shape[0] // 2
            maps = jnp.concatenate([jnp.zeros_like(maps[:rank]), maps[:rank]], axis=0)
            found = dot(sums[g][i * cap * TILE : (i + 1) * cap * TILE, :], maps)
            for c in range(cap):
                rows = tile_rows(tile[slot * cap + c])
                before = term[rows, :].astype(jnp.float32)
                term[rows, :] = (before + found[c * TILE : (c + 1) * TILE]).astype(term.dtype)
    row_sums(0, count, near, term, turned, blocks, out, done, sem)


def far_kernel(count, start, near, term, turned, *refs):
    out, token, done, sem = refs[-4:]
    token[...] = jnp.zeros_like(token)
    row_sums(start, count, near, term, turned, refs[:count], out, done, sem)


def final_kernel(count, scale, *refs):
    down, up = refs[-2:]
    rank = down.shape[0]
    for out, rows in ((down, slice(0, rank)), (up, slice(rank, 2 * rank))):
        total = refs[0][rows, :].astype(jnp.float32)
        for x in refs[1:count]:
            total += x[rows, :].astype(jnp.float32)
        out[...] = (total * scale).astype(out.dtype)


def on_device(
    activations,
    cotangent,
    frozen_weight,
    adapter_down_maps,
    adapter_up_maps,
    adapter_per_tile,
    live_per_tile,
    adapter_stored_row,
):
    rows, features = activations.shape
    tiles = rows // TILE
    stored, _, rank = adapter_down_maps.shape
    n = lax.axis_size("adapter")
    tensors = lax.axis_size("tensor")
    subs = lax.axis_size("sub")
    me = lax.axis_index("adapter")
    t_me, s_me = lax.axis_index("tensor"), lax.axis_index("sub")
    extents = [rows * c // sum(CHUNKS) for c in CHUNKS]
    starts = [sum(extents[:c]) for c in range(len(extents))]
    bf16, f32 = jnp.bfloat16, jnp.float32

    cap = -(-tiles // n)
    places = [t_me * subs + s_me, t_me * subs + (1 - s_me)]
    for s in (s_me, 1 - s_me):
        places += [jnp.remainder(t_me - k, tensors) * subs + s for k in range(1, tensors)]
    place = jnp.stack(places).astype(jnp.int32)

    groups = [[k for k in range(n) if 1 <= min(k, n - k) <= n // 4]]
    groups.append([k for k in range(n) if k not in groups[0]])

    down = jnp.swapaxes(adapter_down_maps, 1, 2).reshape(stored * rank, features)
    up = adapter_up_maps.reshape(stored * rank, features)
    pack_shape = jax.ShapeDtypeStruct((2 * rank, features), bf16)
    *parts, pack, pack_again = call(
        head_kernel,
        mib=56,
        in_specs=[ANY] * 3,
        out_specs=[ANY] * (FIRST + 2),
        out_shape=[jax.ShapeDtypeStruct((e, features), bf16) for e in extents[:FIRST]]
        + [pack_shape] * 2,
        scratch_shapes=[
            pltpu.VMEM((starts[FIRST], features), bf16),
            pltpu.VMEM(pack_shape.shape, bf16),
            pltpu.SemaphoreType.DMA((3, FIRST + 2)),
        ],
    )(cotangent, down, up)
    def across(part, aside=0):
        slice_axes, found = ("tensor", "sub"), []
        for k in range(1, tensors):
            to = [(t + k) % tensors * subs + (s + aside) % subs for t in range(tensors) for s in range(subs)]
            found.append(lax.ppermute(part, slice_axes, list(enumerate(to))))
        return found

    def forward(blocks):
        return [shift(x, "sub", subs, 1) for x in blocks]

    direct = [across(part) for part in parts]
    pair = shift(cotangent, "sub", subs, 1)
    table = jax.ShapeDtypeStruct((n * cap,), jnp.int32)
    later = [jax.ShapeDtypeStruct((e, features), bf16) for e in extents[FIRST:]]
    tile, live, *rest = call(
        functools.partial(plan_kernel, n, cap, tiles),
        in_specs=[SMEM] * 4 + [VMEM],
        out_specs=[SMEM] * 2 + [VMEM] * len(later),
        out_shape=[table] * 2 + later,
        scratch_shapes=[pltpu.SMEM((n,), jnp.int32)],
    )(adapter_per_tile, live_per_tile, adapter_stored_row, me.astype(jnp.int32).reshape(1), cotangent)
    parts = [*parts, *rest]

    def after(arrays):
        return [ANY] * len(arrays)

    def gate(blocks, ready):
        found = call(
            gate_kernel,
            in_specs=after(blocks) + [ANY],
            out_specs=after(blocks),
            out_shape=[jax.ShapeDtypeStruct(x.shape, x.dtype) for x in blocks],
            input_output_aliases={i: i for i in range(len(blocks))},
        )(*blocks, ready)
        return list(found)

    def near_part(which, data, ready, *before):
        return call(
            functools.partial(near_kernel, which),
            flops=HEAVY,
            in_specs=[SMEM] + [VMEM] * (2 + len(before)) + [ANY],
            out_specs=VMEM,
            out_shape=jax.ShapeDtypeStruct((rows, features), f32),
            input_output_aliases={3: 0} if before else {},
        )(place, data, frozen_weight, *before, ready)

    def tick(*ready):
        return call(
            tick_kernel,
            flops=HEAVY,
            in_specs=after(ready),
            out_specs=VMEM,
            out_shape=jax.ShapeDtypeStruct((8, 128), f32),
        )(*ready)

    def ranks(g, *wait):
        return call(
            functools.partial(rank_kernel, g, cap),
            in_specs=[SMEM] * 2 + [VMEM] * (2 + len(g)) + after(wait),
            out_specs=VMEM,
            out_shape=jax.ShapeDtypeStruct((len(g) * cap * TILE, 2 * rank), bf16),
        )(tile, live, activations, cotangent, *[packs[k] for k in g], *wait)

    def chip_sum(own, *wait):
        given = shift(own, "sub", subs, 1)
        sent = call(
            functools.partial(sum_kernel, 2, -1),
            in_specs=[VMEM] * 2 + after(wait),
            out_specs=VMEM,
            out_shape=jax.ShapeDtypeStruct(own.shape, bf16),
        )(own, given, *wait)
        return given, sent

    def slice_sum(own, given, others, held_parts, *wait):
        found = [own, given, *others]
        shapes = [jax.ShapeDtypeStruct(x.shape, x.dtype) for x in held_parts]
        return call(
            functools.partial(sum_kernel, len(found), -1 - len(shapes)),
            in_specs=[VMEM] * len(found) + after(held_parts) + after(wait),
            out_specs=[VMEM] + after(held_parts),
            out_shape=[jax.ShapeDtypeStruct(own.shape, bf16)] + shapes,
            input_output_aliases={len(found) + i: 1 + i for i in range(len(shapes))},
        )(*found, *held_parts, *wait)

    def adapter_terms(g, held, *wait):
        found = call(
            functools.partial(terms_kernel, g, cap),
            in_specs=[SMEM] + [VMEM] * 3 + after(wait),
            out_specs=[VMEM] * len(g),
            out_shape=[jax.ShapeDtypeStruct((2 * rank, features), bf16)] * len(g),
        )(tile, held, activations, cotangent, *wait)
        return dict(zip(g, found))

    first, second = groups
    packs = {0: pack} | {k: shift(pack, "adapter", n, k) for k in first}
    (pack_again,) = gate([pack_again], tile)
    packs |= {k: shift(pack_again, "adapter", n, k) for k in second if k}

    forwards = [forward(direct[0])]
    turned = call(
        turn_kernel,
        in_specs=[SMEM, VMEM],
        out_specs=VMEM,
        out_shape=jax.ShapeDtypeStruct((2 * (tensors - 1) * features, features), bf16),
    )(place, frozen_weight)
    own = ranks(first, tick(*direct[0], pair, turned))
    given, sent = chip_sum(own, tick(own), *forwards[0])
    mark = tick(sent)
    opened = gate([parts[1]], mark)
    direct.append(across(*opened))
    near = near_part(0, cotangent, opened[0])
    (held,) = slice_sum(own, given, across(sent), [], near)
    sums = [held]
    own = ranks(second, held)
    terms = adapter_terms(first, held, own)
    given, sent = chip_sum(own, tick(own), terms[first[0]])
    mark = tick(sent)
    leaving = gate([terms[k] for k in first], mark)
    arrived = {k: shift(x, "adapter", n, -k) for k, x in zip(first, leaving)}
    near = near_part(1, pair, mark, near)
    direct[1] = gate(direct[1], near)
    forwards.append(forward(direct[1]))
    (held,) = slice_sum(own, given, across(sent), [], near)
    sums.append(held)
    direct.append(across(*gate([parts[2]], held)))
    terms |= adapter_terms(second, held, *direct[1])
    arrived |= {k: shift(terms[k], "adapter", n, -k) for k in second if k}

    blocks = [x for c in range(2) for x in direct[c] + forwards[c]]
    count = len(blocks) // 2
    operands = [tile, *blocks, *sums, *[packs[k] for k in range(n)], near, turned]
    whole_shape = jax.ShapeDtypeStruct((rows, features), bf16)
    out, term = call(
        functools.partial(middle_kernel, groups, cap, count),
        mib=20,
        flops=HEAVY,
        in_specs=[SMEM] + [VMEM] * (len(operands) - 1) + [ANY] * 2,
        out_specs=[HBM, VMEM],
        out_shape=[whole_shape] * 2,
        scratch_shapes=[pltpu.VMEM((starts[2], features), bf16), pltpu.SemaphoreType.DMA],
    )(*operands, terms[second[-1]], tick(held))
    direct[2] = gate(direct[2], term)
    forwards.append(forward(direct[2]))
    operands = [near, term, turned, *direct[2], *forwards[2]]
    out, token = call(
        functools.partial(far_kernel, count, starts[2]),
        mib=16,
        in_specs=[VMEM] * len(operands) + [HBM, ANY],
        out_specs=[HBM, VMEM],
        out_shape=[whole_shape, jax.ShapeDtypeStruct((8, 128), f32)],
        scratch_shapes=[pltpu.VMEM((rows - starts[2], features), bf16), pltpu.SemaphoreType.DMA],
        input_output_aliases={len(operands): 0},
    )(*operands, out, tick(held, terms[second[-1]]))
    maps_shape = jax.ShapeDtypeStruct((rank, features), bf16)
    down_grad, up_grad = call(
        functools.partial(final_kernel, n, (stored / rows) ** 0.5),
        in_specs=[VMEM] * n + [ANY],
        out_specs=[VMEM] * 2,
        out_shape=[maps_shape] * 2,
    )(terms[0], *[arrived[k] for k in range(1, n)], token)
    down_grad = jnp.swapaxes(down_grad.reshape(stored, rank, features), 1, 2)
    up_grad = up_grad.reshape(stored, rank, features)
    return (out, down_grad, up_grad)


def solution(mesh):
    return jax.shard_map(
        on_device,
        mesh=mesh,
        in_specs=(
            P(("groups", "adapter"), ("tensor", "sub")),
            P(("groups", "adapter"), ("tensor", "sub")),
            P(("tensor", "sub"), None),
            P(("groups", "adapter"), ("tensor", "sub"), None),
            P(("groups", "adapter"), None, ("tensor", "sub")),
            P("groups"),
            P("groups"),
            P("groups"),
        ),
        out_specs=(
            P(("groups", "adapter"), ("tensor", "sub")),
            P(("groups", "adapter"), ("tensor", "sub"), None),
            P(("groups", "adapter"), None, ("tensor", "sub")),
        ),
        check_vma=False,
    )
```

```python
import functools

import jax
import jax.numpy as jnp
from jax import lax
from jax.experimental import pallas as pl
from jax.experimental.pallas import tpu as pltpu
from jax.sharding import PartitionSpec as P

TILE = 128
HEAVY = 1 << 33
CHUNKS = (3, 4, 4, 5)
FIRST = 2
NT = (((1,), (1,)), ((), ()))
SMEM = pl.BlockSpec(memory_space=pltpu.SMEM)
VMEM = pl.BlockSpec(memory_space=pltpu.VMEM)
ANY = pl.BlockSpec(memory_space=pl.ANY)
HBM = pl.BlockSpec(memory_space=pltpu.HBM)


def shift(array, axis, size, by):
    return lax.ppermute(array, axis, [(i, (i + by) % size) for i in range(size)])


def call(body, mib=12, flops=0, **kwargs):
    params = pltpu.CompilerParams(vmem_limit_bytes=mib * 1024 * 1024)
    cost = pl.CostEstimate(flops=flops, bytes_accessed=0, transcendentals=0)
    name = getattr(body, "func", body).__name__
    return pl.pallas_call(body, compiler_params=params, cost_estimate=cost, name=name, **kwargs)


def dot(a, b, dims=(((1,), (0,)), ((), ()))):
    return lax.dot_general(a, b, dims, preferred_element_type=jnp.float32)


def tile_rows(index):
    return pl.ds(pl.multiple_of(index * TILE, TILE), TILE)


def slot_rows(data, tile, entries):
    return jnp.concatenate([data[tile_rows(tile[e]), :] for e in entries], axis=0)


def copy_all(pairs, sems):
    copies = [pltpu.make_async_copy(a, b, sems.at[i]) for i, (a, b) in enumerate(pairs)]
    for copy in copies:
        copy.start()
    return copies


def head_kernel(cot, down, up, *refs):
    *parts, pack, again, held, pack_held, sems = refs
    rank, rows, start = down.shape[0], [], 0
    for part in parts:
        rows.append(pl.ds(start, part.shape[0]))
        start += part.shape[0]
    pairs = [(cot.at[r, :], held.at[r, :]) for r in rows]
    pairs += [(down, pack_held.at[pl.ds(0, rank), :]), (up, pack_held.at[pl.ds(rank, rank), :])]
    loads = copy_all(pairs, sems.at[0])
    stores = []
    for i, part in enumerate(parts):
        loads[i].wait()
        stores.append(pltpu.make_async_copy(held.at[rows[i], :], part, sems.at[1, i]))
        stores[-1].start()
    for load in loads[-2:]:
        load.wait()
    stores += copy_all([(pack_held, pack), (pack_held, again)], sems.at[2])
    for store in stores:
        store.wait()


def plan_kernel(n, cap, tiles, ids, live_all, stored, me, own, tile, live, *refs):
    *parts, count = refs
    start = own.shape[0] - sum(part.shape[0] for part in parts)
    for part in parts:
        part[...] = own[start : start + part.shape[0], :]
        start += part.shape[0]
    for k in range(n):
        count[k] = 0
    for e in range(n * cap):
        tile[e] = 0
        live[e] = 0
    for t in range(tiles):
        at = me[0] * tiles + t
        k = lax.rem(me[0] - stored[ids[at]] + n, n)
        e = jnp.minimum(k * cap + count[k], n * cap - 1)
        tile[e] = t
        live[e] = live_all[at]
        count[k] = count[k] + 1


def rank_kernel(slots, cap, tile, live, act, cot, *refs):
    packs, out = refs[: len(slots)], refs[-1]
    width = packs[0].shape[0]
    part = lax.broadcasted_iota(jnp.int32, packs[0].shape, 0) < width // 2
    row = lax.broadcasted_iota(jnp.int32, (TILE, width), 0)
    for i, (slot, pack) in enumerate(zip(slots, packs)):
        entries = range(slot * cap, (slot + 1) * cap)
        maps = pack[...]
        zero = jnp.zeros_like(maps)
        both = dot(slot_rows(act, tile, entries), jnp.where(part, maps, zero), NT)
        both += dot(slot_rows(cot, tile, entries), jnp.where(part, zero, maps), NT)
        for c, e in enumerate(entries):
            at = (i * cap + c) * TILE
            out[at : at + TILE, :] = jnp.where(
                row < live[e], both[c * TILE : (c + 1) * TILE], 0.0
            ).astype(jnp.bfloat16)


def sum_kernel(count, place, *refs):
    total = refs[0][...].astype(jnp.float32)
    for x in refs[1:count]:
        total += x[...].astype(jnp.float32)
    out = refs[place]
    out[...] = total.astype(out.dtype)


def gate_kernel(*refs):
    pass


def tick_kernel(*refs):
    refs[-1][...] = jnp.zeros_like(refs[-1])


def terms_kernel(slots, cap, tile, held, act, cot, *refs):
    terms = refs[-len(slots) :]
    rank = held.shape[1] // 2
    for i, slot in enumerate(slots):
        entries = range(slot * cap, (slot + 1) * cap)
        both = held[i * cap * TILE : (i + 1) * cap * TILE, :].astype(jnp.float32)
        both = both.T.astype(jnp.bfloat16)
        terms[i][:rank, :] = dot(both[rank:], slot_rows(act, tile, entries)).astype(jnp.bfloat16)
        terms[i][rank:, :] = dot(both[:rank], slot_rows(cot, tile, entries)).astype(jnp.bfloat16)


def weight_columns(weight, place):
    features = weight.shape[0]
    return weight[:, pl.ds(pl.multiple_of(place * features, 128), features)]


def near_kernel(which, place, data, weight, *refs):
    total = dot(data[...], weight_columns(weight, place[which]), NT)
    refs[-1][...] = total if which == 0 else refs[0][...] + total


def turn_kernel(place, weight, out):
    features = weight.shape[0]
    for i in range(out.shape[0] // features):
        out[i * features : (i + 1) * features, :] = weight_columns(weight, place[2 + i]).T


def row_sums(start, count, near, term, turned, blocks, out, done, sem):
    at = 0
    for first in range(0, len(blocks), count):
        extent = blocks[first].shape[0]
        rows = slice(start + at, start + at + extent)
        total = near[rows, :] + term[rows, :].astype(jnp.float32)
        for i in range(count):
            features = turned.shape[1]
            total += dot(blocks[first + i][...], turned[i * features : (i + 1) * features, :])
        done[at : at + extent, :] = total.astype(jnp.bfloat16)
        at += extent
    copy = pltpu.make_async_copy(done, out.at[pl.ds(start, at), :], sem)
    copy.start()
    copy.wait()


def middle_kernel(groups, cap, count, tile, *refs):
    n = sum(len(g) for g in groups)
    blocks, refs = refs[: 3 * count], refs[3 * count :]
    sums, refs = refs[: len(groups)], refs[len(groups) :]
    packs, (near, turned), refs = refs[:n], refs[n : n + 2], refs[n + 2 :]
    out, term, done, sem = refs[-4:]
    term[...] = jnp.zeros_like(term)
    for g, slots in enumerate(groups):
        for i, slot in enumerate(slots):
            maps = packs[slot][...]
            rank = maps.shape[0] // 2
            maps = jnp.concatenate([jnp.zeros_like(maps[:rank]), maps[:rank]], axis=0)
            found = dot(sums[g][i * cap * TILE : (i + 1) * cap * TILE, :], maps)
            for c in range(cap):
                rows = tile_rows(tile[slot * cap + c])
                before = term[rows, :].astype(jnp.float32)
                term[rows, :] = (before + found[c * TILE : (c + 1) * TILE]).astype(term.dtype)
    row_sums(0, count, near, term, turned, blocks, out, done, sem)


def far_kernel(count, start, near, term, turned, *refs):
    out, token, done, sem = refs[-4:]
    token[...] = jnp.zeros_like(token)
    row_sums(start, count, near, term, turned, refs[:count], out, done, sem)


def final_kernel(count, scale, *refs):
    down, up = refs[-2:]
    rank = down.shape[0]
    for out, rows in ((down, slice(0, rank)), (up, slice(rank, 2 * rank))):
        total = refs[0][rows, :].astype(jnp.float32)
        for x in refs[1:count]:
            total += x[rows, :].astype(jnp.float32)
        out[...] = (total * scale).astype(out.dtype)


def on_device(
    activations,
    cotangent,
    frozen_weight,
    adapter_down_maps,
    adapter_up_maps,
    adapter_per_tile,
    live_per_tile,
    adapter_stored_row,
):
    rows, features = activations.shape
    tiles = rows // TILE
    stored, _, rank = adapter_down_maps.shape
    n = lax.axis_size("adapter")
    tensors = lax.axis_size("tensor")
    subs = lax.axis_size("sub")
    me = lax.axis_index("adapter")
    t_me, s_me = lax.axis_index("tensor"), lax.axis_index("sub")
    extents = [rows * c // sum(CHUNKS) for c in CHUNKS]
    starts = [sum(extents[:c]) for c in range(len(extents))]
    bf16, f32 = jnp.bfloat16, jnp.float32

    cap = -(-tiles // n)
    places = [t_me * subs + s_me, t_me * subs + (1 - s_me)]
    for s in (s_me, 1 - s_me):
        places += [jnp.remainder(t_me - k, tensors) * subs + s for k in range(1, tensors)]
    place = jnp.stack(places).astype(jnp.int32)

    groups = [[k for k in range(n) if 1 <= min(k, n - k) <= n // 4]]
    groups.append([k for k in range(n) if k not in groups[0]])

    down = jnp.swapaxes(adapter_down_maps, 1, 2).reshape(stored * rank, features)
    up = adapter_up_maps.reshape(stored * rank, features)
    pack_shape = jax.ShapeDtypeStruct((2 * rank, features), bf16)
    *parts, pack, pack_again = call(
        head_kernel,
        mib=56,
        in_specs=[ANY] * 3,
        out_specs=[ANY] * (FIRST + 2),
        out_shape=[jax.ShapeDtypeStruct((e, features), bf16) for e in extents[:FIRST]]
        + [pack_shape] * 2,
        scratch_shapes=[
            pltpu.VMEM((starts[FIRST], features), bf16),
            pltpu.VMEM(pack_shape.shape, bf16),
            pltpu.SemaphoreType.DMA((3, FIRST + 2)),
        ],
    )(cotangent, down, up)
    def across(part, aside=0):
        slice_axes, found = ("tensor", "sub"), []
        for k in range(1, tensors):
            to = [(t + k) % tensors * subs + (s + aside) % subs for t in range(tensors) for s in range(subs)]
            found.append(lax.ppermute(part, slice_axes, list(enumerate(to))))
        return found

    def forward(blocks):
        return [shift(x, "sub", subs, 1) for x in blocks]

    direct = [across(part) for part in parts]
    pair = shift(cotangent, "sub", subs, 1)
    table = jax.ShapeDtypeStruct((n * cap,), jnp.int32)
    later = [jax.ShapeDtypeStruct((e, features), bf16) for e in extents[FIRST:]]
    tile, live, *rest = call(
        functools.partial(plan_kernel, n, cap, tiles),
        in_specs=[SMEM] * 4 + [VMEM],
        out_specs=[SMEM] * 2 + [VMEM] * len(later),
        out_shape=[table] * 2 + later,
        scratch_shapes=[pltpu.SMEM((n,), jnp.int32)],
    )(adapter_per_tile, live_per_tile, adapter_stored_row, me.astype(jnp.int32).reshape(1), cotangent)
    parts = [*parts, *rest]

    def after(arrays):
        return [ANY] * len(arrays)

    def gate(blocks, ready):
        found = call(
            gate_kernel,
            in_specs=after(blocks) + [ANY],
            out_specs=after(blocks),
            out_shape=[jax.ShapeDtypeStruct(x.shape, x.dtype) for x in blocks],
            input_output_aliases={i: i for i in range(len(blocks))},
        )(*blocks, ready)
        return list(found)

    def near_part(which, data, ready, *before):
        return call(
            functools.partial(near_kernel, which),
            flops=HEAVY,
            in_specs=[SMEM] + [VMEM] * (2 + len(before)) + [ANY],
            out_specs=VMEM,
            out_shape=jax.ShapeDtypeStruct((rows, features), f32),
            input_output_aliases={3: 0} if before else {},
        )(place, data, frozen_weight, *before, ready)

    def tick(*ready):
        return call(
            tick_kernel,
            flops=HEAVY,
            in_specs=after(ready),
            out_specs=VMEM,
            out_shape=jax.ShapeDtypeStruct((8, 128), f32),
        )(*ready)

    def ranks(g, *wait):
        return call(
            functools.partial(rank_kernel, g, cap),
            in_specs=[SMEM] * 2 + [VMEM] * (2 + len(g)) + after(wait),
            out_specs=VMEM,
            out_shape=jax.ShapeDtypeStruct((len(g) * cap * TILE, 2 * rank), bf16),
        )(tile, live, activations, cotangent, *[packs[k] for k in g], *wait)

    def chip_sum(own, *wait):
        given = shift(own, "sub", subs, 1)
        sent = call(
            functools.partial(sum_kernel, 2, -1),
            in_specs=[VMEM] * 2 + after(wait),
            out_specs=VMEM,
            out_shape=jax.ShapeDtypeStruct(own.shape, bf16),
        )(own, given, *wait)
        return given, sent

    def slice_sum(own, given, others, held_parts, *wait):
        found = [own, given, *others]
        shapes = [jax.ShapeDtypeStruct(x.shape, x.dtype) for x in held_parts]
        return call(
            functools.partial(sum_kernel, len(found), -1 - len(shapes)),
            in_specs=[VMEM] * len(found) + after(held_parts) + after(wait),
            out_specs=[VMEM] + after(held_parts),
            out_shape=[jax.ShapeDtypeStruct(own.shape, bf16)] + shapes,
            input_output_aliases={len(found) + i: 1 + i for i in range(len(shapes))},
        )(*found, *held_parts, *wait)

    def adapter_terms(g, held, *wait):
        found = call(
            functools.partial(terms_kernel, g, cap),
            in_specs=[SMEM] + [VMEM] * 3 + after(wait),
            out_specs=[VMEM] * len(g),
            out_shape=[jax.ShapeDtypeStruct((2 * rank, features), bf16)] * len(g),
        )(tile, held, activations, cotangent, *wait)
        return dict(zip(g, found))

    first, second = groups
    packs = {0: pack} | {k: shift(pack, "adapter", n, k) for k in first}
    (pack_again,) = gate([pack_again], tile)
    packs |= {k: shift(pack_again, "adapter", n, k) for k in second if k}

    forwards = [forward(direct[0])]
    turned = call(
        turn_kernel,
        in_specs=[SMEM, VMEM],
        out_specs=VMEM,
        out_shape=jax.ShapeDtypeStruct((2 * (tensors - 1) * features, features), bf16),
    )(place, frozen_weight)
    own = ranks(first, tick(*direct[0], pair, turned))
    given, sent = chip_sum(own, tick(own), *forwards[0])
    mark = tick(sent)
    opened = gate([parts[2]], mark)
    direct.append(across(*opened))
    near = near_part(0, cotangent, opened[0])
    (held,) = slice_sum(own, given, across(sent), [], near)
    direct[1] = gate(direct[1], held)
    forwards.insert(1, forward(direct[1]))
    sums = [held]
    own = ranks(second, held)
    terms = adapter_terms(first, held, own)
    given, sent = chip_sum(own, tick(own), terms[first[0]], *forwards[1])
    mark = tick(sent)
    leaving = gate([terms[k] for k in first], mark)
    arrived = {k: shift(x, "adapter", n, -k) for k, x in zip(first, leaving)}
    direct.append(across(*gate([parts[3]], mark)))
    near = near_part(1, pair, mark, near)
    (held,) = slice_sum(own, given, across(sent), [], near)
    sums.append(held)
    terms |= adapter_terms(second, held)
    arrived |= {k: shift(terms[k], "adapter", n, -k) for k in second if k}
    direct[2] = gate(direct[2], held)
    forwards.append(forward(direct[2]))

    blocks = [x for c in range(3) for x in direct[c] + forwards[c]]
    count = len(blocks) // 3
    operands = [tile, *blocks, *sums, *[packs[k] for k in range(n)], near, turned]
    whole_shape = jax.ShapeDtypeStruct((rows, features), bf16)
    out, term = call(
        functools.partial(middle_kernel, groups, cap, count),
        mib=20,
        flops=HEAVY,
        in_specs=[SMEM] + [VMEM] * (len(operands) - 1) + [ANY] * 2,
        out_specs=[HBM, VMEM],
        out_shape=[whole_shape] * 2,
        scratch_shapes=[pltpu.VMEM((starts[3], features), bf16), pltpu.SemaphoreType.DMA],
    )(*operands, terms[second[-1]], tick(held))
    direct[3] = gate(direct[3], term)
    forwards.append(forward(direct[3]))
    operands = [near, term, turned, *direct[3], *forwards[3]]
    out, token = call(
        functools.partial(far_kernel, count, starts[3]),
        mib=16,
        in_specs=[VMEM] * len(operands) + [HBM, ANY],
        out_specs=[HBM, VMEM],
        out_shape=[whole_shape, jax.ShapeDtypeStruct((8, 128), f32)],
        scratch_shapes=[pltpu.VMEM((rows - starts[3], features), bf16), pltpu.SemaphoreType.DMA],
        input_output_aliases={len(operands): 0},
    )(*operands, out, tick(held, terms[second[-1]]))
    maps_shape = jax.ShapeDtypeStruct((rank, features), bf16)
    down_grad, up_grad = call(
        functools.partial(final_kernel, n, (stored / rows) ** 0.5),
        in_specs=[VMEM] * n + [ANY],
        out_specs=[VMEM] * 2,
        out_shape=[maps_shape] * 2,
    )(terms[0], *[arrived[k] for k in range(1, n)], token)
    down_grad = jnp.swapaxes(down_grad.reshape(stored, rank, features), 1, 2)
    up_grad = up_grad.reshape(stored, rank, features)
    return (out, down_grad, up_grad)


def solution(mesh):
    return jax.shard_map(
        on_device,
        mesh=mesh,
        in_specs=(
            P(("groups", "adapter"), ("tensor", "sub")),
            P(("groups", "adapter"), ("tensor", "sub")),
            P(("tensor", "sub"), None),
            P(("groups", "adapter"), ("tensor", "sub"), None),
            P(("groups", "adapter"), None, ("tensor", "sub")),
            P("groups"),
            P("groups"),
            P("groups"),
        ),
        out_specs=(
            P(("groups", "adapter"), ("tensor", "sub")),
            P(("groups", "adapter"), ("tensor", "sub"), None),
            P(("groups", "adapter"), None, ("tensor", "sub")),
        ),
        check_vma=False,
    )
```

```python
import functools

import jax
import jax.numpy as jnp
from jax import lax
from jax.experimental import pallas as pl
from jax.experimental.pallas import tpu as pltpu
from jax.sharding import PartitionSpec as P

TILE = 128
HEAVY = 1 << 33
CHUNKS = (3, 4, 4, 5)
FIRST = 2
NT = (((1,), (1,)), ((), ()))
SMEM = pl.BlockSpec(memory_space=pltpu.SMEM)
VMEM = pl.BlockSpec(memory_space=pltpu.VMEM)
ANY = pl.BlockSpec(memory_space=pl.ANY)
HBM = pl.BlockSpec(memory_space=pltpu.HBM)


def shift(array, axis, size, by):
    return lax.ppermute(array, axis, [(i, (i + by) % size) for i in range(size)])


def call(body, mib=12, flops=0, **kwargs):
    params = pltpu.CompilerParams(vmem_limit_bytes=mib * 1024 * 1024)
    cost = pl.CostEstimate(flops=flops, bytes_accessed=0, transcendentals=0)
    name = getattr(body, "func", body).__name__
    return pl.pallas_call(body, compiler_params=params, cost_estimate=cost, name=name, **kwargs)


def dot(a, b, dims=(((1,), (0,)), ((), ()))):
    return lax.dot_general(a, b, dims, preferred_element_type=jnp.float32)


def tile_rows(index):
    return pl.ds(pl.multiple_of(index * TILE, TILE), TILE)


def slot_rows(data, tile, entries):
    return jnp.concatenate([data[tile_rows(tile[e]), :] for e in entries], axis=0)


def copy_all(pairs, sems):
    copies = [pltpu.make_async_copy(a, b, sems.at[i]) for i, (a, b) in enumerate(pairs)]
    for copy in copies:
        copy.start()
    return copies


def head_kernel(cot, down, up, *refs):
    *parts, pack, again, held, pack_held, sems = refs
    rank, rows, start = down.shape[0], [], 0
    for part in parts:
        rows.append(pl.ds(start, part.shape[0]))
        start += part.shape[0]
    pairs = [(cot.at[r, :], held.at[r, :]) for r in rows]
    pairs += [(down, pack_held.at[pl.ds(0, rank), :]), (up, pack_held.at[pl.ds(rank, rank), :])]
    loads = copy_all(pairs, sems.at[0])
    stores = []
    for i, part in enumerate(parts):
        loads[i].wait()
        stores.append(pltpu.make_async_copy(held.at[rows[i], :], part, sems.at[1, i]))
        stores[-1].start()
    for load in loads[-2:]:
        load.wait()
    stores += copy_all([(pack_held, pack), (pack_held, again)], sems.at[2])
    for store in stores:
        store.wait()


def plan_kernel(n, cap, tiles, ids, live_all, stored, me, own, tile, live, *refs):
    *parts, count = refs
    start = own.shape[0] - sum(part.shape[0] for part in parts)
    for part in parts:
        part[...] = own[start : start + part.shape[0], :]
        start += part.shape[0]
    for k in range(n):
        count[k] = 0
    for e in range(n * cap):
        tile[e] = 0
        live[e] = 0
    for t in range(tiles):
        at = me[0] * tiles + t
        k = lax.rem(me[0] - stored[ids[at]] + n, n)
        e = jnp.minimum(k * cap + count[k], n * cap - 1)
        tile[e] = t
        live[e] = live_all[at]
        count[k] = count[k] + 1


def rank_kernel(slots, cap, tile, live, act, cot, *refs):
    packs, out = refs[: len(slots)], refs[-1]
    width = packs[0].shape[0]
    part = lax.broadcasted_iota(jnp.int32, packs[0].shape, 0) < width // 2
    row = lax.broadcasted_iota(jnp.int32, (TILE, width), 0)
    for i, (slot, pack) in enumerate(zip(slots, packs)):
        entries = range(slot * cap, (slot + 1) * cap)
        maps = pack[...]
        zero = jnp.zeros_like(maps)
        both = dot(slot_rows(act, tile, entries), jnp.where(part, maps, zero), NT)
        both += dot(slot_rows(cot, tile, entries), jnp.where(part, zero, maps), NT)
        for c, e in enumerate(entries):
            at = (i * cap + c) * TILE
            out[at : at + TILE, :] = jnp.where(
                row < live[e], both[c * TILE : (c + 1) * TILE], 0.0
            ).astype(jnp.bfloat16)


def sum_kernel(count, place, *refs):
    total = refs[0][...].astype(jnp.float32)
    for x in refs[1:count]:
        total += x[...].astype(jnp.float32)
    out = refs[place]
    out[...] = total.astype(out.dtype)


def gate_kernel(*refs):
    pass


def tick_kernel(*refs):
    refs[-1][...] = jnp.zeros_like(refs[-1])


def terms_kernel(slots, cap, tile, held, act, cot, *refs):
    terms = refs[-len(slots) :]
    rank = held.shape[1] // 2
    for i, slot in enumerate(slots):
        entries = range(slot * cap, (slot + 1) * cap)
        both = held[i * cap * TILE : (i + 1) * cap * TILE, :].astype(jnp.float32)
        both = both.T.astype(jnp.bfloat16)
        terms[i][:rank, :] = dot(both[rank:], slot_rows(act, tile, entries)).astype(jnp.bfloat16)
        terms[i][rank:, :] = dot(both[:rank], slot_rows(cot, tile, entries)).astype(jnp.bfloat16)


def weight_columns(weight, place):
    features = weight.shape[0]
    return weight[:, pl.ds(pl.multiple_of(place * features, 128), features)]


def near_kernel(which, place, data, weight, *refs):
    total = dot(data[...], weight_columns(weight, place[which]), NT)
    refs[-1][...] = total if which == 0 else refs[0][...] + total


def turn_kernel(place, weight, out):
    features = weight.shape[0]
    for i in range(out.shape[0] // features):
        out[i * features : (i + 1) * features, :] = weight_columns(weight, place[2 + i]).T


def row_sums(start, count, near, term, turned, blocks, out, done, sem):
    at = 0
    for first in range(0, len(blocks), count):
        extent = blocks[first].shape[0]
        rows = slice(start + at, start + at + extent)
        total = near[rows, :] + term[rows, :].astype(jnp.float32)
        for i in range(count):
            features = turned.shape[1]
            total += dot(blocks[first + i][...], turned[i * features : (i + 1) * features, :])
        done[at : at + extent, :] = total.astype(jnp.bfloat16)
        at += extent
    copy = pltpu.make_async_copy(done, out.at[pl.ds(start, at), :], sem)
    copy.start()
    copy.wait()


def middle_kernel(groups, cap, count, tile, *refs):
    n = sum(len(g) for g in groups)
    blocks, refs = refs[: 3 * count], refs[3 * count :]
    sums, refs = refs[: len(groups)], refs[len(groups) :]
    packs, (near, turned), refs = refs[:n], refs[n : n + 2], refs[n + 2 :]
    out, term, done, sem = refs[-4:]
    term[...] = jnp.zeros_like(term)
    for g, slots in enumerate(groups):
        for i, slot in enumerate(slots):
            maps = packs[slot][...]
            rank = maps.shape[0] // 2
            maps = jnp.concatenate([jnp.zeros_like(maps[:rank]), maps[:rank]], axis=0)
            found = dot(sums[g][i * cap * TILE : (i + 1) * cap * TILE, :], maps)
            for c in range(cap):
                rows = tile_rows(tile[slot * cap + c])
                before = term[rows, :].astype(jnp.float32)
                term[rows, :] = (before + found[c * TILE : (c + 1) * TILE]).astype(term.dtype)
    row_sums(0, count, near, term, turned, blocks, out, done, sem)


def far_kernel(count, start, near, term, turned, *refs):
    out, token, done, sem = refs[-4:]
    token[...] = jnp.zeros_like(token)
    row_sums(start, count, near, term, turned, refs[:count], out, done, sem)


def final_kernel(count, scale, *refs):
    down, up = refs[-2:]
    rank = down.shape[0]
    for out, rows in ((down, slice(0, rank)), (up, slice(rank, 2 * rank))):
        total = refs[0][rows, :].astype(jnp.float32)
        for x in refs[1:count]:
            total += x[rows, :].astype(jnp.float32)
        out[...] = (total * scale).astype(out.dtype)


def on_device(
    activations,
    cotangent,
    frozen_weight,
    adapter_down_maps,
    adapter_up_maps,
    adapter_per_tile,
    live_per_tile,
    adapter_stored_row,
):
    rows, features = activations.shape
    tiles = rows // TILE
    stored, _, rank = adapter_down_maps.shape
    n = lax.axis_size("adapter")
    tensors = lax.axis_size("tensor")
    subs = lax.axis_size("sub")
    me = lax.axis_index("adapter")
    t_me, s_me = lax.axis_index("tensor"), lax.axis_index("sub")
    extents = [rows * c // sum(CHUNKS) for c in CHUNKS]
    starts = [sum(extents[:c]) for c in range(len(extents))]
    bf16, f32 = jnp.bfloat16, jnp.float32

    cap = -(-tiles // n)
    places = [t_me * subs + s_me, t_me * subs + (1 - s_me)]
    for s in (s_me, 1 - s_me):
        places += [jnp.remainder(t_me - k, tensors) * subs + s for k in range(1, tensors)]
    place = jnp.stack(places).astype(jnp.int32)

    groups = [[k for k in range(n) if 1 <= min(k, n - k) <= n // 4]]
    groups.append([k for k in range(n) if k not in groups[0]])

    down = jnp.swapaxes(adapter_down_maps, 1, 2).reshape(stored * rank, features)
    up = adapter_up_maps.reshape(stored * rank, features)
    pack_shape = jax.ShapeDtypeStruct((2 * rank, features), bf16)
    *parts, pack, pack_again = call(
        head_kernel,
        mib=56,
        in_specs=[ANY] * 3,
        out_specs=[ANY] * (FIRST + 2),
        out_shape=[jax.ShapeDtypeStruct((e, features), bf16) for e in extents[:FIRST]]
        + [pack_shape] * 2,
        scratch_shapes=[
            pltpu.VMEM((starts[FIRST], features), bf16),
            pltpu.VMEM(pack_shape.shape, bf16),
            pltpu.SemaphoreType.DMA((3, FIRST + 2)),
        ],
    )(cotangent, down, up)
    def across(part, aside=0):
        slice_axes, found = ("tensor", "sub"), []
        for k in range(1, tensors):
            to = [(t + k) % tensors * subs + (s + aside) % subs for t in range(tensors) for s in range(subs)]
            found.append(lax.ppermute(part, slice_axes, list(enumerate(to))))
        return found

    def forward(blocks):
        return [shift(x, "sub", subs, 1) for x in blocks]

    direct = [across(part) for part in parts]
    pair = shift(cotangent, "sub", subs, 1)
    table = jax.ShapeDtypeStruct((n * cap,), jnp.int32)
    later = [jax.ShapeDtypeStruct((e, features), bf16) for e in extents[FIRST:]]
    tile, live, *rest = call(
        functools.partial(plan_kernel, n, cap, tiles),
        in_specs=[SMEM] * 4 + [VMEM],
        out_specs=[SMEM] * 2 + [VMEM] * len(later),
        out_shape=[table] * 2 + later,
        scratch_shapes=[pltpu.SMEM((n,), jnp.int32)],
    )(adapter_per_tile, live_per_tile, adapter_stored_row, me.astype(jnp.int32).reshape(1), cotangent)
    parts = [*parts, *rest]

    def after(arrays):
        return [ANY] * len(arrays)

    def gate(blocks, ready):
        found = call(
            gate_kernel,
            in_specs=after(blocks) + [ANY],
            out_specs=after(blocks),
            out_shape=[jax.ShapeDtypeStruct(x.shape, x.dtype) for x in blocks],
            input_output_aliases={i: i for i in range(len(blocks))},
        )(*blocks, ready)
        return list(found)

    def near_part(which, data, ready, *before):
        return call(
            functools.partial(near_kernel, which),
            flops=which * HEAVY,
            in_specs=[SMEM] + [VMEM] * (2 + len(before)) + [ANY],
            out_specs=VMEM,
            out_shape=jax.ShapeDtypeStruct((rows, features), f32),
            input_output_aliases={3: 0} if before else {},
        )(place, data, frozen_weight, *before, ready)

    def tick(*ready):
        return call(
            tick_kernel,
            flops=HEAVY,
            in_specs=after(ready),
            out_specs=VMEM,
            out_shape=jax.ShapeDtypeStruct((8, 128), f32),
        )(*ready)

    def ranks(g, *wait):
        return call(
            functools.partial(rank_kernel, g, cap),
            in_specs=[SMEM] * 2 + [VMEM] * (2 + len(g)) + after(wait),
            out_specs=VMEM,
            out_shape=jax.ShapeDtypeStruct((len(g) * cap * TILE, 2 * rank), bf16),
        )(tile, live, activations, cotangent, *[packs[k] for k in g], *wait)

    def chip_sum(own, *wait):
        given = shift(own, "sub", subs, 1)
        sent = call(
            functools.partial(sum_kernel, 2, -1),
            in_specs=[VMEM] * 2 + after(wait),
            out_specs=VMEM,
            out_shape=jax.ShapeDtypeStruct(own.shape, bf16),
        )(own, given, *wait)
        return given, sent

    def slice_sum(own, given, others, held_parts, *wait):
        found = [own, given, *others]
        shapes = [jax.ShapeDtypeStruct(x.shape, x.dtype) for x in held_parts]
        return call(
            functools.partial(sum_kernel, len(found), -1 - len(shapes)),
            in_specs=[VMEM] * len(found) + after(held_parts) + after(wait),
            out_specs=[VMEM] + after(held_parts),
            out_shape=[jax.ShapeDtypeStruct(own.shape, bf16)] + shapes,
            input_output_aliases={len(found) + i: 1 + i for i in range(len(shapes))},
        )(*found, *held_parts, *wait)

    def adapter_terms(g, held, *wait):
        found = call(
            functools.partial(terms_kernel, g, cap),
            in_specs=[SMEM] + [VMEM] * 3 + after(wait),
            out_specs=[VMEM] * len(g),
            out_shape=[jax.ShapeDtypeStruct((2 * rank, features), bf16)] * len(g),
        )(tile, held, activations, cotangent, *wait)
        return dict(zip(g, found))

    first, second = groups
    packs = {0: pack} | {k: shift(pack, "adapter", n, k) for k in first}
    (pack_again,) = gate([pack_again], tile)
    packs |= {k: shift(pack_again, "adapter", n, k) for k in second if k}

    forwards = [forward(direct[0])]
    turned = call(
        turn_kernel,
        in_specs=[SMEM, VMEM],
        out_specs=VMEM,
        out_shape=jax.ShapeDtypeStruct((2 * (tensors - 1) * features, features), bf16),
    )(place, frozen_weight)
    near = near_part(0, cotangent, direct[0][0])
    own = ranks(first, tick(pair, near, turned))
    given, sent = chip_sum(own, tick(own), *forwards[0])
    mark = tick(sent)
    opened = gate([parts[2]], mark)
    direct.append(across(*opened))
    near = near_part(1, pair, opened[0], near)
    (held,) = slice_sum(own, given, across(sent), [], near)
    direct[1] = gate(direct[1], held)
    forwards.insert(1, forward(direct[1]))
    sums = [held]
    own = ranks(second, held)
    terms = adapter_terms(first, held, own)
    given, sent = chip_sum(own, tick(own), terms[first[0]], *forwards[1])
    mark = tick(sent)
    leaving = gate([terms[k] for k in first], mark)
    arrived = {k: shift(x, "adapter", n, -k) for k, x in zip(first, leaving)}
    direct.append(across(*gate([parts[3]], mark)))
    (held,) = slice_sum(own, given, across(sent), [], mark)
    sums.append(held)
    terms |= adapter_terms(second, held)
    arrived |= {k: shift(terms[k], "adapter", n, -k) for k in second if k}
    direct[2] = gate(direct[2], held)
    forwards.append(forward(direct[2]))

    blocks = [x for c in range(3) for x in direct[c] + forwards[c]]
    count = len(blocks) // 3
    operands = [tile, *blocks, *sums, *[packs[k] for k in range(n)], near, turned]
    whole_shape = jax.ShapeDtypeStruct((rows, features), bf16)
    out, term = call(
        functools.partial(middle_kernel, groups, cap, count),
        mib=20,
        flops=HEAVY,
        in_specs=[SMEM] + [VMEM] * (len(operands) - 1) + [ANY] * 2,
        out_specs=[HBM, VMEM],
        out_shape=[whole_shape] * 2,
        scratch_shapes=[pltpu.VMEM((starts[3], features), bf16), pltpu.SemaphoreType.DMA],
    )(*operands, terms[second[-1]], tick(held))
    direct[3] = gate(direct[3], term)
    forwards.append(forward(direct[3]))
    operands = [near, term, turned, *direct[3], *forwards[3]]
    out, token = call(
        functools.partial(far_kernel, count, starts[3]),
        mib=16,
        in_specs=[VMEM] * len(operands) + [HBM, ANY],
        out_specs=[HBM, VMEM],
        out_shape=[whole_shape, jax.ShapeDtypeStruct((8, 128), f32)],
        scratch_shapes=[pltpu.VMEM((rows - starts[3], features), bf16), pltpu.SemaphoreType.DMA],
        input_output_aliases={len(operands): 0},
    )(*operands, out, tick(held, terms[second[-1]]))
    maps_shape = jax.ShapeDtypeStruct((rank, features), bf16)
    down_grad, up_grad = call(
        functools.partial(final_kernel, n, (stored / rows) ** 0.5),
        in_specs=[VMEM] * n + [ANY],
        out_specs=[VMEM] * 2,
        out_shape=[maps_shape] * 2,
    )(terms[0], *[arrived[k] for k in range(1, n)], token)
    down_grad = jnp.swapaxes(down_grad.reshape(stored, rank, features), 1, 2)
    up_grad = up_grad.reshape(stored, rank, features)
    return (out, down_grad, up_grad)


def solution(mesh):
    return jax.shard_map(
        on_device,
        mesh=mesh,
        in_specs=(
            P(("groups", "adapter"), ("tensor", "sub")),
            P(("groups", "adapter"), ("tensor", "sub")),
            P(("tensor", "sub"), None),
            P(("groups", "adapter"), ("tensor", "sub"), None),
            P(("groups", "adapter"), None, ("tensor", "sub")),
            P("groups"),
            P("groups"),
            P("groups"),
        ),
        out_specs=(
            P(("groups", "adapter"), ("tensor", "sub")),
            P(("groups", "adapter"), ("tensor", "sub"), None),
            P(("groups", "adapter"), None, ("tensor", "sub")),
        ),
        check_vma=False,
    )
```

```python
import functools

import jax
import jax.numpy as jnp
from jax import lax
from jax.experimental import pallas as pl
from jax.experimental.pallas import tpu as pltpu
from jax.sharding import PartitionSpec as P

TILE = 128
HEAVY = 1 << 33
CHUNKS = (3, 4, 3, 6)
FIRST = 2
NT = (((1,), (1,)), ((), ()))
SMEM = pl.BlockSpec(memory_space=pltpu.SMEM)
VMEM = pl.BlockSpec(memory_space=pltpu.VMEM)
ANY = pl.BlockSpec(memory_space=pl.ANY)
HBM = pl.BlockSpec(memory_space=pltpu.HBM)


def shift(array, axis, size, by):
    return lax.ppermute(array, axis, [(i, (i + by) % size) for i in range(size)])


def call(body, mib=12, flops=0, **kwargs):
    params = pltpu.CompilerParams(vmem_limit_bytes=mib * 1024 * 1024)
    cost = pl.CostEstimate(flops=flops, bytes_accessed=0, transcendentals=0)
    name = getattr(body, "func", body).__name__
    return pl.pallas_call(body, compiler_params=params, cost_estimate=cost, name=name, **kwargs)


def dot(a, b, dims=(((1,), (0,)), ((), ()))):
    return lax.dot_general(a, b, dims, preferred_element_type=jnp.float32)


def tile_rows(index):
    return pl.ds(pl.multiple_of(index * TILE, TILE), TILE)


def slot_rows(data, tile, entries):
    return jnp.concatenate([data[tile_rows(tile[e]), :] for e in entries], axis=0)


def copy_all(pairs, sems):
    copies = [pltpu.make_async_copy(a, b, sems.at[i]) for i, (a, b) in enumerate(pairs)]
    for copy in copies:
        copy.start()
    return copies


def head_kernel(cot, down, up, *refs):
    *parts, pack, again, held, pack_held, sems = refs
    rank, rows, start = down.shape[0], [], 0
    for part in parts:
        rows.append(pl.ds(start, part.shape[0]))
        start += part.shape[0]
    pairs = [(cot.at[r, :], held.at[r, :]) for r in rows]
    pairs += [(down, pack_held.at[pl.ds(0, rank), :]), (up, pack_held.at[pl.ds(rank, rank), :])]
    loads = copy_all(pairs, sems.at[0])
    stores = []
    for i, part in enumerate(parts):
        loads[i].wait()
        stores.append(pltpu.make_async_copy(held.at[rows[i], :], part, sems.at[1, i]))
        stores[-1].start()
    for load in loads[-2:]:
        load.wait()
    stores += copy_all([(pack_held, pack), (pack_held, again)], sems.at[2])
    for store in stores:
        store.wait()


def plan_kernel(n, cap, tiles, ids, live_all, stored, me, own, tile, live, *refs):
    *parts, count = refs
    start = own.shape[0] - sum(part.shape[0] for part in parts)
    for part in parts:
        part[...] = own[start : start + part.shape[0], :]
        start += part.shape[0]
    for k in range(n):
        count[k] = 0
    for e in range(n * cap):
        tile[e] = 0
        live[e] = 0
    for t in range(tiles):
        at = me[0] * tiles + t
        k = lax.rem(me[0] - stored[ids[at]] + n, n)
        e = jnp.minimum(k * cap + count[k], n * cap - 1)
        tile[e] = t
        live[e] = live_all[at]
        count[k] = count[k] + 1


def rank_kernel(slots, cap, tile, live, act, cot, *refs):
    packs, out = refs[: len(slots)], refs[-1]
    width = packs[0].shape[0]
    part = lax.broadcasted_iota(jnp.int32, packs[0].shape, 0) < width // 2
    row = lax.broadcasted_iota(jnp.int32, (TILE, width), 0)
    for i, (slot, pack) in enumerate(zip(slots, packs)):
        entries = range(slot * cap, (slot + 1) * cap)
        maps = pack[...]
        zero = jnp.zeros_like(maps)
        both = dot(slot_rows(act, tile, entries), jnp.where(part, maps, zero), NT)
        both += dot(slot_rows(cot, tile, entries), jnp.where(part, zero, maps), NT)
        for c, e in enumerate(entries):
            at = (i * cap + c) * TILE
            out[at : at + TILE, :] = jnp.where(
                row < live[e], both[c * TILE : (c + 1) * TILE], 0.0
            ).astype(jnp.bfloat16)


def sum_kernel(count, place, *refs):
    total = refs[0][...].astype(jnp.float32)
    for x in refs[1:count]:
        total += x[...].astype(jnp.float32)
    out = refs[place]
    out[...] = total.astype(out.dtype)


def gate_kernel(*refs):
    pass


def tick_kernel(*refs):
    refs[-1][...] = jnp.zeros_like(refs[-1])


def terms_kernel(slots, cap, tile, held, act, cot, *refs):
    terms = refs[-len(slots) :]
    rank = held.shape[1] // 2
    for i, slot in enumerate(slots):
        entries = range(slot * cap, (slot + 1) * cap)
        both = held[i * cap * TILE : (i + 1) * cap * TILE, :].astype(jnp.float32)
        both = both.T.astype(jnp.bfloat16)
        terms[i][:rank, :] = dot(both[rank:], slot_rows(act, tile, entries)).astype(jnp.bfloat16)
        terms[i][rank:, :] = dot(both[:rank], slot_rows(cot, tile, entries)).astype(jnp.bfloat16)


def weight_columns(weight, place):
    features = weight.shape[0]
    return weight[:, pl.ds(pl.multiple_of(place * features, 128), features)]


def near_kernel(which, place, data, weight, *refs):
    total = dot(data[...], weight_columns(weight, place[which]), NT)
    refs[-1][...] = total if which == 0 else refs[0][...] + total


def turn_kernel(place, weight, out):
    features = weight.shape[0]
    for i in range(out.shape[0] // features):
        out[i * features : (i + 1) * features, :] = weight_columns(weight, place[2 + i]).T


def row_sums(start, count, near, term, turned, blocks, out, done, sem):
    at = 0
    for first in range(0, len(blocks), count):
        extent = blocks[first].shape[0]
        rows = slice(start + at, start + at + extent)
        total = near[rows, :] + term[rows, :].astype(jnp.float32)
        for i in range(count):
            features = turned.shape[1]
            total += dot(blocks[first + i][...], turned[i * features : (i + 1) * features, :])
        done[at : at + extent, :] = total.astype(jnp.bfloat16)
        at += extent
    copy = pltpu.make_async_copy(done, out.at[pl.ds(start, at), :], sem)
    copy.start()
    copy.wait()


def middle_kernel(groups, cap, count, tile, *refs):
    n = sum(len(g) for g in groups)
    blocks, refs = refs[: 3 * count], refs[3 * count :]
    sums, refs = refs[: len(groups)], refs[len(groups) :]
    packs, (near, turned), refs = refs[:n], refs[n : n + 2], refs[n + 2 :]
    out, term, done, sem = refs[-4:]
    term[...] = jnp.zeros_like(term)
    for g, slots in enumerate(groups):
        for i, slot in enumerate(slots):
            maps = packs[slot][...]
            rank = maps.shape[0] // 2
            maps = jnp.concatenate([jnp.zeros_like(maps[:rank]), maps[:rank]], axis=0)
            found = dot(sums[g][i * cap * TILE : (i + 1) * cap * TILE, :], maps)
            for c in range(cap):
                rows = tile_rows(tile[slot * cap + c])
                before = term[rows, :].astype(jnp.float32)
                term[rows, :] = (before + found[c * TILE : (c + 1) * TILE]).astype(term.dtype)
    row_sums(0, count, near, term, turned, blocks, out, done, sem)


def far_kernel(count, start, near, term, turned, *refs):
    out, token, done, sem = refs[-4:]
    token[...] = jnp.zeros_like(token)
    row_sums(start, count, near, term, turned, refs[:count], out, done, sem)


def final_kernel(count, scale, *refs):
    down, up = refs[-2:]
    rank = down.shape[0]
    for out, rows in ((down, slice(0, rank)), (up, slice(rank, 2 * rank))):
        total = refs[0][rows, :].astype(jnp.float32)
        for x in refs[1:count]:
            total += x[rows, :].astype(jnp.float32)
        out[...] = (total * scale).astype(out.dtype)


def on_device(
    activations,
    cotangent,
    frozen_weight,
    adapter_down_maps,
    adapter_up_maps,
    adapter_per_tile,
    live_per_tile,
    adapter_stored_row,
):
    rows, features = activations.shape
    tiles = rows // TILE
    stored, _, rank = adapter_down_maps.shape
    n = lax.axis_size("adapter")
    tensors = lax.axis_size("tensor")
    subs = lax.axis_size("sub")
    me = lax.axis_index("adapter")
    t_me, s_me = lax.axis_index("tensor"), lax.axis_index("sub")
    extents = [rows * c // sum(CHUNKS) for c in CHUNKS]
    starts = [sum(extents[:c]) for c in range(len(extents))]
    bf16, f32 = jnp.bfloat16, jnp.float32

    cap = -(-tiles // n)
    places = [t_me * subs + s_me, t_me * subs + (1 - s_me)]
    for s in (s_me, 1 - s_me):
        places += [jnp.remainder(t_me - k, tensors) * subs + s for k in range(1, tensors)]
    place = jnp.stack(places).astype(jnp.int32)

    groups = [[k for k in range(n) if 1 <= min(k, n - k) <= n // 4]]
    groups.append([k for k in range(n) if k not in groups[0]])

    down = jnp.swapaxes(adapter_down_maps, 1, 2).reshape(stored * rank, features)
    up = adapter_up_maps.reshape(stored * rank, features)
    pack_shape = jax.ShapeDtypeStruct((2 * rank, features), bf16)
    *parts, pack, pack_again = call(
        head_kernel,
        mib=56,
        in_specs=[ANY] * 3,
        out_specs=[ANY] * (FIRST + 2),
        out_shape=[jax.ShapeDtypeStruct((e, features), bf16) for e in extents[:FIRST]]
        + [pack_shape] * 2,
        scratch_shapes=[
            pltpu.VMEM((starts[FIRST], features), bf16),
            pltpu.VMEM(pack_shape.shape, bf16),
            pltpu.SemaphoreType.DMA((3, FIRST + 2)),
        ],
    )(cotangent, down, up)
    def across(part, aside=0):
        slice_axes, found = ("tensor", "sub"), []
        for k in range(1, tensors):
            to = [(t + k) % tensors * subs + (s + aside) % subs for t in range(tensors) for s in range(subs)]
            found.append(lax.ppermute(part, slice_axes, list(enumerate(to))))
        return found

    def forward(blocks):
        return [shift(x, "sub", subs, 1) for x in blocks]

    direct = [across(part) for part in parts]
    pair = shift(cotangent, "sub", subs, 1)
    table = jax.ShapeDtypeStruct((n * cap,), jnp.int32)
    later = [jax.ShapeDtypeStruct((e, features), bf16) for e in extents[FIRST:]]
    tile, live, *rest = call(
        functools.partial(plan_kernel, n, cap, tiles),
        in_specs=[SMEM] * 4 + [VMEM],
        out_specs=[SMEM] * 2 + [VMEM] * len(later),
        out_shape=[table] * 2 + later,
        scratch_shapes=[pltpu.SMEM((n,), jnp.int32)],
    )(adapter_per_tile, live_per_tile, adapter_stored_row, me.astype(jnp.int32).reshape(1), cotangent)
    parts = [*parts, *rest]

    def after(arrays):
        return [ANY] * len(arrays)

    def gate(blocks, ready):
        found = call(
            gate_kernel,
            in_specs=after(blocks) + [ANY],
            out_specs=after(blocks),
            out_shape=[jax.ShapeDtypeStruct(x.shape, x.dtype) for x in blocks],
            input_output_aliases={i: i for i in range(len(blocks))},
        )(*blocks, ready)
        return list(found)

    def near_part(which, data, ready, *before):
        return call(
            functools.partial(near_kernel, which),
            flops=which * HEAVY,
            in_specs=[SMEM] + [VMEM] * (2 + len(before)) + [ANY],
            out_specs=VMEM,
            out_shape=jax.ShapeDtypeStruct((rows, features), f32),
            input_output_aliases={3: 0} if before else {},
        )(place, data, frozen_weight, *before, ready)

    def tick(*ready):
        return call(
            tick_kernel,
            flops=HEAVY,
            in_specs=after(ready),
            out_specs=VMEM,
            out_shape=jax.ShapeDtypeStruct((8, 128), f32),
        )(*ready)

    def ranks(g, *wait):
        return call(
            functools.partial(rank_kernel, g, cap),
            in_specs=[SMEM] * 2 + [VMEM] * (2 + len(g)) + after(wait),
            out_specs=VMEM,
            out_shape=jax.ShapeDtypeStruct((len(g) * cap * TILE, 2 * rank), bf16),
        )(tile, live, activations, cotangent, *[packs[k] for k in g], *wait)

    def chip_sum(own, *wait):
        given = shift(own, "sub", subs, 1)
        sent = call(
            functools.partial(sum_kernel, 2, -1),
            in_specs=[VMEM] * 2 + after(wait),
            out_specs=VMEM,
            out_shape=jax.ShapeDtypeStruct(own.shape, bf16),
        )(own, given, *wait)
        return given, sent

    def slice_sum(own, given, others, held_parts, *wait):
        found = [own, given, *others]
        shapes = [jax.ShapeDtypeStruct(x.shape, x.dtype) for x in held_parts]
        return call(
            functools.partial(sum_kernel, len(found), -1 - len(shapes)),
            in_specs=[VMEM] * len(found) + after(held_parts) + after(wait),
            out_specs=[VMEM] + after(held_parts),
            out_shape=[jax.ShapeDtypeStruct(own.shape, bf16)] + shapes,
            input_output_aliases={len(found) + i: 1 + i for i in range(len(shapes))},
        )(*found, *held_parts, *wait)

    def adapter_terms(g, held, *wait):
        found = call(
            functools.partial(terms_kernel, g, cap),
            in_specs=[SMEM] + [VMEM] * 3 + after(wait),
            out_specs=[VMEM] * len(g),
            out_shape=[jax.ShapeDtypeStruct((2 * rank, features), bf16)] * len(g),
        )(tile, held, activations, cotangent, *wait)
        return dict(zip(g, found))

    first, second = groups
    packs = {0: pack} | {k: shift(pack, "adapter", n, k) for k in first}
    (pack_again,) = gate([pack_again], tile)
    packs |= {k: shift(pack_again, "adapter", n, k) for k in second if k}

    forwards = [forward(direct[0])]
    turned = call(
        turn_kernel,
        in_specs=[SMEM, VMEM],
        out_specs=VMEM,
        out_shape=jax.ShapeDtypeStruct((2 * (tensors - 1) * features, features), bf16),
    )(place, frozen_weight)
    near = near_part(0, cotangent, direct[0][0])
    own = ranks(first, tick(pair, near, turned))
    given, sent = chip_sum(own, tick(own), *forwards[0])
    mark = tick(sent)
    opened = gate([parts[2]], mark)
    direct.append(across(*opened))
    near = near_part(1, pair, opened[0], near)
    (held,) = slice_sum(own, given, across(sent), [], near)
    direct[1] = gate(direct[1], held)
    forwards.insert(1, forward(direct[1]))
    sums = [held]
    own = ranks(second, held)
    terms = adapter_terms(first, held, own)
    given, sent = chip_sum(own, tick(own), terms[first[0]], *forwards[1])
    mark = tick(sent)
    leaving = gate([terms[k] for k in first], mark)
    arrived = {k: shift(x, "adapter", n, -k) for k, x in zip(first, leaving)}
    direct.append(across(*gate([parts[3]], mark)))
    (held,) = slice_sum(own, given, across(sent), [], mark)
    sums.append(held)
    terms |= adapter_terms(second, held)
    arrived |= {k: shift(terms[k], "adapter", n, -k) for k in second if k}
    direct[2] = gate(direct[2], held)
    forwards.append(forward(direct[2]))

    blocks = [x for c in range(3) for x in direct[c] + forwards[c]]
    count = len(blocks) // 3
    operands = [tile, *blocks, *sums, *[packs[k] for k in range(n)], near, turned]
    whole_shape = jax.ShapeDtypeStruct((rows, features), bf16)
    out, term = call(
        functools.partial(middle_kernel, groups, cap, count),
        mib=20,
        flops=HEAVY,
        in_specs=[SMEM] + [VMEM] * (len(operands) - 1) + [ANY] * 2,
        out_specs=[HBM, VMEM],
        out_shape=[whole_shape] * 2,
        scratch_shapes=[pltpu.VMEM((starts[3], features), bf16), pltpu.SemaphoreType.DMA],
    )(*operands, terms[second[-1]], tick(held))
    direct[3] = gate(direct[3], term)
    forwards.append(forward(direct[3]))
    operands = [near, term, turned, *direct[3], *forwards[3]]
    out, token = call(
        functools.partial(far_kernel, count, starts[3]),
        mib=16,
        in_specs=[VMEM] * len(operands) + [HBM, ANY],
        out_specs=[HBM, VMEM],
        out_shape=[whole_shape, jax.ShapeDtypeStruct((8, 128), f32)],
        scratch_shapes=[pltpu.VMEM((rows - starts[3], features), bf16), pltpu.SemaphoreType.DMA],
        input_output_aliases={len(operands): 0},
    )(*operands, out, tick(held, terms[second[-1]]))
    maps_shape = jax.ShapeDtypeStruct((rank, features), bf16)
    down_grad, up_grad = call(
        functools.partial(final_kernel, n, (stored / rows) ** 0.5),
        in_specs=[VMEM] * n + [ANY],
        out_specs=[VMEM] * 2,
        out_shape=[maps_shape] * 2,
    )(terms[0], *[arrived[k] for k in range(1, n)], token)
    down_grad = jnp.swapaxes(down_grad.reshape(stored, rank, features), 1, 2)
    up_grad = up_grad.reshape(stored, rank, features)
    return (out, down_grad, up_grad)


def solution(mesh):
    return jax.shard_map(
        on_device,
        mesh=mesh,
        in_specs=(
            P(("groups", "adapter"), ("tensor", "sub")),
            P(("groups", "adapter"), ("tensor", "sub")),
            P(("tensor", "sub"), None),
            P(("groups", "adapter"), ("tensor", "sub"), None),
            P(("groups", "adapter"), None, ("tensor", "sub")),
            P("groups"),
            P("groups"),
            P("groups"),
        ),
        out_specs=(
            P(("groups", "adapter"), ("tensor", "sub")),
            P(("groups", "adapter"), ("tensor", "sub"), None),
            P(("groups", "adapter"), None, ("tensor", "sub")),
        ),
        check_vma=False,
    )
```

```python
import functools

import jax
import jax.numpy as jnp
from jax import lax
from jax.experimental import pallas as pl
from jax.experimental.pallas import tpu as pltpu
from jax.sharding import PartitionSpec as P

TILE = 128
HEAVY = 1 << 33
CHUNKS = (5, 3, 3, 5)
FIRST = 2
NT = (((1,), (1,)), ((), ()))
SMEM = pl.BlockSpec(memory_space=pltpu.SMEM)
VMEM = pl.BlockSpec(memory_space=pltpu.VMEM)
ANY = pl.BlockSpec(memory_space=pl.ANY)
HBM = pl.BlockSpec(memory_space=pltpu.HBM)


def shift(array, axis, size, by):
    return lax.ppermute(array, axis, [(i, (i + by) % size) for i in range(size)])


def call(body, mib=12, flops=0, **kwargs):
    params = pltpu.CompilerParams(vmem_limit_bytes=mib * 1024 * 1024)
    cost = pl.CostEstimate(flops=flops, bytes_accessed=0, transcendentals=0)
    name = getattr(body, "func", body).__name__
    return pl.pallas_call(body, compiler_params=params, cost_estimate=cost, name=name, **kwargs)


def dot(a, b, dims=(((1,), (0,)), ((), ()))):
    return lax.dot_general(a, b, dims, preferred_element_type=jnp.float32)


def tile_rows(index):
    return pl.ds(pl.multiple_of(index * TILE, TILE), TILE)


def slot_rows(data, tile, entries):
    return jnp.concatenate([data[tile_rows(tile[e]), :] for e in entries], axis=0)


def copy_all(pairs, sems):
    copies = [pltpu.make_async_copy(a, b, sems.at[i]) for i, (a, b) in enumerate(pairs)]
    for copy in copies:
        copy.start()
    return copies


def head_kernel(cot, down, up, *refs):
    *parts, pack, again, held, pack_held, sems = refs
    rank, rows, start = down.shape[0], [], 0
    for part in parts:
        rows.append(pl.ds(start, part.shape[0]))
        start += part.shape[0]
    pairs = [(cot.at[r, :], held.at[r, :]) for r in rows]
    pairs += [(down, pack_held.at[pl.ds(0, rank), :]), (up, pack_held.at[pl.ds(rank, rank), :])]
    loads = copy_all(pairs, sems.at[0])
    stores = []
    for i, part in enumerate(parts):
        loads[i].wait()
        stores.append(pltpu.make_async_copy(held.at[rows[i], :], part, sems.at[1, i]))
        stores[-1].start()
    for load in loads[-2:]:
        load.wait()
    stores += copy_all([(pack_held, pack), (pack_held, again)], sems.at[2])
    for store in stores:
        store.wait()


def plan_kernel(n, cap, tiles, ids, live_all, stored, me, own, tile, live, *refs):
    *parts, count = refs
    start = own.shape[0] - sum(part.shape[0] for part in parts)
    for part in parts:
        part[...] = own[start : start + part.shape[0], :]
        start += part.shape[0]
    for k in range(n):
        count[k] = 0
    for e in range(n * cap):
        tile[e] = 0
        live[e] = 0
    for t in range(tiles):
        at = me[0] * tiles + t
        k = lax.rem(me[0] - stored[ids[at]] + n, n)
        e = jnp.minimum(k * cap + count[k], n * cap - 1)
        tile[e] = t
        live[e] = live_all[at]
        count[k] = count[k] + 1


def rank_kernel(slots, cap, tile, live, act, cot, *refs):
    packs, out = refs[: len(slots)], refs[-1]
    width = packs[0].shape[0]
    part = lax.broadcasted_iota(jnp.int32, packs[0].shape, 0) < width // 2
    row = lax.broadcasted_iota(jnp.int32, (TILE, width), 0)
    for i, (slot, pack) in enumerate(zip(slots, packs)):
        entries = range(slot * cap, (slot + 1) * cap)
        maps = pack[...]
        zero = jnp.zeros_like(maps)
        both = dot(slot_rows(act, tile, entries), jnp.where(part, maps, zero), NT)
        both += dot(slot_rows(cot, tile, entries), jnp.where(part, zero, maps), NT)
        for c, e in enumerate(entries):
            at = (i * cap + c) * TILE
            out[at : at + TILE, :] = jnp.where(
                row < live[e], both[c * TILE : (c + 1) * TILE], 0.0
            ).astype(jnp.bfloat16)


def sum_kernel(count, place, *refs):
    total = refs[0][...].astype(jnp.float32)
    for x in refs[1:count]:
        total += x[...].astype(jnp.float32)
    out = refs[place]
    out[...] = total.astype(out.dtype)


def gate_kernel(*refs):
    pass


def tick_kernel(*refs):
    refs[-1][...] = jnp.zeros_like(refs[-1])


def terms_kernel(slots, cap, tile, held, act, cot, *refs):
    terms = refs[-len(slots) :]
    rank = held.shape[1] // 2
    for i, slot in enumerate(slots):
        entries = range(slot * cap, (slot + 1) * cap)
        both = held[i * cap * TILE : (i + 1) * cap * TILE, :].astype(jnp.float32)
        both = both.T.astype(jnp.bfloat16)
        terms[i][:rank, :] = dot(both[rank:], slot_rows(act, tile, entries)).astype(jnp.bfloat16)
        terms[i][rank:, :] = dot(both[:rank], slot_rows(cot, tile, entries)).astype(jnp.bfloat16)


def weight_columns(weight, place):
    features = weight.shape[0]
    return weight[:, pl.ds(pl.multiple_of(place * features, 128), features)]


def near_kernel(which, place, data, weight, *refs):
    total = dot(data[...], weight_columns(weight, place[which]), NT)
    refs[-1][...] = total if which == 0 else refs[0][...] + total


def turn_kernel(place, weight, out):
    features = weight.shape[0]
    for i in range(out.shape[0] // features):
        out[i * features : (i + 1) * features, :] = weight_columns(weight, place[2 + i]).T


def row_sums(start, count, near, term, turned, blocks, out, done, sem):
    at = 0
    for first in range(0, len(blocks), count):
        extent = blocks[first].shape[0]
        rows = slice(start + at, start + at + extent)
        total = near[rows, :] + term[rows, :].astype(jnp.float32)
        for i in range(count):
            features = turned.shape[1]
            total += dot(blocks[first + i][...], turned[i * features : (i + 1) * features, :])
        done[at : at + extent, :] = total.astype(jnp.bfloat16)
        at += extent
    copy = pltpu.make_async_copy(done, out.at[pl.ds(start, at), :], sem)
    copy.start()
    copy.wait()


def middle_kernel(groups, cap, count, tile, *refs):
    n = sum(len(g) for g in groups)
    blocks, refs = refs[: 3 * count], refs[3 * count :]
    sums, refs = refs[: len(groups)], refs[len(groups) :]
    packs, (near, turned), refs = refs[:n], refs[n : n + 2], refs[n + 2 :]
    out, term, done, sem = refs[-4:]
    term[...] = jnp.zeros_like(term)
    for g, slots in enumerate(groups):
        for i, slot in enumerate(slots):
            maps = packs[slot][...]
            rank = maps.shape[0] // 2
            maps = jnp.concatenate([jnp.zeros_like(maps[:rank]), maps[:rank]], axis=0)
            found = dot(sums[g][i * cap * TILE : (i + 1) * cap * TILE, :], maps)
            for c in range(cap):
                rows = tile_rows(tile[slot * cap + c])
                before = term[rows, :].astype(jnp.float32)
                term[rows, :] = (before + found[c * TILE : (c + 1) * TILE]).astype(term.dtype)
    row_sums(0, count, near, term, turned, blocks, out, done, sem)


def far_kernel(count, start, near, term, turned, *refs):
    out, token, done, sem = refs[-4:]
    token[...] = jnp.zeros_like(token)
    row_sums(start, count, near, term, turned, refs[:count], out, done, sem)


def final_kernel(count, scale, *refs):
    down, up = refs[-2:]
    rank = down.shape[0]
    for out, rows in ((down, slice(0, rank)), (up, slice(rank, 2 * rank))):
        total = refs[0][rows, :].astype(jnp.float32)
        for x in refs[1:count]:
            total += x[rows, :].astype(jnp.float32)
        out[...] = (total * scale).astype(out.dtype)


def on_device(
    activations,
    cotangent,
    frozen_weight,
    adapter_down_maps,
    adapter_up_maps,
    adapter_per_tile,
    live_per_tile,
    adapter_stored_row,
):
    rows, features = activations.shape
    tiles = rows // TILE
    stored, _, rank = adapter_down_maps.shape
    n = lax.axis_size("adapter")
    tensors = lax.axis_size("tensor")
    subs = lax.axis_size("sub")
    me = lax.axis_index("adapter")
    t_me, s_me = lax.axis_index("tensor"), lax.axis_index("sub")
    extents = [rows * c // sum(CHUNKS) for c in CHUNKS]
    starts = [sum(extents[:c]) for c in range(len(extents))]
    bf16, f32 = jnp.bfloat16, jnp.float32

    cap = -(-tiles // n)
    places = [t_me * subs + s_me, t_me * subs + (1 - s_me)]
    for s in (s_me, 1 - s_me):
        places += [jnp.remainder(t_me - k, tensors) * subs + s for k in range(1, tensors)]
    place = jnp.stack(places).astype(jnp.int32)

    groups = [[k for k in range(n) if 1 <= min(k, n - k) <= n // 4]]
    groups.append([k for k in range(n) if k not in groups[0]])

    down = jnp.swapaxes(adapter_down_maps, 1, 2).reshape(stored * rank, features)
    up = adapter_up_maps.reshape(stored * rank, features)
    pack_shape = jax.ShapeDtypeStruct((2 * rank, features), bf16)
    *parts, pack, pack_again = call(
        head_kernel,
        mib=56,
        in_specs=[ANY] * 3,
        out_specs=[ANY] * (FIRST + 2),
        out_shape=[jax.ShapeDtypeStruct((e, features), bf16) for e in extents[:FIRST]]
        + [pack_shape] * 2,
        scratch_shapes=[
            pltpu.VMEM((starts[FIRST], features), bf16),
            pltpu.VMEM(pack_shape.shape, bf16),
            pltpu.SemaphoreType.DMA((3, FIRST + 2)),
        ],
    )(cotangent, down, up)
    def across(part, aside=0):
        slice_axes, found = ("tensor", "sub"), []
        for k in range(1, tensors):
            to = [(t + k) % tensors * subs + (s + aside) % subs for t in range(tensors) for s in range(subs)]
            found.append(lax.ppermute(part, slice_axes, list(enumerate(to))))
        return found

    def forward(blocks):
        return [shift(x, "sub", subs, 1) for x in blocks]

    direct = [across(part) for part in parts]
    pair = shift(cotangent, "sub", subs, 1)
    table = jax.ShapeDtypeStruct((n * cap,), jnp.int32)
    later = [jax.ShapeDtypeStruct((e, features), bf16) for e in extents[FIRST:]]
    tile, live, *rest = call(
        functools.partial(plan_kernel, n, cap, tiles),
        in_specs=[SMEM] * 4 + [VMEM],
        out_specs=[SMEM] * 2 + [VMEM] * len(later),
        out_shape=[table] * 2 + later,
        scratch_shapes=[pltpu.SMEM((n,), jnp.int32)],
    )(adapter_per_tile, live_per_tile, adapter_stored_row, me.astype(jnp.int32).reshape(1), cotangent)
    parts = [*parts, *rest]

    def after(arrays):
        return [ANY] * len(arrays)

    def gate(blocks, ready):
        found = call(
            gate_kernel,
            in_specs=after(blocks) + [ANY],
            out_specs=after(blocks),
            out_shape=[jax.ShapeDtypeStruct(x.shape, x.dtype) for x in blocks],
            input_output_aliases={i: i for i in range(len(blocks))},
        )(*blocks, ready)
        return list(found)

    def near_part(which, data, ready, *before):
        return call(
            functools.partial(near_kernel, which),
            flops=which * HEAVY,
            in_specs=[SMEM] + [VMEM] * (2 + len(before)) + [ANY],
            out_specs=VMEM,
            out_shape=jax.ShapeDtypeStruct((rows, features), f32),
            input_output_aliases={3: 0} if before else {},
        )(place, data, frozen_weight, *before, ready)

    def tick(*ready):
        return call(
            tick_kernel,
            flops=HEAVY,
            in_specs=after(ready),
            out_specs=VMEM,
            out_shape=jax.ShapeDtypeStruct((8, 128), f32),
        )(*ready)

    def ranks(g, *wait):
        return call(
            functools.partial(rank_kernel, g, cap),
            in_specs=[SMEM] * 2 + [VMEM] * (2 + len(g)) + after(wait),
            out_specs=VMEM,
            out_shape=jax.ShapeDtypeStruct((len(g) * cap * TILE, 2 * rank), bf16),
        )(tile, live, activations, cotangent, *[packs[k] for k in g], *wait)

    def chip_sum(own, *wait):
        given = shift(own, "sub", subs, 1)
        sent = call(
            functools.partial(sum_kernel, 2, -1),
            in_specs=[VMEM] * 2 + after(wait),
            out_specs=VMEM,
            out_shape=jax.ShapeDtypeStruct(own.shape, bf16),
        )(own, given, *wait)
        return given, sent

    def slice_sum(own, given, others, held_parts, *wait):
        found = [own, given, *others]
        shapes = [jax.ShapeDtypeStruct(x.shape, x.dtype) for x in held_parts]
        return call(
            functools.partial(sum_kernel, len(found), -1 - len(shapes)),
            in_specs=[VMEM] * len(found) + after(held_parts) + after(wait),
            out_specs=[VMEM] + after(held_parts),
            out_shape=[jax.ShapeDtypeStruct(own.shape, bf16)] + shapes,
            input_output_aliases={len(found) + i: 1 + i for i in range(len(shapes))},
        )(*found, *held_parts, *wait)

    def adapter_terms(g, held, *wait):
        found = call(
            functools.partial(terms_kernel, g, cap),
            in_specs=[SMEM] + [VMEM] * 3 + after(wait),
            out_specs=[VMEM] * len(g),
            out_shape=[jax.ShapeDtypeStruct((2 * rank, features), bf16)] * len(g),
        )(tile, held, activations, cotangent, *wait)
        return dict(zip(g, found))

    first, second = groups
    packs = {0: pack} | {k: shift(pack, "adapter", n, k) for k in first}
    (pack_again,) = gate([pack_again], tile)
    packs |= {k: shift(pack_again, "adapter", n, k) for k in second if k}

    forwards = [forward(direct[0])]
    turned = call(
        turn_kernel,
        in_specs=[SMEM, VMEM],
        out_specs=VMEM,
        out_shape=jax.ShapeDtypeStruct((2 * (tensors - 1) * features, features), bf16),
    )(place, frozen_weight)
    near = near_part(0, cotangent, direct[0][0])
    own = ranks(first, tick(pair, near, turned))
    given, sent = chip_sum(own, tick(own), *forwards[0])
    mark = tick(sent)
    opened = gate([parts[2]], mark)
    direct.append(across(*opened))
    near = near_part(1, pair, opened[0], near)
    (held,) = slice_sum(own, given, across(sent), [], near)
    direct[1] = gate(direct[1], held)
    forwards.insert(1, forward(direct[1]))
    sums = [held]
    own = ranks(second, held)
    terms = adapter_terms(first, held, own)
    given, sent = chip_sum(own, tick(own), terms[first[0]], *forwards[1])
    mark = tick(sent)
    leaving = gate([terms[k] for k in first], mark)
    arrived = {k: shift(x, "adapter", n, -k) for k, x in zip(first, leaving)}
    direct.append(across(*gate([parts[3]], mark)))
    (held,) = slice_sum(own, given, across(sent), [], mark)
    sums.append(held)
    terms |= adapter_terms(second, held)
    arrived |= {k: shift(terms[k], "adapter", n, -k) for k in second if k}
    direct[2] = gate(direct[2], held)
    forwards.append(forward(direct[2]))

    blocks = [x for c in range(3) for x in direct[c] + forwards[c]]
    count = len(blocks) // 3
    operands = [tile, *blocks, *sums, *[packs[k] for k in range(n)], near, turned]
    whole_shape = jax.ShapeDtypeStruct((rows, features), bf16)
    out, term = call(
        functools.partial(middle_kernel, groups, cap, count),
        mib=20,
        flops=HEAVY,
        in_specs=[SMEM] + [VMEM] * (len(operands) - 1) + [ANY] * 2,
        out_specs=[HBM, VMEM],
        out_shape=[whole_shape] * 2,
        scratch_shapes=[pltpu.VMEM((starts[3], features), bf16), pltpu.SemaphoreType.DMA],
    )(*operands, terms[second[-1]], tick(held))
    direct[3] = gate(direct[3], term)
    forwards.append(forward(direct[3]))
    operands = [near, term, turned, *direct[3], *forwards[3]]
    out, token = call(
        functools.partial(far_kernel, count, starts[3]),
        mib=16,
        in_specs=[VMEM] * len(operands) + [HBM, ANY],
        out_specs=[HBM, VMEM],
        out_shape=[whole_shape, jax.ShapeDtypeStruct((8, 128), f32)],
        scratch_shapes=[pltpu.VMEM((rows - starts[3], features), bf16), pltpu.SemaphoreType.DMA],
        input_output_aliases={len(operands): 0},
    )(*operands, out, tick(held, terms[second[-1]]))
    maps_shape = jax.ShapeDtypeStruct((rank, features), bf16)
    down_grad, up_grad = call(
        functools.partial(final_kernel, n, (stored / rows) ** 0.5),
        in_specs=[VMEM] * n + [ANY],
        out_specs=[VMEM] * 2,
        out_shape=[maps_shape] * 2,
    )(terms[0], *[arrived[k] for k in range(1, n)], token)
    down_grad = jnp.swapaxes(down_grad.reshape(stored, rank, features), 1, 2)
    up_grad = up_grad.reshape(stored, rank, features)
    return (out, down_grad, up_grad)


def solution(mesh):
    return jax.shard_map(
        on_device,
        mesh=mesh,
        in_specs=(
            P(("groups", "adapter"), ("tensor", "sub")),
            P(("groups", "adapter"), ("tensor", "sub")),
            P(("tensor", "sub"), None),
            P(("groups", "adapter"), ("tensor", "sub"), None),
            P(("groups", "adapter"), None, ("tensor", "sub")),
            P("groups"),
            P("groups"),
            P("groups"),
        ),
        out_specs=(
            P(("groups", "adapter"), ("tensor", "sub")),
            P(("groups", "adapter"), ("tensor", "sub"), None),
            P(("groups", "adapter"), None, ("tensor", "sub")),
        ),
        check_vma=False,
    )
```
